32 devices in a mesh: dp: 8 (over z, x), tensor: 4 (over y, core).
Axes of the slice: x: 2, y: 2, z: 4, core: 2. Of those that a mesh axis runs over, the one named last changes fastest.
Arguments:
- tokens: bfloat16 [512, 64, 768], P('tensor', 'dp'), may hold values from -6 to 6
- w_qkv: bfloat16 [768, 3, 768], P('dp', None, 'tensor'), may hold values from -0.21875 to 0.21875
- b_qv: bfloat16 [2, 12, 64], P(None, 'tensor', 'dp'), may hold values from -2 to 2
- w_out: bfloat16 [768, 768], P('tensor', 'dp'), may hold values from -1.75 to 1.75
- w_up: bfloat16 [768, 3072], P('dp', 'tensor'), may hold values from -0.21875 to 0.21875
- b_up: bfloat16 [48, 64], P('tensor', 'dp'), may hold values from -2 to 2
- w_down: bfloat16 [3072, 768], P('tensor', 'dp'), may hold values from -0.109375 to 0.109375
- ln_gains: bfloat16 [2, 768], P(None, 'dp'), may hold values from 0.25 to 1.75
- shifts: bfloat16 [4, 768], P(None, 'dp'), may hold values from -2 to 2
- lengths: int32 [64], P('dp'), may hold values from 170 to 512, as said below
- segments: int32 [64, 512], P('dp'), may hold values from 0 to 3, as said below
- pair_ids: int32 [256], replicated, may hold values from 0 to 255, each once
- targets: float32 [128], replicated, may hold values from 0 to 1
Outputs:
- hidden_out: bfloat16 [512, 64, 768], P('tensor', 'dp')
- grad_tokens: bfloat16 [512, 64, 768], P('tensor', 'dp')
- grad_w_qkv: float32 [768, 3, 768], P('dp', None, 'tensor')
- grad_b_qv: float32 [2, 12, 64], P(None, 'tensor', 'dp')
- grad_w_out: float32 [768, 768], P('tensor', 'dp')
- grad_w_up: float32 [768, 3072], P('dp', 'tensor')
- grad_b_up: float32 [48, 64], P('tensor', 'dp')
- grad_w_down: float32 [3072, 768], P('tensor', 'dp')
- grad_ln_gains: float32 [2, 768], P(None, ('dp', 'tensor'))
- grad_shifts: float32 [4, 768], P(None, ('dp', 'tensor'))
The draws below stay inside these ranges and needn't reach their ends.
Inputs may be any that keep to these rules, and one draw needn't show every extreme that they name: Rows are grouped by length: the rows of a higher index of dp are drawn from a range of longer lengths; in every index of dp some row has length 448 or more; some row of the batch has length 512. `segments`: ids never fall along a row; every sentence has one or more positions below its row's length; positions at or after the length carry the id 4 - 1.
All inputs are finite; a program needn't handle non-finite values.
Results may differ from the reference program's by a relative error of at most 0.018.
Values may be sent and summed in bfloat16 or wider, within the bound.
No kernel may reach another device: no remote copies, remote signals or barrier semaphores. Data moves between devices by JAX's collectives and lax.ppermute only.
A program may use at most 192 MiB of HBM per device.

```python
import jax
import jax.numpy as jnp
from jax import lax

HEADS = 12
HD = 64
D = 768
FF = 3072
SEQ = 512
SEGS = 4
ROWS_DEV = 8
ROWS = 64
POOLED = 256
PAIRS = 128


def row_layout(key):
    row_index = jnp.arange(ROWS)
    device_of = row_index // ROWS_DEV
    groups = ROWS // ROWS_DEV
    lowest = SEQ // 3 + (SEQ - SEQ // 3) * device_of // groups
    length_key, pick_key, cut_key, long_key, full_key, short_cut_key = jax.random.split(key, 6)
    length = jax.random.randint(length_key, (ROWS,), lowest, SEQ + 1)
    chosen = jax.random.randint(pick_key, (groups,), 0, ROWS_DEV)
    is_long = row_index % ROWS_DEV == jnp.repeat(chosen, ROWS_DEV, total_repeat_length=ROWS)
    long_length = jax.random.randint(long_key, (ROWS,), SEQ - SEQ // 8, SEQ + 1)
    length = jnp.where(is_long, long_length, length)
    full_group = jax.random.randint(full_key, (), 0, groups)
    length = jnp.where(is_long & (device_of == full_group), SEQ, length)
    share = length // SEGS
    pieces = jax.random.randint(cut_key, (ROWS, SEGS - 1), 1, share[:, None] + 1)
    short_pieces = jax.random.randint(short_cut_key, (ROWS, SEGS - 1), 1, 3)
    pieces = jnp.where(is_long[:, None], short_pieces, pieces)
    cuts = jnp.cumsum(pieces, axis=1)
    places = jnp.arange(SEQ)
    segment = jnp.sum((places[None, :, None] >= cuts[:, None, :]).astype(jnp.int32), axis=2)
    return (length.astype(jnp.int32), segment.astype(jnp.int32))


def draw_lengths(key, part):
    return row_layout(key)[0]


def draw_segments(key, part):
    return row_layout(key)[1]


def block_scale(own_key, extent, shards, least, largest):
    level = 1.0
    for position, blocks in shards:
        draws = jax.random.uniform(jax.random.fold_in(jax.random.fold_in(own_key, 6), position), (blocks,), jnp.float32, least / len(shards), largest / len(shards))
        level = level * jnp.repeat(jnp.exp(draws), extent[position] // blocks).reshape((-1,) + (1,) * (len(extent) - 1 - position))
    return level


def bell_draw(key, shape, spread, most, cuts=(), dtype=jnp.bfloat16):
    array = spread * jax.random.normal(key, shape, jnp.float32)
    if cuts:
        array = array * block_scale(key, shape, cuts, -0.22, 0.18)
    return jnp.clip(array, -most, most).astype(dtype)


def setup_inputs(seed: int = 0) -> dict:
    seeds = jax.random.split(jax.random.key(seed), 14)
    tokens = bell_draw(seeds[0], (SEQ, ROWS, D), 1.0, 6.0, ((0, 4), (1, 8)))
    w_qkv = bell_draw(seeds[1], (D, 3, D), D ** -0.5, 0.21875, ((0, 8), (2, 4)))
    b_qv = bell_draw(seeds[2], (2, HEADS, HD), 0.3, 2.0, ((1, 4), (2, 8)))
    w_out = bell_draw(seeds[3], (D, D), (D // 64) ** -0.5, 1.75, ((0, 4), (1, 8)))
    w_up = bell_draw(seeds[4], (D, FF), D ** -0.5, 0.21875, ((0, 8), (1, 4)))
    b_up = bell_draw(seeds[5], (FF // HD, HD), 0.3, 2.0, ((0, 4), (1, 8)))
    w_down = bell_draw(seeds[6], (FF, D), FF ** -0.5, 0.109375, ((0, 4), (1, 8)))
    ln_gains = jnp.clip(1.0 + 0.15 * jax.random.normal(seeds[7], (2, D), jnp.float32), 0.25, 1.75).astype(jnp.bfloat16)
    shifts = bell_draw(seeds[8], (4, D), 0.3, 2.0, ((1, 8),))
    lengths = draw_lengths(jax.random.fold_in(seeds[13], 71), 0)
    segments = draw_segments(jax.random.fold_in(seeds[13], 71), 0)
    pair_ids = jax.random.permutation(seeds[11], POOLED).astype(jnp.int32)
    targets = jnp.clip(jax.random.uniform(seeds[12], (PAIRS,), jnp.float32, 0.0, 1.0), 0.0, 1.0)
    return dict(tokens=tokens, w_qkv=w_qkv, b_qv=b_qv, w_out=w_out, w_up=w_up, b_up=b_up, w_down=w_down, ln_gains=ln_gains, shifts=shifts, lengths=lengths, segments=segments, pair_ids=pair_ids, targets=targets)


@jax.custom_vjp
def low(v):
    return lax.optimization_barrier(v.astype(jnp.bfloat16)).astype(jnp.float32)

@jax.custom_vjp
def low_back(v):
    return v

def low_keep(v):
    return (low(v), None)

def low_pass(kept, grad):
    return (grad,)

def back_keep(v):
    return (v, None)

def back_low(kept, grad):
    return (low(grad),)
low.defvjp(low_keep, low_pass)
low_back.defvjp(back_keep, back_low)
eps_norm = 1e-05
eps_cosine = 1e-06
loss_scale = 4096.0
neg_large = -1e+30

def layer_norm(values, gain, shift):
    centred = values - lax.optimization_barrier(jnp.mean(values, axis=-1, keepdims=True))
    inverse = lax.rsqrt(lax.optimization_barrier(jnp.mean(centred * centred, axis=-1, keepdims=True)) + eps_norm)
    return centred * inverse * gain + shift

def pair_loss(pooled, pair_ids, targets):
    first = pooled[pair_ids[0::2]]
    second = pooled[pair_ids[1::2]]
    inner = lax.optimization_barrier(jnp.sum(first * second, axis=-1))
    cosine = inner * lax.rsqrt(lax.optimization_barrier(jnp.sum(first * first, axis=-1)) + eps_cosine) * lax.rsqrt(lax.optimization_barrier(jnp.sum(second * second, axis=-1)) + eps_cosine)
    missed = cosine - targets
    return loss_scale * jnp.sum(missed * missed)

def row_mask(seg_row, row_length):
    places = jnp.arange(seg_row.shape[0])
    live_key = places < row_length
    same_seg = seg_row[:, None] == seg_row[None, :]
    return live_key[None, :] & (same_seg | jnp.logical_not(live_key)[:, None])

def attend_row(packed):
    q_row, k_row, v_row, seg_row, row_length = packed
    highest = lax.Precision.HIGHEST
    scores = low_back(jnp.einsum('ihd,jhd->hij', q_row, k_row, precision=highest))
    scores = jnp.where(row_mask(seg_row, row_length)[None], scores, neg_large)
    weights = low(jax.nn.softmax(scores, axis=-1))
    return jnp.einsum('hij,jhd->ihd', weights, v_row, precision=highest)

def pool_table(lengths, segments):
    labels = jnp.arange(SEGS)
    live_pos = jnp.arange(SEQ)[None, :] < lengths[:, None]
    member = ((segments[:, :, None] == labels[None, None, :]) & live_pos[:, :, None]).astype(jnp.float32)
    counts = lax.optimization_barrier(jnp.sum(member, axis=1))
    return member / counts[:, None, :]

def by_row(matrix):
    return matrix.reshape(SEQ, ROWS, HEADS, HD).transpose(1, 0, 2, 3)

def forward(tokens, w_qkv, b_qv, w_out, w_up, b_up, w_down, ln_gains, shifts, lengths, segments, pair_ids, targets):
    highest = lax.Precision.HIGHEST
    x_rows = tokens.reshape(SEQ * ROWS, D)
    projected = jnp.dot(x_rows, w_qkv.reshape(D, 3 * D), precision=highest)
    head_bias = b_qv.reshape(2, D)
    q_all = low_back(low((projected[:, :D] + head_bias[0]) * 0.125))
    k_all = low_back(low(projected[:, D:2 * D]))
    v_all = low_back(low(projected[:, 2 * D:] + head_bias[1]))
    attended = lax.map(jax.checkpoint(attend_row), (by_row(q_all), by_row(k_all), by_row(v_all), segments, lengths))
    joined = low_back(low(attended.transpose(1, 0, 2, 3).reshape(SEQ * ROWS, D)))
    branch = low_back(jnp.dot(joined, w_out, precision=highest)) + shifts[0]
    normed = layer_norm(x_rows + branch, ln_gains[0], shifts[1])
    before = low_back(jnp.dot(low(normed), w_up, precision=highest) + b_up.reshape(FF))
    hidden = low(jax.nn.gelu(before, approximate=False))
    feed_out = low_back(jnp.dot(hidden, w_down, precision=highest)) + shifts[2]
    output = layer_norm(normed + feed_out, ln_gains[1], shifts[3])
    table = pool_table(lengths, segments)
    pooled = jnp.einsum('rts,trd->rsd', table, output.reshape(SEQ, ROWS, D), precision=highest)
    pooled = low(pooled.reshape(POOLED, D))
    return (pair_loss(pooled, pair_ids, targets), output)

def reference(tokens, w_qkv, b_qv, w_out, w_up, b_up, w_down, ln_gains, shifts, lengths, segments, pair_ids, targets):
    floats = jax.tree.map(lambda entry: entry.astype(jnp.float32), (tokens, w_qkv, b_qv, w_out, w_up, b_up, w_down, ln_gains, shifts))
    target_f = targets.astype(jnp.float32)

    def closure(tok_f, wqkv_f, bqv_f, wout_f, wup_f, bup_f, wdown_f, gains_f, shifts_f):
        return forward(tok_f, wqkv_f, bqv_f, wout_f, wup_f, bup_f, wdown_f, gains_f, shifts_f, lengths, segments, pair_ids, target_f)
    loss_value, pull_back, output = jax.vjp(closure, floats[0], floats[1], floats[2], floats[3], floats[4], floats[5], floats[6], floats[7], floats[8], has_aux=True)
    grads = pull_back(jnp.ones_like(loss_value))
    hidden_out = output.reshape(SEQ, ROWS, D).astype(jnp.bfloat16)
    grad_tokens = grads[0].astype(jnp.bfloat16)
    return (hidden_out, grad_tokens, grads[1], grads[2], grads[3], grads[4], grads[5], grads[6], grads[7], grads[8])
```

```python
import math

import jax
import jax.numpy as jnp
import numpy as np
from jax import lax
from jax.experimental import pallas as pl
from jax.experimental.pallas import tpu as pltpu
from jax.sharding import PartitionSpec as P

SEGS = 4
EPS_NORM = 1e-05
EPS_COS = 1e-06
LOSS_SCALE = 4096.0
NEG = -1e30
DEAD = 99

BF = jnp.bfloat16
F32 = jnp.float32
MIB = 1024 * 1024


def dot(a, b, ca, cb):
    return lax.dot_general(a, b, (((ca,), (cb,)), ((), ())), preferred_element_type=F32)


def nn(a, b):
    return dot(a, b, 1, 0)


def nt(a, b):
    return dot(a, b, 1, 1)


def tn(a, b):
    return dot(a, b, 0, 0)


def call(kernel, grid, ins, outs, scratch=(), limit=48, cost=None, scalars=0):
    def spec(shape, block, index):
        if block is None:
            zeros = (0,) * len(shape)
            return pl.BlockSpec(shape, lambda *_: zeros)
        return pl.BlockSpec(block, index)

    in_specs = [spec(a.shape, b, m) for a, b, m in ins[scalars:]]
    out_specs = [spec(s, b, m) for s, _, b, m in outs]
    flops, nbytes, trans = cost or (0, 0, 0)
    return pl.pallas_call(
        kernel,
        grid_spec=pltpu.PrefetchScalarGridSpec(
            num_scalar_prefetch=scalars,
            grid=grid,
            in_specs=in_specs,
            out_specs=out_specs,
            scratch_shapes=list(scratch),
        ),
        out_shape=[jax.ShapeDtypeStruct(s, d) for s, d, _, _ in outs],
        compiler_params=pltpu.CompilerParams(
            dimension_semantics=("arbitrary",) * len(grid), vmem_limit_bytes=limit * MIB
        ),
        cost_estimate=pl.CostEstimate(flops=flops, bytes_accessed=nbytes, transcendentals=trans),
    )(*[a for a, _, _ in ins])


def deal_kernel(t_ref, tok_ref, *out_refs):
    size = tok_ref.shape[0]
    parts = len(out_refs)
    rows, block = out_refs[0].shape[0], out_refs[0].shape[1]
    t = t_ref[0]
    m = lax.broadcasted_iota(jnp.int32, (size, size), 0)
    n = lax.broadcasted_iota(jnp.int32, (size, size), 1)
    part, row, place = m // (rows * block), (m // block) % rows, m % block
    source = place * (parts * rows) + jnp.bitwise_xor(part, t) * rows + row
    pick = jnp.where(source == n, 1.0, 0.0).astype(BF)
    moved = nn(pick, tok_ref[...]).astype(BF)
    for j, out in enumerate(out_refs):
        for r in range(rows):
            at = (j * rows + r) * block
            out[r] = moved[at : at + block]


def collect_kernel(t_ref, *refs):
    *in_refs, out_ref = refs
    size = out_ref.shape[0]
    parts = len(in_refs)
    rows, block = in_refs[0].shape[0], in_refs[0].shape[1]
    t = t_ref[0]
    m = lax.broadcasted_iota(jnp.int32, (size, size), 1)
    n = lax.broadcasted_iota(jnp.int32, (size, size), 0)
    part, row, place = m // (rows * block), (m // block) % rows, m % block
    target = place * (parts * rows) + jnp.bitwise_xor(part, t) * rows + row
    pick = jnp.where(target == n, 1.0, 0.0).astype(BF)
    joined = jnp.concatenate([ref[r] for ref in in_refs for r in range(rows)], axis=0)
    out_ref[...] = nn(pick, joined).astype(BF)


def lay(own, other, lo, dest, width):
    depth, rows = own.shape[0], own.shape[1]
    for z in range(depth):
        mine, theirs = own[z, :, :width], other[z, :, :width]
        for b in range(2):
            at = (2 * z + b) * rows
            dest[at : at + rows, :] = jnp.where(lo == b, mine, theirs)


def attn_fwd_kernel(
    lo_ref, x_ref, a0, a1, b0, b1, sup_ref, sqv_ref, kc_ref, qc_ref,
    qkv_ref, p_ref, o_ref, w_ref, small_ref, bias_ref, mask_ref,
):
    j, r = pl.program_id(0), pl.program_id(1)
    local = o_ref.shape[3]
    heads = p_ref.shape[2]
    hd = local // heads
    lo = lo_ref[0]

    @pl.when(r == 0)
    def _():
        @pl.when(j == 0)
        def _():
            lay(a0, a1, lo, w_ref.at[0], w_ref.shape[2])

        @pl.when(j == 1)
        def _():
            lay(b0, b1, lo, w_ref.at[0], w_ref.shape[2])

        cols = w_ref[0, :, 3 * local :][:, :8]
        width = w_ref.shape[1]
        rows = lax.broadcasted_iota(jnp.int32, (8, width), 0)
        eye = (
            lax.broadcasted_iota(jnp.int32, (width, width), 0)
            == lax.broadcasted_iota(jnp.int32, (width, width), 1)
        ).astype(BF)
        small_ref[0] = jnp.where(rows == 6, tn(cols, sup_ref[...]), tn(cols, eye))
        bias_ref[...] = tn(cols, sqv_ref[...])

    kc, qc = kc_ref[0], qc_ref[0]
    allowed = (kc == qc) | ((qc == DEAD) & (kc >= 0))
    mask_ref[...] = jnp.where(allowed, 0.0, NEG)

    projected = nn(x_ref[0], w_ref[0, :, : 3 * local])
    q_all = ((projected[:, :local] + bias_ref[7:8, :local]) * 0.125).astype(BF)
    k_all = projected[:, local : 2 * local].astype(BF)
    v_all = (projected[:, 2 * local :] + bias_ref[7:8, local:]).astype(BF)
    qkv_ref[0, 0, :, :local] = q_all
    qkv_ref[0, 0, :, local : 2 * local] = k_all
    qkv_ref[0, 0, :, 2 * local :] = v_all
    outs = []
    for h in range(heads):
        at = slice(h * hd, (h + 1) * hd)
        s = nt(q_all[:, at], k_all[:, at]) + mask_ref[...]
        top = jnp.max(s, axis=-1, keepdims=True)
        e = jnp.exp(s - top)
        total = jnp.sum(e, axis=-1, keepdims=True)
        p = (e * (1.0 / total)).astype(BF)
        p_ref[0, 0, h] = p
        outs.append(nn(p, v_all[:, at]).astype(BF))
    o_ref[0, 0] = jnp.concatenate(outs, axis=1)


def norm(z):
    centred = z - jnp.mean(z, axis=-1, keepdims=True)
    rstd = lax.rsqrt(jnp.mean(centred * centred, axis=-1, keepdims=True) + EPS_NORM)
    return centred * rstd, rstd


def norm_back(dy, xh, rstd, gain):
    dxh = dy * gain
    mean = jnp.mean(dxh, axis=-1, keepdims=True)
    proj = jnp.mean(dxh * xh, axis=-1, keepdims=True)
    return rstd * (dxh - mean - xh * proj)


def out_kernel(lo_ref, oa, ob, x_ref, small_ref, *refs):
    ws, (xh_ref, rstd_ref, u_ref, wo_ref) = refs[:8], refs[8:]
    local = oa.shape[2]

    @pl.when(pl.program_id(0) == 0)
    def _():
        for j in range(4):
            lay(ws[2 * j], ws[2 * j + 1], lo_ref[0], wo_ref.at[j], local)

    a = nt(oa[0], wo_ref[0]) + nt(oa[1], wo_ref[1]) + nt(ob[0], wo_ref[2]) + nt(ob[1], wo_ref[3])
    z = x_ref[...].astype(F32) + (a + small_ref[2:3])
    xh, rstd = norm(z)
    xh_ref[...] = xh
    rstd_ref[...] = rstd
    u_ref[...] = (xh * small_ref[0:1] + small_ref[3:4]).astype(BF)


def gelu_parts(e):
    size = jnp.abs(e)
    density = jnp.exp(-0.5 * e * e)
    t = 1.0 / (1.0 + (0.3275911 / math.sqrt(2.0)) * size)
    poly = t * (
        0.5 * 0.254829592
        + t * (0.5 * -0.284496736 + t * (0.5 * 1.421413741 + t * (0.5 * -1.453152027 + t * (0.5 * 1.061405429))))
    )
    tail = poly * density
    cdf = jnp.where(e < 0, tail, 1.0 - tail)
    return e * cdf, cdf + e * (density * (1.0 / math.sqrt(2.0 * math.pi)))


def up_kernel(lo_ref, u_ref, bup_ref, *refs):
    ws, (h_ref, g_ref, w_ref) = refs[:8], refs[8:]

    @pl.when(pl.program_id(0) == 0)
    def _():
        for j in range(4):
            lay(ws[2 * j], ws[2 * j + 1], lo_ref[0], w_ref.at[j], w_ref.shape[2])

    u = u_ref[...]
    for j in range(4):
        e = nn(u, w_ref[j]) + bup_ref[j, 6:7]
        h, g = gelu_parts(e)
        h_ref[j] = h.astype(BF)
        g_ref[j] = g.astype(BF)


def split3(v):
    a = v.astype(BF)
    rest = v - a.astype(F32)
    b = rest.astype(BF)
    c = (rest - b.astype(F32)).astype(BF)
    return a, b, c


def down_kernel(lo_ref, h_ref, xh1_ref, small_ref, code_ref, inv_ref, *refs):
    ws, (xh_ref, rstd_ref, y_ref, w_ref, pool_ref, acc_ref) = refs[:8], refs[8:]
    step = pl.program_id(0)

    @pl.when(step == 0)
    def _():
        for j in range(4):
            lay(ws[2 * j], ws[2 * j + 1], lo_ref[0], w_ref.at[j], w_ref.shape[2])
        acc_ref[...] = jnp.zeros_like(acc_ref)

    f = nt(h_ref[0], w_ref[0])
    for j in range(1, 4):
        f += nt(h_ref[j], w_ref[j])
    y1 = xh1_ref[...] * small_ref[0:1] + small_ref[3:4]
    xh, rstd = norm(y1 + (f + small_ref[4:5]))
    y2 = xh * small_ref[1:2] + small_ref[5:6]
    xh_ref[...] = xh
    rstd_ref[...] = rstd
    y_ref[...] = y2.astype(BF)
    member = (lax.broadcasted_iota(jnp.int32, (8, y2.shape[0]), 0) == code_ref[...]).astype(BF)
    a, b, c = split3(y2)
    acc_ref[...] += nn(member, a) + nn(member, b) + nn(member, c)

    @pl.when(step == pl.num_programs(0) - 1)
    def _():
        pool_ref[...] = (acc_ref[...] * inv_ref[...]).astype(BF)


def loss_grad(pooled_ref, ids_ref, mate_ref, target_ref, inv_ref):
    pooled = pooled_ref[...]
    places = lax.broadcasted_iota(jnp.int32, (8, pooled.shape[0]), 1)
    first = nn((places == ids_ref[...]).astype(BF), pooled)
    second = nn((places == mate_ref[...]).astype(BF), pooled)
    inner = jnp.sum(first * second, axis=-1, keepdims=True)
    ra = lax.rsqrt(jnp.sum(first * first, axis=-1, keepdims=True) + EPS_COS)
    rb = lax.rsqrt(jnp.sum(second * second, axis=-1, keepdims=True) + EPS_COS)
    missed = inner * ra * rb - target_ref[...]
    grad = (2.0 * LOSS_SCALE) * missed * (second * (ra * rb) - first * (inner * rb * ra * ra * ra))
    return grad * inv_ref[...]


def rowsum(v):
    return jnp.sum(v, axis=0, keepdims=True)


def feed_back_kernel(
    pooled_ref, ids_ref, mate_ref, target_ref, inv_ref, code_ref, xh_ref, rstd_ref, small_ref, w_ref, g_ref,
    df_ref, dz_ref, de_ref, sum_ref, bup_ref, gp_ref,
):
    step = pl.program_id(0)

    @pl.when(step == 0)
    def _():
        grad = loss_grad(pooled_ref, ids_ref, mate_ref, target_ref, inv_ref)
        for i, part in enumerate(split3(grad)):
            gp_ref[i] = part
        sum_ref[...] = jnp.zeros_like(sum_ref)
        bup_ref[...] = jnp.zeros_like(bup_ref)

    member = (lax.broadcasted_iota(jnp.int32, (8, xh_ref.shape[0]), 0) == code_ref[...]).astype(BF)
    dy = tn(member, gp_ref[0]) + tn(member, gp_ref[1]) + tn(member, gp_ref[2])
    xh = xh_ref[...]
    dz = norm_back(dy, xh, rstd_ref[...], small_ref[1:2])
    sum_ref[0:1] += rowsum(dy * xh)
    sum_ref[1:2] += rowsum(dy)
    sum_ref[2:3] += rowsum(dz)
    df = dz.astype(BF)
    df_ref[...] = df
    dz_ref[...] = dz
    for j in range(4):
        de = (nn(df, w_ref[j]) * g_ref[j].astype(F32)).astype(BF)
        de_ref[j] = de
        bup_ref[j, 0:1] += rowsum(de.astype(F32))


def norm_back_kernel(
    de_ref, dz2_ref, xh_ref, rstd_ref, small_ref, w_ref, wo_ref, dz_ref, da_ref, do_ref, sum_ref
):
    @pl.when(pl.program_id(0) == 0)
    def _():
        sum_ref[...] = jnp.zeros_like(sum_ref)

    dy = nt(de_ref[0], w_ref[0])
    for j in range(1, 4):
        dy += nt(de_ref[j], w_ref[j])
    dy = dz2_ref[...] + dy
    xh = xh_ref[...]
    dz = norm_back(dy, xh, rstd_ref[...], small_ref[0:1])
    sum_ref[0:1] += rowsum(dy * xh)
    sum_ref[1:2] += rowsum(dy)
    sum_ref[2:3] += rowsum(dz)
    da = dz.astype(BF)
    dz_ref[...] = dz
    da_ref[...] = da
    for j in range(4):
        do_ref[j] = nn(da, wo_ref[j]).astype(BF)


def pieces(grad, lo, keep_ref, send_ref, j, at):
    depth, rows = keep_ref.shape[2], keep_ref.shape[3]
    low = grad.astype(BF)

    def put(ref):
        for z in range(depth):
            first, second = (low[(2 * z + b) * rows : (2 * z + b + 1) * rows] for b in range(2))
            ref[0, 0, z, :, at] = jnp.where(lo == 0, first, second)
            ref[0, 1, z, :, at] = jnp.where(lo == 0, second, first)

    @pl.when(j % 2 == 0)
    def _():
        put(keep_ref)

    @pl.when(j % 2 == 1)
    def _():
        put(send_ref)


def grad_kernel(lo_ref, a_ref, b_ref, keep_ref, send_ref):
    grad = tn(a_ref[...], b_ref[0])
    pieces(grad, lo_ref[0], keep_ref, send_ref, pl.program_id(0), slice(0, grad.shape[1]))


def grad_two_kernel(lo_ref, a_ref, b_ref, c_ref, d_ref, keep_ref, send_ref):
    j = pl.program_id(0)
    wide = b_ref.shape[2]
    grad = tn(a_ref[...], b_ref[0])
    pieces(grad, lo_ref[0], keep_ref, send_ref, j, slice(0, wide))
    other = tn(c_ref[...], d_ref[0])
    other = jnp.concatenate([other, jnp.zeros((other.shape[0], 64), F32)], axis=1)
    pieces(other, lo_ref[0], keep_ref, send_ref, j, slice(wide, wide + other.shape[1]))


def attn_bwd_kernel(
    lo_ref, qkv_ref, p_ref, o_ref, do_ref, x_ref, w_ref, dxin_ref,
    keep_ref, send_ref, dx_ref, sum_ref, acc_ref,
):
    j, r = pl.program_id(0), pl.program_id(1)
    local = o_ref.shape[3]
    heads = p_ref.shape[2]
    hd = local // heads
    q_all, k_all, v_all = (qkv_ref[0, 0, :, i * local : (i + 1) * local] for i in range(3))
    o_all, do_all = o_ref[0, 0], do_ref[0, 0]
    prod = o_all.astype(F32) * do_all.astype(F32)
    dq, dk, dv = [], [], []
    for h in range(heads):
        at = slice(h * hd, (h + 1) * hd)
        p = p_ref[0, 0, h]
        do = do_all[:, at]
        dv.append(tn(do, p))
        dp = nt(do, v_all[:, at])
        mid = jnp.sum(prod[:, at], axis=-1, keepdims=True)
        ds = (p.astype(F32) * (dp - mid)).astype(BF)
        dq.append(nn(ds, k_all[:, at]))
        dk.append(tn(q_all[:, at], ds))
    dq = (jnp.concatenate(dq, axis=1).astype(BF).astype(F32) * 0.125).astype(BF)
    dkv = jnp.concatenate(dk + dv, axis=0).astype(BF).astype(F32)
    dkv = jnp.transpose(dkv).astype(BF)
    dproj = jnp.concatenate([dq, dkv], axis=1)
    sums = rowsum(dproj.astype(F32))
    grad = tn(x_ref[0], dproj)

    @pl.when(r == 0)
    def _():
        acc_ref[...] = grad
        sum_ref[0] = jnp.broadcast_to(sums, sum_ref.shape[1:])

    @pl.when(r > 0)
    def _():
        acc_ref[...] += grad
        sum_ref[0] += jnp.broadcast_to(sums, sum_ref.shape[1:])

    @pl.when(r == pl.num_programs(1) - 1)
    def _():
        full = jnp.concatenate([acc_ref[...], jnp.zeros((acc_ref.shape[0], 64), F32)], axis=1)
        pieces(full, lo_ref[0], keep_ref, send_ref, j, slice(0, full.shape[1]))

    dx = nt(dproj, w_ref[0, :, : 3 * local])

    @pl.when(j == 0)
    def _():
        dx_ref[r] = dxin_ref[r] + dx

    @pl.when(j > 0)
    def _():
        dx_ref[r] += dx


def make(mesh):
    nd, ntens = mesh.shape["dp"], mesh.shape["tensor"]
    nh = nd // 2
    groups = [[2 * z + b for z in range(nh)] for b in range(2)]

    def across(array, axis, bit):
        size = nd if axis == "dp" else ntens
        return lax.ppermute(array, axis, [(i, i ^ bit) for i in range(size)])

    def along(array):
        return lax.all_to_all(array, "dp", 0, 0, tiled=True, axis_index_groups=groups)

    def gather(piece, order):
        own = along(jnp.broadcast_to(piece[None], (nh,) + piece.shape))
        if order == "xy":
            lo = across(own, "dp", 1)
            far, far_lo = across(own, "tensor", 2), across(lo, "tensor", 2)
        else:
            far = across(own, "tensor", 2)
            lo, far_lo = across(own, "dp", 1), across(far, "dp", 1)
        out = {0: (own, lo), 2: (far, far_lo)}
        for j in (0, 2):
            out[j + 1] = tuple(across(v, "tensor", 1) for v in out[j])
        return out

    def reduce(keep, send, order):
        both = keep.astype(F32) + across(send, "tensor", 1).astype(F32)
        if order == "yx":
            half = both[0] + across(both[1].astype(BF), "tensor", 2).astype(F32)
            own = half[0] + across(half[1].astype(BF), "dp", 1).astype(F32)
        else:
            half = both[:, 0] + across(both[:, 1].astype(BF), "dp", 1).astype(F32)
            own = half[0] + across(half[1].astype(BF), "tensor", 2).astype(F32)
        return jnp.sum(along(own.astype(BF)).astype(F32), axis=0)

    def shards(
        tokens, w_qkv, b_qv, w_out, w_up, b_up, w_down, ln_gains, shifts, lengths, segments, pair_ids, targets
    ):
        part_len, row_count, width = tokens.shape
        rb = w_up.shape[0]
        hidden = w_up.shape[1]
        local = w_qkv.shape[2]
        hb = b_up.shape[1]
        hd = hb * nd
        heads = local // hd
        seq = segments.shape[1]
        rows = row_count // ntens
        count = rows * seq
        sents = rows * SEGS
        blk = 256
        steps = count // blk
        t = lax.axis_index("tensor")
        d = lax.axis_index("dp")
        fused = rb % 16 == 0
        depth, rbk = (nh, rb) if fused else (1, width // 2)
        lo_bit = (d % 2 if fused else d * 0).astype(jnp.int32).reshape(1)
        t_arr = t.astype(jnp.int32).reshape(1)

        def straight(own, other):
            first = jnp.where(d % 2 == 0, own, other)
            second = jnp.where(d % 2 == 0, other, own)
            full = jnp.stack([first, second], axis=1).reshape(2, 1, width // 2, own.shape[2])
            return full[0], full[1]

        def ready(parts):
            if fused:
                return parts
            return {j: straight(*v) for j, v in parts.items()}

        def cut(array):
            if fused:
                return array
            full = array.reshape(2, nh, 2, rb, array.shape[-1])
            first, second = full[:, :, 0], full[:, :, 1]
            return jnp.stack(
                [jnp.where(d % 2 == 0, first, second), jnp.where(d % 2 == 0, second, first)], axis=1
            )

        deal_block = blk // row_count
        dealt = call(
            deal_kernel,
            (part_len // deal_block,),
            [(t_arr, None, None), (tokens.reshape(part_len * row_count, width), (blk, width), lambda i, *_: (i, 0))],
            [((rows, part_len, width), BF, (rows, deal_block, width), lambda i, *_: (0, i, 0))] * ntens,
            scalars=1,
            cost=(2 * 1024 * 256 * 768, 3 * MIB, 0),
        )
        x_parts = [dealt[0]] + [across(dealt[j], "tensor", j) for j in range(1, ntens)]
        x = jnp.concatenate(x_parts, axis=1)
        x_flat = x.reshape(count, width)

        qv_col = jnp.pad(b_qv.reshape(-1, 1), ((0, rb - b_qv.size), (0, 0)))
        first_piece = jnp.concatenate(
            [w_qkv.reshape(rb, 3 * local), ln_gains.T, shifts.T, b_up.reshape(-1, 1), qv_col, jnp.zeros((rb, 56), BF)],
            axis=1,
        )
        second_piece = jnp.concatenate([w_up, w_out.T, jnp.zeros((rb, 64), BF)], axis=1)
        w1 = ready(gather(first_piece, "xy"))
        w2 = ready(gather(second_piece, "yx"))
        w3 = ready(gather(w_down.T, "yx"))

        mine = lax.dynamic_slice_in_dim(segments, t * rows, rows, 0).reshape(rows, ntens, part_len)
        own_len = lax.dynamic_slice_in_dim(lengths, t * rows, rows, 0)
        seg = jnp.stack([lax.dynamic_index_in_dim(mine, t ^ j, 1, False) for j in range(ntens)], axis=1)
        place = jnp.stack([(t ^ j) * part_len + jnp.arange(part_len) for j in range(ntens)])
        live = (place[None] < own_len[:, None, None]).reshape(rows, seq)
        seg = seg.reshape(rows, seq)
        key_code = jnp.where(live, seg, -1)
        query_code = jnp.where(live, seg, DEAD)
        sent_code = jnp.where(live, seg + SEGS * jnp.arange(rows)[:, None], -1).reshape(1, count)
        member = (key_code[:, None, :] == jnp.arange(SEGS)[None, :, None]).astype(F32)
        inv_count = (1.0 / jnp.sum(member, axis=2)).reshape(sents, 1)
        own_ids = (d * row_count + t * rows) * SEGS + jnp.arange(sents, dtype=jnp.int32)
        here = pair_ids[None, :] == own_ids[:, None]
        mates = pair_ids.reshape(-1, 2)[:, ::-1].reshape(-1)
        mate = jnp.sum(jnp.where(here, mates[None, :], 0), axis=1, keepdims=True)
        goal = jnp.sum(jnp.where(here, jnp.repeat(targets, 2)[None, :], 0.0), axis=1, keepdims=True)
        own_ids = own_ids[:, None]

        k = np.arange(width)
        dd, within = k // rb, k % rb
        up_at = (within // hb) * hd + dd * hb + within % hb
        sup = np.zeros((width, width), np.float32)
        sup[k, up_at] = 1.0
        qv = within < 2 * heads * hb
        qv_at = (within // (heads * hb)) * local + ((within // hb) % heads) * hd + dd * hb + within % hb
        sqv = np.zeros((width, 2 * local), np.float32)
        sqv[k[qv], qv_at[qv]] = 1.0
        sup, sqv = jnp.asarray(sup, BF), jnp.asarray(sqv, BF)

        wide = w1[0][0].shape[2]

        def attend(pair):
            ws = [v for j in pair for v in w1[j]]
            return call(
                attn_fwd_kernel,
                (2, rows),
                [(lo_bit, None, None), (x, (1, seq, width), lambda j, r, *_: (r, 0, 0))]
                + [(w, None, None) for w in ws]
                + [
                    (sup, None, None),
                    (sqv, None, None),
                    (key_code.reshape(rows, 1, seq), (1, 1, seq), lambda j, r, *_: (r, 0, 0)),
                    (query_code.reshape(rows, seq, 1), (1, seq, 1), lambda j, r, *_: (r, 0, 0)),
                ],
                [
                    ((2, rows, seq, 3 * local), BF, (1, 1, seq, 3 * local), lambda j, r, *_: (j, r, 0, 0)),
                    ((2, rows, heads, seq, seq), BF, (1, 1, heads, seq, seq), lambda j, r, *_: (j, r, 0, 0, 0)),
                    ((2, rows, seq, local), BF, (1, 1, seq, local), lambda j, r, *_: (j, r, 0, 0)),
                    ((2, width, wide), BF, (1, width, wide), lambda j, r, *_: (j, 0, 0)),
                    ((2, 8, width), F32, (1, 8, width), lambda j, r, *_: (j, 0, 0)),
                ],
                scratch=[pltpu.VMEM((8, 2 * local), F32), pltpu.VMEM((seq, seq), F32)],
                scalars=1,
                cost=(4 * 10**9, 12 * MIB, 4 * 10**6),
            )

        near = attend((0, 1))
        far = attend((2, 3))
        small = near[4][0]
        bup_rows = jnp.concatenate([near[4], far[4]], axis=0)
        o_near, o_far = (v[2].reshape(2, count, local) for v in (near, far))

        def rows_of(array, *lead):
            if array.ndim == 3:
                return (array, (array.shape[0], blk, array.shape[2]), lambda i, *_: (0, i, 0))
            return (array, (blk, array.shape[1]), lambda i, *_: (i, 0))

        def rows_out(shape, dtype):
            if len(shape) == 3:
                return (shape, dtype, (shape[0], blk, shape[2]), lambda i, *_: (0, i, 0))
            return (shape, dtype, (blk, shape[1]), lambda i, *_: (i, 0))

        def whole(array):
            return (array, None, None)

        def whole_out(shape, dtype):
            return (shape, dtype, None, None)

        ws2 = [v for j in range(4) for v in w2[j]]
        xh1, rstd1, u, wo = call(
            out_kernel,
            (steps,),
            [whole(lo_bit), rows_of(o_near), rows_of(o_far), rows_of(x_flat), whole(small)]
            + [(w, (depth, rbk, 256), lambda i, *_: (0, 0, hidden // 256)) for w in ws2],
            [
                rows_out((count, width), F32),
                rows_out((count, 1), F32),
                rows_out((count, width), BF),
                whole_out((4, width, local), BF),
            ],
            scalars=1,
            cost=(2 * 10**9, 10 * MIB, 0),
        )
        h, g, wup = call(
            up_kernel,
            (steps,),
            [whole(lo_bit), rows_of(u), whole(bup_rows)]
            + [(w, (depth, rbk, hidden), lambda i, *_: (0, 0, 0)) for w in ws2],
            [
                rows_out((4, count, hidden), BF),
                rows_out((4, count, hidden), BF),
                whole_out((4, width, hidden), BF),
            ],
            scalars=1,
            cost=(5 * 10**9, 20 * MIB, 6 * 10**6),
        )
        code_spec = (sent_code, (1, blk), lambda i, *_: (0, i))
        xh2, rstd2, y_low, wdown, pooled = call(
            down_kernel,
            (steps,),
            [whole(lo_bit), rows_of(h), rows_of(xh1), whole(small), code_spec, whole(inv_count)]
            + [whole(w) for j in range(4) for w in w3[j]],
            [
                rows_out((count, width), F32),
                rows_out((count, 1), F32),
                rows_out((count, width), BF),
                whole_out((4, width, hidden), BF),
                whole_out((sents, width), BF),
            ],
            scratch=[pltpu.VMEM((sents, width), F32)],
            scalars=1,
            cost=(5 * 10**9, 20 * MIB, 0),
        )

        def send_back(array):
            blocks = array.reshape(rows, ntens, part_len, width)
            got = [blocks[:, 0]] + [across(blocks[:, j], "tensor", j) for j in range(1, ntens)]
            (out,) = call(
                collect_kernel,
                (part_len // deal_block,),
                [whole(t_arr)] + [(a, (rows, deal_block, width), lambda i, *_: (0, i, 0)) for a in got],
                [((part_len * row_count, width), BF, (blk, width), lambda i, *_: (i, 0))],
                scalars=1,
                cost=(2 * 1024 * 256 * 768, 3 * MIB, 0),
            )
            return out.reshape(part_len, row_count, width)

        every = lax.all_to_all(
            jnp.broadcast_to(pooled[None], (nd * ntens,) + pooled.shape), ("dp", "tensor"), 0, 0, tiled=True
        ).reshape(nd * ntens * sents, width)
        hidden_out = send_back(y_low)

        df, dz2, de, sums2, dbup = call(
            feed_back_kernel,
            (steps,),
            [whole(every), whole(own_ids), whole(mate), whole(goal), whole(inv_count), code_spec]
            + [rows_of(xh2), rows_of(rstd2), whole(small), whole(wdown), rows_of(g)],
            [
                rows_out((count, width), BF),
                rows_out((count, width), F32),
                rows_out((4, count, hidden), BF),
                whole_out((8, width), F32),
                whole_out((4, 8, hidden), F32),
            ],
            scratch=[pltpu.VMEM((3, sents, width), BF)],
            cost=(5 * 10**9, 20 * MIB, 0),
        )

        def grad_outs(columns):
            shape = (2, 2, depth, rbk, columns)
            return [(shape, BF, (1,) + shape[1:], lambda j, *_: (j // 2, 0, 0, 0, 0))] * 2

        by_j = lambda array: (array, (1,) + array.shape[1:], lambda j, *_: (j, 0, 0))
        keep3, send3 = call(
            grad_kernel,
            (4,),
            [whole(lo_bit), whole(df), by_j(h)],
            grad_outs(hidden),
            scalars=1,
            cost=(5 * 10**9, 15 * MIB, 0),
        )
        grad_down = reduce(cut(keep3), cut(send3), "xy")
        dz1, da, do, sums1 = call(
            norm_back_kernel,
            (steps,),
            [rows_of(de), rows_of(dz2), rows_of(xh1), rows_of(rstd1), whole(small), whole(wup), whole(wo)],
            [
                rows_out((count, width), F32),
                rows_out((count, width), BF),
                rows_out((4, count, local), BF),
                whole_out((8, width), F32),
            ],
            cost=(6 * 10**9, 20 * MIB, 0),
        )
        o_all = jnp.concatenate([o_near, o_far], axis=0)
        keep2, send2 = call(
            grad_two_kernel,
            (4,),
            [whole(lo_bit), whole(u), by_j(de), whole(da), by_j(o_all)],
            grad_outs(hidden + 256),
            scalars=1,
            cost=(6 * 10**9, 15 * MIB, 0),
        )
        grad_two = reduce(cut(keep2), cut(send2), "yx")

        do_rows = do.reshape(2, 2, rows, seq, local)

        def attend_back(kept, do_pair, dx_in):
            per = lambda j, r, *_: (j, r, 0, 0)
            shape = (1, 2, depth, rbk, wide)
            return call(
                attn_bwd_kernel,
                (2, rows),
                [
                    whole(lo_bit),
                    (kept[0], (1, 1, seq, 3 * local), per),
                    (kept[1], (1, 1, heads, seq, seq), lambda j, r, *_: (j, r, 0, 0, 0)),
                    (kept[2], (1, 1, seq, local), per),
                    (do_pair, (1, 1, seq, local), per),
                    (x, (1, seq, width), lambda j, r, *_: (r, 0, 0)),
                    (kept[3], (1, width, wide), lambda j, r, *_: (j, 0, 0)),
                    whole(dx_in),
                ],
                [
                    whole_out(shape, BF),
                    whole_out(shape, BF),
                    whole_out((rows, seq, width), F32),
                    ((2, 8, 3 * local), F32, (1, 8, 3 * local), lambda j, r, *_: (j, 0, 0)),
                ],
                scratch=[pltpu.VMEM((width, 3 * local), F32)],
                scalars=1,
                cost=(9 * 10**9, 20 * MIB, 0),
            )

        keep_f, send_f, dx, sum_f = attend_back(far, do_rows[1], dz1.reshape(rows, seq, width))
        keep_n, send_n, dx, sum_n = attend_back(near, do_rows[0], dx)
        grad_tokens = send_back(dx.astype(BF))
        keep1 = jnp.concatenate([keep_n, keep_f], axis=0)
        send1 = jnp.concatenate([send_n, send_f], axis=0)
        grad_one = reduce(cut(keep1), cut(send1), "xy")

        def to_axes(rows_by_d):
            order = jnp.arange(ntens) ^ t
            return jnp.take(rows_by_d, order, axis=0).transpose(1, 0, 2)

        sums = jnp.concatenate([sum_n[:, 0], sum_f[:, 0]], axis=0)
        qv_sum = jnp.stack([sums[:, :local], sums[:, 2 * local :]], axis=1)
        qv_sum = qv_sum.reshape(4, 2 * heads, nd, hb).transpose(0, 2, 1, 3).reshape(4, nd, 2 * heads * hb)
        up_sum = dbup[:, 0].reshape(4, hidden // hd, nd, hb).transpose(0, 2, 1, 3).reshape(4, nd, -1)
        norms = jnp.stack([sums1[0], sums2[0], sums1[2], sums1[1], sums2[2], sums2[1]])
        norms = norms.reshape(6, nd, ntens, -1).transpose(1, 2, 0, 3).reshape(nd, ntens, -1)
        message = jnp.concatenate([to_axes(qv_sum), to_axes(up_sum), norms], axis=2)
        message = message.reshape(nd * ntens, 1, -1)
        got = jnp.sum(lax.all_to_all(message, ("dp", "tensor"), 0, 0, tiled=True), axis=(0, 1))
        n1 = qv_sum.shape[2]
        n2 = n1 + up_sum.shape[2]
        grad_b_qv = got[:n1].reshape(2, heads, hb)
        grad_b_up = got[n1:n2].reshape(hidden // hd, hb)
        rest = got[n2:].reshape(6, -1)
        return (
            hidden_out,
            grad_tokens,
            grad_one[:, : 3 * local].reshape(rb, 3, local),
            grad_b_qv,
            grad_two[:, hidden : hidden + local].T,
            grad_two[:, :hidden],
            grad_b_up,
            grad_down.T,
            rest[:2],
            rest[2:],
        )

    return shards


def solution(mesh):
    return jax.shard_map(
        make(mesh),
        mesh=mesh,
        in_specs=(
            P("tensor", "dp", None),
            P("dp", None, "tensor"),
            P(None, "tensor", "dp"),
            P("tensor", "dp"),
            P("dp", "tensor"),
            P("tensor", "dp"),
            P("tensor", "dp"),
            P(None, "dp"),
            P(None, "dp"),
            P("dp"),
            P("dp", None),
            P(),
            P(),
        ),
        out_specs=(
            P("tensor", "dp", None),
            P("tensor", "dp", None),
            P("dp", None, "tensor"),
            P(None, "tensor", "dp"),
            P("tensor", "dp"),
            P("dp", "tensor"),
            P("tensor", "dp"),
            P("tensor", "dp"),
            P(None, ("dp", "tensor")),
            P(None, ("dp", "tensor")),
        ),
        check_vma=False,
    )
```

```python
import functools
import math

import jax
import jax.numpy as jnp
import numpy as np
from jax import lax
from jax.experimental import pallas as pl
from jax.experimental.pallas import tpu as pltpu
from jax.sharding import PartitionSpec as P

SEGS = 4
EPS_NORM = 1e-05
EPS_COS = 1e-06
LOSS_SCALE = 4096.0
NEG = -1e30
DEAD = 99

BF = jnp.bfloat16
F32 = jnp.float32
MIB = 1024 * 1024
SHARE = 0.05


def dot(a, b, ca, cb):
    return lax.dot_general(a, b, (((ca,), (cb,)), ((), ())), preferred_element_type=F32)


def nn(a, b):
    return dot(a, b, 1, 0)


def nt(a, b):
    return dot(a, b, 1, 1)


def tn(a, b):
    return dot(a, b, 0, 0)


def call(kernel, grid, ins, outs, scratch=(), limit=60, cost=1.0, scalars=0, after=()):
    def spec(shape, block, index):
        if block is None:
            zeros = (0,) * len(shape)
            return pl.BlockSpec(shape, lambda *_: zeros)
        return pl.BlockSpec(block, index)

    in_specs = [spec(a.shape, b, m) for a, b, m in ins[scalars:]]
    out_specs = [spec(s, b, m) for s, _, b, m in outs]
    flops = int(cost * SHARE * 1.15e9)
    body, known = kernel, len(ins)
    if after:
        in_specs += [pl.BlockSpec(memory_space=pl.ANY)] * len(after)

        def body(*refs):
            return kernel(*refs[:known], *refs[known + len(after) :])

    return pl.pallas_call(
        body,
        grid_spec=pltpu.PrefetchScalarGridSpec(
            num_scalar_prefetch=scalars,
            grid=grid,
            in_specs=in_specs,
            out_specs=out_specs,
            scratch_shapes=list(scratch),
        ),
        out_shape=[jax.ShapeDtypeStruct(s, d) for s, d, _, _ in outs],
        compiler_params=pltpu.CompilerParams(
            dimension_semantics=("arbitrary",) * len(grid), vmem_limit_bytes=limit * MIB
        ),
        cost_estimate=pl.CostEstimate(flops=flops, bytes_accessed=1024, transcendentals=0),
    )(*[a for a, _, _ in ins], *after)


def gate(arrays, after):
    n = len(arrays)
    anywhere = pl.BlockSpec(memory_space=pl.ANY)
    return pl.pallas_call(
        lambda *refs: None,
        in_specs=[anywhere] * (n + len(after)),
        out_specs=[anywhere] * n,
        out_shape=[jax.ShapeDtypeStruct(a.shape, a.dtype) for a in arrays],
        input_output_aliases={i: i for i in range(n)},
        cost_estimate=pl.CostEstimate(flops=1, bytes_accessed=1, transcendentals=0),
    )(*arrays, *after)


def deal_kernel(t_ref, tok_ref, *out_refs):
    size = tok_ref.shape[0]
    parts = len(out_refs)
    rows, block = out_refs[0].shape[0], out_refs[0].shape[1]
    t = t_ref[0]
    m = lax.broadcasted_iota(jnp.int32, (size, size), 0)
    n = lax.broadcasted_iota(jnp.int32, (size, size), 1)
    part, row, place = m // (rows * block), (m // block) % rows, m % block
    source = place * (parts * rows) + jnp.bitwise_xor(part, t) * rows + row
    pick = jnp.where(source == n, 1.0, 0.0).astype(BF)
    moved = nn(pick, tok_ref[...]).astype(BF)
    for j, out in enumerate(out_refs):
        for r in range(rows):
            at = (j * rows + r) * block
            out[r] = moved[at : at + block]


def collect_kernel(t_ref, *refs):
    *in_refs, out_ref = refs
    size = out_ref.shape[0]
    parts = len(in_refs)
    rows, block = in_refs[0].shape[0], in_refs[0].shape[1]
    t = t_ref[0]
    m = lax.broadcasted_iota(jnp.int32, (size, size), 1)
    n = lax.broadcasted_iota(jnp.int32, (size, size), 0)
    part, row, place = m // (rows * block), (m // block) % rows, m % block
    target = place * (parts * rows) + jnp.bitwise_xor(part, t) * rows + row
    pick = jnp.where(target == n, 1.0, 0.0).astype(BF)
    joined = jnp.concatenate([ref[r] for ref in in_refs for r in range(rows)], axis=0)
    out_ref[...] = nn(pick, joined).astype(BF)


def stack_kernel(*refs):
    *ins, out_ref = refs
    for i, ref in enumerate(ins):
        out_ref[i] = ref[...]


def merge_kernel(here_ref, own_ref, other_ref, out_ref):
    depth, rows = own_ref.shape[0], own_ref.shape[1]
    lo = here_ref[0]
    for z in range(depth):
        at = lax.rem(z + depth - here_ref[1], depth)
        mine, theirs = own_ref[at], other_ref[at]
        for b in range(2):
            at = (2 * z + b) * rows
            out_ref[at : at + rows, :] = jnp.where(lo == b, mine, theirs)


def attn_fwd_kernel(parts, *refs):
    x_refs, refs = refs[:parts], refs[parts:]
    w_ref, sqv_ref, kc_ref, qc_ref, qkv_ref, p_ref, o_ref, *refs = refs
    *x_out, bias_ref, mask_ref = refs
    local = o_ref.shape[2]
    heads = p_ref.shape[1]
    hd = local // heads

    @pl.when(pl.program_id(0) == 0)
    def _():
        bias_ref[...] = tn(w_ref[:, 3 * local :][:, :8], sqv_ref[...])

    x = x_refs[0][0]
    if parts > 1:
        x = jnp.concatenate([ref[0] for ref in x_refs], axis=0)
        x_out[0][0] = x
    kc, qc = kc_ref[0], qc_ref[0]
    allowed = (kc == qc) | ((qc == DEAD) & (kc >= 0))
    mask_ref[...] = jnp.where(allowed, 0.0, NEG)

    projected = nn(x, w_ref[:, : 3 * local])
    q_all = ((projected[:, :local] + bias_ref[0:1, :local]) * 0.125).astype(BF)
    k_all = projected[:, local : 2 * local].astype(BF)
    v_all = (projected[:, 2 * local :] + bias_ref[0:1, local:]).astype(BF)
    qkv_ref[0, :, :local] = q_all
    qkv_ref[0, :, local : 2 * local] = k_all
    qkv_ref[0, :, 2 * local :] = v_all
    outs = []
    for h in range(heads):
        at = slice(h * hd, (h + 1) * hd)
        s = nt(q_all[:, at], k_all[:, at]) + mask_ref[...]
        top = jnp.max(s, axis=-1, keepdims=True)
        e = jnp.exp(s - top)
        total = jnp.sum(e, axis=-1, keepdims=True)
        p = (e * (1.0 / total)).astype(BF)
        p_ref[0, h] = p
        outs.append(nn(p, v_all[:, at]).astype(BF))
    o_ref[0] = jnp.concatenate(outs, axis=1)


def norm(z):
    centred = z - jnp.mean(z, axis=-1, keepdims=True)
    rstd = lax.rsqrt(jnp.mean(centred * centred, axis=-1, keepdims=True) + EPS_NORM)
    return centred * rstd, rstd


def norm_back(dy, xh, rstd, gain):
    dxh = dy * gain
    mean = jnp.mean(dxh, axis=-1, keepdims=True)
    proj = jnp.mean(dxh * xh, axis=-1, keepdims=True)
    return rstd * (dxh - mean - xh * proj)


def out_kernel(o0, o1, o2, o3, x_ref, sup_ref, w0, w1, w2, w3, xh_ref, rstd_ref, u_ref, small_ref, bup_ref):
    local = o0.shape[1]
    width = x_ref.shape[1]
    ws = (w0, w1, w2, w3)

    @pl.when(pl.program_id(0) == 0)
    def _():
        eye = (
            lax.broadcasted_iota(jnp.int32, (width, width), 0)
            == lax.broadcasted_iota(jnp.int32, (width, width), 1)
        ).astype(BF)
        small_ref[...] = tn(w0[:, local:][:, :8], eye)
        for j in range(4):
            bup_ref[j] = tn(ws[j][:, local:][:, :8], sup_ref[...])

    a = nt(o0[...], w0[:, :local])
    for w, o in ((w1, o1), (w2, o2), (w3, o3)):
        a += nt(o[...], w[:, :local])
    z = x_ref[...].astype(F32) + (a + small_ref[2:3])
    xh, rstd = norm(z)
    xh_ref[...] = xh
    rstd_ref[...] = rstd
    u_ref[...] = (xh * small_ref[0:1] + small_ref[3:4]).astype(BF)


def turned(a):
    rows = a.shape[1]
    eye = (
        lax.broadcasted_iota(jnp.int32, (rows, rows), 0) == lax.broadcasted_iota(jnp.int32, (rows, rows), 1)
    ).astype(BF)
    return nt(eye, a).astype(BF)


def pack_one_kernel(w_ref, extra_ref, piece_ref):
    piece_ref[...] = jnp.concatenate([w_ref[...], extra_ref[...]], axis=1)


def pack_two_kernel(up_ref, out_ref, extra_ref, piece_ref):
    hidden = up_ref.shape[1]
    piece_ref[0, :, :hidden] = up_ref[...]
    piece_ref[0, :, hidden:] = jnp.concatenate([turned(out_ref[...]), extra_ref[...]], axis=1)


def pack_three_kernel(a_ref, piece_ref):
    piece_ref[0] = turned(a_ref[...])


def gelu_parts(e):
    size = jnp.abs(e)
    density = jnp.exp(-0.5 * e * e)
    t = 1.0 / (1.0 + (0.3275911 / math.sqrt(2.0)) * size)
    poly = t * (
        0.5 * 0.254829592
        + t * (0.5 * -0.284496736 + t * (0.5 * 1.421413741 + t * (0.5 * -1.453152027 + t * (0.5 * 1.061405429))))
    )
    tail = poly * density
    cdf = jnp.where(e < 0, tail, 1.0 - tail)
    return e * cdf, cdf + e * (density * (1.0 / math.sqrt(2.0 * math.pi)))


def up_kernel(u_ref, bup_ref, w0, w1, w2, w3, h_ref, g_ref):
    u = u_ref[...]
    for j, w in enumerate((w0, w1, w2, w3)):
        e = nn(u, w[...]) + bup_ref[j, 6:7]
        h, g = gelu_parts(e)
        h_ref[j] = h.astype(BF)
        g_ref[j] = g.astype(BF)


def split3(v):
    a = v.astype(BF)
    rest = v - a.astype(F32)
    b = rest.astype(BF)
    c = (rest - b.astype(F32)).astype(BF)
    return a, b, c


def down_kernel(
    h_ref, xh1_ref, small_ref, code_ref, inv_ref, w0, w1, w2, w3,
    xh_ref, rstd_ref, y0, y1, y2, y3, pool_ref, acc_ref,
):
    y_refs = (y0, y1, y2, y3)
    step = pl.program_id(0)

    @pl.when(step == 0)
    def _():
        acc_ref[...] = jnp.zeros_like(acc_ref)

    f = nt(h_ref[0], w0[...])
    for j, w in ((1, w1), (2, w2), (3, w3)):
        f += nt(h_ref[j], w[...])
    first = xh1_ref[...] * small_ref[0:1] + small_ref[3:4]
    xh, rstd = norm(first + (f + small_ref[4:5]))
    y2 = xh * small_ref[1:2] + small_ref[5:6]
    xh_ref[...] = xh
    rstd_ref[...] = rstd
    low = y2.astype(BF)
    size = y_refs[0].shape[1]
    here = low.shape[0] // size
    for j, ref in enumerate(y_refs):

        @pl.when(lax.rem(step, 4 // here) == j // here)
        def _():
            ref[0] = low[(j % here) * size : (j % here + 1) * size]

    member = (lax.broadcasted_iota(jnp.int32, (8, y2.shape[0]), 0) == code_ref[...]).astype(BF)
    a, b, c = split3(y2)
    acc_ref[...] += nn(member, a) + nn(member, b) + nn(member, c)

    @pl.when(step == pl.num_programs(0) - 1)
    def _():
        low = (acc_ref[...] * inv_ref[...]).astype(BF)

        def put(i, carry):
            pool_ref[i] = low
            return carry

        lax.fori_loop(0, pool_ref.shape[0], put, 0)


def loss_grad(pooled_ref, ids_ref, mate_ref, target_ref, inv_ref):
    pooled = pooled_ref[...]
    places = lax.broadcasted_iota(jnp.int32, (8, pooled.shape[0]), 1)
    first = nn((places == ids_ref[...]).astype(BF), pooled)
    second = nn((places == mate_ref[...]).astype(BF), pooled)
    inner = jnp.sum(first * second, axis=-1, keepdims=True)
    ra = lax.rsqrt(jnp.sum(first * first, axis=-1, keepdims=True) + EPS_COS)
    rb = lax.rsqrt(jnp.sum(second * second, axis=-1, keepdims=True) + EPS_COS)
    missed = inner * ra * rb - target_ref[...]
    grad = (2.0 * LOSS_SCALE) * missed * (second * (ra * rb) - first * (inner * rb * ra * ra * ra))
    return grad * inv_ref[...]


def rowsum(v):
    return jnp.sum(v, axis=0, keepdims=True)


def feed_back_kernel(
    pooled_ref, ids_ref, mate_ref, target_ref, inv_ref, code_ref, xh_ref, rstd_ref, small_ref, w0, w1, w2, w3, g_ref,
    df_ref, dz_ref, de_ref, sum_ref, bup_ref, gp_ref,
):
    step = pl.program_id(0)

    @pl.when(step == 0)
    def _():
        grad = loss_grad(pooled_ref, ids_ref, mate_ref, target_ref, inv_ref)
        for i, part in enumerate(split3(grad)):
            gp_ref[i] = part
        sum_ref[...] = jnp.zeros_like(sum_ref)
        bup_ref[...] = jnp.zeros_like(bup_ref)

    member = (lax.broadcasted_iota(jnp.int32, (8, xh_ref.shape[0]), 0) == code_ref[...]).astype(BF)
    dy = tn(member, gp_ref[0]) + tn(member, gp_ref[1]) + tn(member, gp_ref[2])
    xh = xh_ref[...]
    dz = norm_back(dy, xh, rstd_ref[...], small_ref[1:2])
    sum_ref[0:1] += rowsum(dy * xh)
    sum_ref[1:2] += rowsum(dy)
    sum_ref[2:3] += rowsum(dz)
    df = dz.astype(BF)
    df_ref[...] = df
    dz_ref[...] = dz
    for j, w in enumerate((w0, w1, w2, w3)):
        de = (nn(df, w[...]) * g_ref[j].astype(F32)).astype(BF)
        de_ref[j] = de
        bup_ref[j, 0:1] += rowsum(de.astype(F32))


def norm_back_kernel(
    de_ref, dz2_ref, xh_ref, rstd_ref, small_ref, w0, w1, w2, w3, o0, o1, o2, o3, dz_ref, da_ref, do_ref, sum_ref
):
    @pl.when(pl.program_id(0) == 0)
    def _():
        sum_ref[...] = jnp.zeros_like(sum_ref)

    dy = nt(de_ref[0], w0[...])
    for j, w in ((1, w1), (2, w2), (3, w3)):
        dy += nt(de_ref[j], w[...])
    dy = dz2_ref[...] + dy
    xh = xh_ref[...]
    dz = norm_back(dy, xh, rstd_ref[...], small_ref[0:1])
    sum_ref[0:1] += rowsum(dy * xh)
    sum_ref[1:2] += rowsum(dy)
    sum_ref[2:3] += rowsum(dz)
    da = dz.astype(BF)
    dz_ref[...] = dz
    da_ref[...] = da
    for j, w in enumerate((o0, o1, o2, o3)):
        do_ref[j] = nn(da, w[:, : do_ref.shape[2]]).astype(BF)


def pieces(grad, here_ref, ref, at):
    depth, rows = ref.shape[1], ref.shape[2]
    lo = here_ref[0]
    low = grad.astype(BF)
    for z in range(depth):
        first, second = (low[(2 * z + b) * rows : (2 * z + b + 1) * rows] for b in range(2))
        ref[0, z, :, at] = jnp.where(lo == 0, first, second)
        ref[1, z, :, at] = jnp.where(lo == 0, second, first)


def grad_send_kernel(here_ref, *refs):
    *ins, send_ref = refs
    at = 0
    for grad in (tn(a[...], b[0]) for a, b in zip(ins[::2], ins[1::2])):
        pieces(grad, here_ref, send_ref.at[0], slice(at, at + grad.shape[1]))
        at += grad.shape[1]


def grad_keep_kernel(by_row, here_ref, *refs):
    *ins, got_ref, stay_ref, fly_ref = refs
    depth, rows = got_ref.shape[2], got_ref.shape[3]
    lo = here_ref[0]
    j = pl.program_id(0)
    at = 0
    for grad in (tn(a[...], b[0]) for a, b in zip(ins[::2], ins[1::2])):
        cols = slice(at, at + grad.shape[1])
        for z in range(depth):
            first, second = (grad[(2 * z + b) * rows : (2 * z + b + 1) * rows] for b in range(2))
            mine, theirs = jnp.where(lo == 0, first, second), jnp.where(lo == 0, second, first)
            mine = (mine + got_ref[0, 0, z, :, cols].astype(F32)).astype(BF)
            theirs = (theirs + got_ref[0, 1, z, :, cols].astype(F32)).astype(BF)
            if by_row:
                stay_ref[0, z, :, cols] = mine
                fly_ref[0, z, :, cols] = theirs
            else:

                @pl.when(j == 0)
                def _():
                    stay_ref[0, z, :, cols] = mine
                    stay_ref[1, z, :, cols] = theirs

                @pl.when(j == 1)
                def _():
                    fly_ref[0, z, :, cols] = mine
                    fly_ref[1, z, :, cols] = theirs

        at += grad.shape[1]


def attn_bwd_kernel(
    here_ref, qkv_ref, p_ref, o_ref, do_ref, x_ref, da_ref, w_ref, dxin_ref, piece_ref, sum_ref, *refs
):
    *dx_refs, acc_ref = refs
    r = pl.program_id(0)
    local = o_ref.shape[2]
    heads = p_ref.shape[1]
    hd = local // heads
    q_all, k_all, v_all = (qkv_ref[0, :, i * local : (i + 1) * local] for i in range(3))
    o_all, do_all = o_ref[0], do_ref[0]
    prod = o_all.astype(F32) * do_all.astype(F32)
    dq, dk, dv = [], [], []
    for h in range(heads):
        at = slice(h * hd, (h + 1) * hd)
        p = p_ref[0, h]
        do = do_all[:, at]
        dv.append(tn(do, p))
        dp = nt(do, v_all[:, at])
        mid = jnp.sum(prod[:, at], axis=-1, keepdims=True)
        ds = (p.astype(F32) * (dp - mid)).astype(BF)
        dq.append(nn(ds, k_all[:, at]))
        dk.append(tn(q_all[:, at], ds))
    dq = (jnp.concatenate(dq, axis=1).astype(BF).astype(F32) * 0.125).astype(BF)
    dkv = jnp.concatenate(dk + dv, axis=0).astype(BF).astype(F32)
    dkv = jnp.transpose(dkv).astype(BF)
    dproj = jnp.concatenate([dq, dkv], axis=1)
    sums = rowsum(dproj.astype(F32))
    grad = jnp.concatenate([tn(x_ref[0], dproj), tn(da_ref[0], o_all)], axis=1)

    @pl.when(r == 0)
    def _():
        acc_ref[...] = grad
        sum_ref[...] = jnp.broadcast_to(sums, sum_ref.shape)

    @pl.when(r > 0)
    def _():
        acc_ref[...] += grad
        sum_ref[...] += jnp.broadcast_to(sums, sum_ref.shape)

    @pl.when(r == pl.num_programs(0) - 1)
    def _():
        pieces(acc_ref[...], here_ref, piece_ref, slice(0, acc_ref.shape[1]))

    dx = dxin_ref[0] + nt(dproj, w_ref[:, : 3 * local])
    if len(dx_refs) == 1:
        dx_refs[0][0] = dx
    else:
        low = dx.astype(BF)
        size = dx_refs[0].shape[1]
        for j, ref in enumerate(dx_refs):
            ref[0] = low[j * size : (j + 1) * size]


def make(mesh):
    nd, ntens = mesh.shape["dp"], mesh.shape["tensor"]
    nh = nd // 2
    groups = [[2 * z + b for z in range(nh)] for b in range(2)]

    def across(array, axis, bit):
        size = nd if axis == "dp" else ntens
        return lax.ppermute(array, axis, [(i, i ^ bit) for i in range(size)])

    def along(array):
        return lax.all_to_all(array, "dp", 0, 0, tiled=True, axis_index_groups=groups)

    def turn(array, k):
        return lax.ppermute(array, "dp", [(2 * ((z + k) % nh) + b, 2 * z + b) for z in range(nh) for b in range(2)])

    def swap(array):
        return across(array, "tensor", 1)

    def total(*arrays):
        out = arrays[0].astype(F32)
        for a in arrays[1:]:
            out = out + a.astype(F32)
        return out

    def settle(array):
        return jnp.sum(array.astype(F32), axis=0)

    def shards(
        tokens, w_qkv, b_qv, w_out, w_up, b_up, w_down, ln_gains, shifts, lengths, segments, pair_ids, targets
    ):
        part_len, row_count, width = tokens.shape
        rb = w_up.shape[0]
        hidden = w_up.shape[1]
        local = w_qkv.shape[2]
        hb = b_up.shape[1]
        hd = hb * nd
        heads = local // hd
        seq = segments.shape[1]
        rows = row_count // ntens
        count = rows * seq
        sents = rows * SEGS
        blk = 256
        steps = count // blk
        t = lax.axis_index("tensor")
        d = lax.axis_index("dp")
        fused = rb % 16 == 0
        depth, rbk = (nh, rb) if fused else (1, width // 2)
        lo_bit = (d % 2 if fused else d * 0).astype(jnp.int32)
        turned_by = (d // 2 if nh <= 4 else d * 0).astype(jnp.int32)
        here, here_first = jnp.stack([lo_bit, lo_bit * 0]), jnp.stack([lo_bit, turned_by])
        t_arr = t.astype(jnp.int32).reshape(1)

        def merged(own, other, after=(), place=here):
            if not fused:
                first = jnp.where(d % 2 == 0, own, other)
                second = jnp.where(d % 2 == 0, other, own)
                return jnp.stack([first, second], axis=1).reshape(width, own.shape[2])
            columns = own.shape[2]
            return call(
                merge_kernel,
                (1,),
                [(place, None, None), (own, None, None), (other, None, None)],
                [((width, columns), BF, None, None)],
                scalars=1,
                after=after,
                cost=1.0,
                limit=16,
            )[0]

        def pack(kernel, arrays, columns, after):
            return call(
                kernel,
                (nh,),
                [(a, None, None) for a in arrays],
                [((nh, rb, columns), BF, (1, rb, columns), lambda i: (i, 0, 0))],
                after=after,
                limit=16,
            )[0]

        def cut(array):
            if fused:
                return array
            lead = array.shape[:-4]
            full = array.reshape(*lead, nh, 2, rb, array.shape[-1])
            first, second = full[..., 0, :, :], full[..., 1, :, :]
            return jnp.stack(
                [jnp.where(d % 2 == 0, first, second), jnp.where(d % 2 == 0, second, first)], axis=len(lead)
            )

        def uncut(array):
            if fused:
                return array
            mine, theirs = array[..., 0, :, :, :], array[..., 1, :, :, :]
            first, second = jnp.where(d % 2 == 0, mine, theirs), jnp.where(d % 2 == 0, theirs, mine)
            return jnp.stack([first, second], axis=-3).reshape(*array.shape[:-4], 2, 1, width // 2, array.shape[-1])

        deal_block = blk // row_count
        dealt = call(
            deal_kernel,
            (part_len // deal_block,),
            [(t_arr, None, None), (tokens.reshape(part_len * row_count, width), (blk, width), lambda i, *_: (i, 0))],
            [((rows, part_len, width), BF, (rows, deal_block, width), lambda i, *_: (0, i, 0))] * ntens,
            scalars=1,
            cost=2.0,
            limit=16,
        )
        x_parts = [dealt[0]] + [across(dealt[j], "tensor", j) for j in range(1, ntens)]

        qv_col = jnp.pad(b_qv.reshape(-1, 1), ((0, rb - b_qv.size), (0, 63)))
        wide = 3 * local + 64
        (first_piece,) = call(
            pack_one_kernel,
            (1,),
            [(w_qkv.reshape(rb, 3 * local), None, None), (qv_col, None, None)],
            [((rb, wide), BF, None, None)],
            limit=16,
        )
        if nh <= 4:
            pieces1 = [first_piece] + [turn(first_piece, k) for k in range(1, nh)]
            own1 = call(
                stack_kernel,
                (1,),
                [(p, None, None) for p in pieces1],
                [((nh, rb, wide), BF, None, None)],
                after=[dealt[1]],
                limit=16,
            )[0]
        else:
            own1 = along(jnp.broadcast_to(first_piece[None], (nh, rb, wide)))
        lo1 = across(own1, "dp", 1)
        w1 = {0: merged(own1, lo1, place=here_first)}
        w1[1] = swap(w1[0])
        w1[2] = across(w1[0], "tensor", 2)
        extra = jnp.concatenate([ln_gains.T, shifts.T, b_up.reshape(-1, 1), jnp.zeros((rb, 57), BF)], axis=1)
        second_piece = pack(pack_two_kernel, [w_up, w_out, extra], hidden + 256, [dealt[1]])
        (second_piece,) = gate([second_piece], [lo1])
        own2 = along(second_piece)
        third_piece = pack(pack_three_kernel, [w_down], hidden, [dealt[1]])

        mine = lax.dynamic_slice_in_dim(segments, t * rows, rows, 0).reshape(rows, ntens, part_len)
        own_len = lax.dynamic_slice_in_dim(lengths, t * rows, rows, 0)
        seg = jnp.stack([lax.dynamic_index_in_dim(mine, t ^ j, 1, False) for j in range(ntens)], axis=1)
        place = jnp.stack([(t ^ j) * part_len + jnp.arange(part_len) for j in range(ntens)])
        live = (place[None] < own_len[:, None, None]).reshape(rows, seq)
        seg = seg.reshape(rows, seq)
        key_code = jnp.where(live, seg, -1)
        query_code = jnp.where(live, seg, DEAD)
        sent_code = jnp.where(live, seg + SEGS * jnp.arange(rows)[:, None], -1).reshape(1, count)
        member = (key_code[:, None, :] == jnp.arange(SEGS)[None, :, None]).astype(F32)
        inv_count = (1.0 / jnp.sum(member, axis=2)).reshape(sents, 1)
        own_ids = (d * row_count + t * rows) * SEGS + jnp.arange(sents, dtype=jnp.int32)
        is_mine = pair_ids[None, :] == own_ids[:, None]
        mates = pair_ids.reshape(-1, 2)[:, ::-1].reshape(-1)
        mate = jnp.sum(jnp.where(is_mine, mates[None, :], 0), axis=1, keepdims=True)
        goal = jnp.sum(jnp.where(is_mine, jnp.repeat(targets, 2)[None, :], 0.0), axis=1, keepdims=True)
        own_ids = own_ids[:, None]

        k = np.arange(width)
        dd, within = k // rb, k % rb
        up_at = (within // hb) * hd + dd * hb + within % hb
        sup = np.zeros((width, width), np.float32)
        sup[k, up_at] = 1.0
        qv = within < 2 * heads * hb
        qv_at = (within // (heads * hb)) * local + ((within // hb) % heads) * hd + dd * hb + within % hb
        sqv = np.zeros((width, 2 * local), np.float32)
        sqv[k[qv], qv_at[qv]] = 1.0
        sup, sqv = jnp.asarray(sup, BF), jnp.asarray(sqv, BF)

        def whole(array):
            return (array, None, None)

        def whole_out(shape, dtype):
            return (shape, dtype, None, None)

        def attend(xs, w, before):
            outs = [
                ((rows, seq, 3 * local), BF, (1, seq, 3 * local), lambda r, *_: (r, 0, 0)),
                ((rows, heads, seq, seq), BF, (1, heads, seq, seq), lambda r, *_: (r, 0, 0, 0)),
                ((rows, seq, local), BF, (1, seq, local), lambda r, *_: (r, 0, 0)),
            ]
            if len(xs) > 1:
                outs.append(((rows, seq, width), BF, (1, seq, width), lambda r, *_: (r, 0, 0)))
            return call(
                functools.partial(attn_fwd_kernel, len(xs)),
                (rows,),
                [(a, (1,) + a.shape[1:], lambda r, *_: (r, 0, 0)) for a in xs]
                + [
                    whole(w),
                    whole(sqv),
                    (key_code.reshape(rows, 1, seq), (1, 1, seq), lambda r, *_: (r, 0, 0)),
                    (query_code.reshape(rows, seq, 1), (1, seq, 1), lambda r, *_: (r, 0, 0)),
                ],
                outs,
                scratch=[pltpu.VMEM((8, 2 * local), F32), pltpu.VMEM((seq, seq), F32)],
                after=before,
                cost=9.0,
            )

        kept = {}
        *kept[0], x = attend(x_parts, w1[0], [second_piece])
        (own2,) = gate([own2], [kept[0][2]])
        lo2 = across(own2, "dp", 1)
        (third_piece,) = gate([third_piece], [own2])
        own3 = along(third_piece)
        kept[1] = attend([x], w1[1], [own2])
        (w1[2],) = gate([w1[2]], [kept[1][2]])
        far2 = across(own2, "tensor", 2)
        w1[3] = swap(w1[2])
        kept[2] = attend([x], w1[2], [])
        own3, lo2 = gate([own3, lo2], [kept[2][2]])
        lo3 = across(own3, "dp", 1)
        w2 = {0: merged(own2, lo2)}
        w2[1] = swap(w2[0])
        kept[3] = attend([x], w1[3], [own3, w2[0]])
        (far2,) = gate([far2], [kept[3][2]])
        far_lo2 = across(far2, "dp", 1)
        (lo3,) = gate([lo3], [kept[3][2]])
        w3 = {0: merged(own3, lo3, [far2])}
        w3[2] = across(w3[0], "tensor", 2)
        w3[1], w3[3] = swap(w3[0]), swap(w3[2])
        w2[2] = merged(far2, far_lo2, [w3[0]])
        w2[3] = swap(w2[2])
        ws2, ws3 = [w2[j] for j in range(4)], [w3[j] for j in range(4)]
        o_parts = [kept[j][2].reshape(count, local) for j in range(4)]
        x_flat = x.reshape(count, width)

        def rows_of(array, *lead):
            if array.ndim == 3:
                return (array, (array.shape[0], blk, array.shape[2]), lambda i, *_: (0, i, 0))
            return (array, (blk, array.shape[1]), lambda i, *_: (i, 0))

        def rows_out(shape, dtype):
            if len(shape) == 3:
                return (shape, dtype, (shape[0], blk, shape[2]), lambda i, *_: (0, i, 0))
            return (shape, dtype, (blk, shape[1]), lambda i, *_: (i, 0))

        ups = [(w, (width, hidden), lambda i, *_: (0, 0)) for w in ws2]
        outs_w = [(w, (width, 256), lambda i, *_: (0, hidden // 256)) for w in ws2]
        xh1, rstd1, u, small, bup_rows = call(
            out_kernel,
            (steps,),
            [rows_of(o) for o in o_parts] + [rows_of(x_flat), whole(sup)] + outs_w,
            [
                rows_out((count, width), F32),
                rows_out((count, 1), F32),
                rows_out((count, width), BF),
                whole_out((8, width), F32),
                whole_out((4, 8, hidden), F32),
            ],
            cost=8.0,
        )
        h, g = call(
            up_kernel,
            (steps,),
            [rows_of(u), whole(bup_rows)] + ups,
            [rows_out((4, count, hidden), BF), rows_out((4, count, hidden), BF)],
            cost=20.0,
        )
        code_spec = (sent_code, (1, blk), lambda i, *_: (0, i))
        span = blk // part_len
        part_out = lambda i, *_: (i * span // ntens, 0, 0)
        xh2, rstd2, y0, y1, y2, y3, pooled = call(
            down_kernel,
            (steps,),
            [rows_of(h), rows_of(xh1), whole(small), code_spec, whole(inv_count)] + [whole(w) for w in ws3],
            [rows_out((count, width), F32), rows_out((count, 1), F32)]
            + [((rows, part_len, width), BF, (1, part_len, width), part_out)] * ntens
            + [whole_out((nd * ntens, sents, width), BF)],
            scratch=[pltpu.VMEM((sents, width), F32)],
            cost=14.0,
        )

        def send_back(parts):
            return [parts[0]] + [across(parts[j], "tensor", j) for j in range(1, ntens)]

        def collected(parts, after=()):
            (out,) = call(
                collect_kernel,
                (part_len // deal_block,),
                [whole(t_arr)] + [(a, (rows, deal_block, width), lambda i, *_: (0, i, 0)) for a in parts],
                [((part_len * row_count, width), BF, (blk, width), lambda i, *_: (i, 0))],
                scalars=1,
                after=after,
                cost=2.0,
                limit=16,
            )
            return out.reshape(part_len, row_count, width)

        every = lax.all_to_all(pooled, ("dp", "tensor"), 0, 0, tiled=True).reshape(nd * ntens * sents, width)

        df, dz2, de, sums2, dbup = call(
            feed_back_kernel,
            (steps,),
            [whole(every), whole(own_ids), whole(mate), whole(goal), whole(inv_count), code_spec]
            + [rows_of(xh2), rows_of(rstd2), whole(small)]
            + [whole(w) for w in ws3]
            + [rows_of(g)],
            [
                rows_out((count, width), BF),
                rows_out((count, width), F32),
                rows_out((4, count, hidden), BF),
                whole_out((8, width), F32),
                whole_out((4, 8, hidden), F32),
            ],
            scratch=[pltpu.VMEM((3, sents, width), BF)],
            cost=14.0,
        )

        hidden_parts = send_back([y0, y1, y2, y3])

        def grad_part(a, b, odd, kernel, got, outs, after):
            return call(
                kernel,
                (2,),
                [whole(here), whole(a), (b, (1,) + b.shape[1:], lambda j, *_: (2 * j + odd, 0, 0))]
                + [(v, (1,) + v.shape[1:], lambda j, *_: (j, 0, 0, 0, 0)) for v in got],
                outs,
                scalars=1,
                after=after,
                cost=5.0,
            )

        shape = (2, 2, depth, rbk, hidden)
        half = (2,) + shape[2:]
        both_out = [(shape, BF, (1,) + shape[1:], lambda j, *_: (j, 0, 0, 0, 0))]
        (send3,) = grad_part(df, h, 1, grad_send_kernel, [], both_out, [])
        (sendu,) = grad_part(u, de, 1, grad_send_kernel, [], both_out, [send3])
        got = uncut(swap(cut(send3)))
        stay3, fly3 = grad_part(
            df, h, 0, functools.partial(grad_keep_kernel, True), [got],
            [(half, BF, (1,) + half[1:], lambda j, *_: (j, 0, 0, 0))] * 2, [sendu],
        )
        if not fused:
            both = cut(jnp.stack([stay3, fly3], axis=1))
            stay3, fly3 = both[:, 0], both[:, 1]
        got = uncut(swap(cut(sendu)))
        stayu, flyu = grad_part(
            u, de, 0, functools.partial(grad_keep_kernel, False), [got], [whole_out(half, BF)] * 2, [fly3]
        )
        stayu, flyu = cut(stayu), cut(flyu)
        got3x = across(fly3, "dp", 1)
        gotuy = across(flyu, "tensor", 2)

        dz1, da, do, sums1 = call(
            norm_back_kernel,
            (steps,),
            [rows_of(de), rows_of(dz2), rows_of(xh1), rows_of(rstd1), whole(small)] + ups + outs_w,
            [
                rows_out((count, width), F32),
                rows_out((count, width), BF),
                rows_out((4, count, local), BF),
                whole_out((8, width), F32),
            ],
            after=[flyu],
            cost=15.0,
        )

        do_rows = do.reshape(4, rows, seq, local)
        da_rows = da.reshape(rows, seq, width)
        per = lambda r, *_: (r, 0, 0)
        grad_cols = 4 * local

        def attend_back(j, dx, after):
            qkv, p, o = kept[j]
            if j > 0:
                dx_out = [((rows, seq, width), F32, (1, seq, width), per)]
            else:
                dx_out = [((rows, part_len, width), BF, (1, part_len, width), per)] * ntens
            piece, sums, *dx = call(
                attn_bwd_kernel,
                (rows,),
                [
                    whole(here),
                    (qkv, (1, seq, 3 * local), per),
                    (p, (1, heads, seq, seq), lambda r, *_: (r, 0, 0, 0)),
                    (o, (1, seq, local), per),
                    (do_rows[j], (1, seq, local), per),
                    (x, (1, seq, width), per),
                    (da_rows, (1, seq, width), per),
                    whole(w1[j]),
                    (dx, (1, seq, width), per),
                ],
                [whole_out((2, depth, rbk, grad_cols), BF), whole_out((8, 3 * local), F32)] + dx_out,
                scratch=[pltpu.VMEM((width, grad_cols), F32)],
                scalars=1,
                after=after,
                cost=14.0,
            )
            return cut(piece), sums, (dx[0] if j > 0 else dx)

        sums_of = {}
        back3, sums_of[3], dx = attend_back(3, dz1.reshape(rows, seq, width), [])
        got_far = swap(back3)
        got3x, gotuy = gate([got3x, gotuy], [back3])
        turn3 = total(stay3[1], got3x[1]).astype(BF)
        turnu = total(stayu[1], gotuy[1]).astype(BF)
        got3y = across(turn3, "tensor", 2)
        gotux = across(turnu, "dp", 1)
        back2, sums_of[2], dx = attend_back(2, dx, [turn3, turnu])
        got3y, gotux = gate([got3y, gotux], [back2])
        last3 = total(stay3[0], got3x[0], got3y).astype(BF)
        lastu = total(stayu[0], gotuy[0], gotux).astype(BF)
        end = along(jnp.concatenate([last3, lastu], axis=2))
        hidden_out = collected(hidden_parts, [back2])
        fly1 = total(back2[1], got_far[1]).astype(BF)
        got_fly1 = across(fly1, "dp", 1)
        back1, sums_of[1], dx = attend_back(1, dx, [last3, lastu, fly1, hidden_out])
        got_near = swap(back1)
        (got_fly1,) = gate([got_fly1], [back1])
        turn1 = total(back2[0], got_far[0], got_fly1).astype(BF)
        got_turn1 = across(turn1, "tensor", 2)
        back0, sums_of[0], dx_parts = attend_back(0, dx, [turn1])
        got1 = across(total(back0[1], got_near[1]).astype(BF), "dp", 1)
        grad_tokens = collected(send_back(dx_parts))
        (end,) = gate([end], [back0])
        got1, got_turn1 = gate([got1, got_turn1], [grad_tokens])
        last1 = total(back0[0], got_near[0], got1, got_turn1).astype(BF)

        def to_axes(rows_by_d):
            order = jnp.arange(ntens) ^ t
            return jnp.take(rows_by_d, order, axis=0).transpose(1, 0, 2)

        sums = jnp.stack([sums_of[j][0] for j in range(4)])
        qv_sum = jnp.stack([sums[:, :local], sums[:, 2 * local :]], axis=1)
        qv_sum = qv_sum.reshape(4, 2 * heads, nd, hb).transpose(0, 2, 1, 3).reshape(4, nd, 2 * heads * hb)
        up_sum = dbup[:, 0].reshape(4, hidden // hd, nd, hb).transpose(0, 2, 1, 3).reshape(4, nd, -1)
        norms = jnp.stack([sums1[0], sums2[0], sums1[2], sums1[1], sums2[2], sums2[1]])
        norms = norms.reshape(6, nd, ntens, -1).transpose(1, 2, 0, 3).reshape(nd, ntens, -1)
        message = jnp.concatenate([to_axes(qv_sum), to_axes(up_sum), norms], axis=2)
        (message,) = gate([message.reshape(nd * ntens, 1, -1)], [end])
        message = lax.all_to_all(message, ("dp", "tensor"), 0, 0, tiled=True)
        (last1,) = gate([last1], [message])
        grad_one = settle(along(last1))
        end = settle(end)
        grad_down, grad_up = end[:, :hidden], end[:, hidden:]
        got = jnp.sum(message, axis=(0, 1))
        n1 = qv_sum.shape[2]
        n2 = n1 + up_sum.shape[2]
        grad_b_qv = got[:n1].reshape(2, heads, hb)
        grad_b_up = got[n1:n2].reshape(hidden // hd, hb)
        rest = got[n2:].reshape(6, -1)
        return (
            hidden_out,
            grad_tokens,
            grad_one[:, : 3 * local].reshape(rb, 3, local),
            grad_b_qv,
            grad_one[:, 3 * local :].T,
            grad_up,
            grad_b_up,
            grad_down.T,
            rest[:2],
            rest[2:],
        )

    return shards


def solution(mesh):
    return jax.shard_map(
        make(mesh),
        mesh=mesh,
        in_specs=(
            P("tensor", "dp", None),
            P("dp", None, "tensor"),
            P(None, "tensor", "dp"),
            P("tensor", "dp"),
            P("dp", "tensor"),
            P("tensor", "dp"),
            P("tensor", "dp"),
            P(None, "dp"),
            P(None, "dp"),
            P("dp"),
            P("dp", None),
            P(),
            P(),
        ),
        out_specs=(
            P("tensor", "dp", None),
            P("tensor", "dp", None),
            P("dp", None, "tensor"),
            P(None, "tensor", "dp"),
            P("tensor", "dp"),
            P("dp", "tensor"),
            P("tensor", "dp"),
            P("tensor", "dp"),
            P(None, ("dp", "tensor")),
            P(None, ("dp", "tensor")),
        ),
        check_vma=False,
    )
```

```python
import functools
import math

import jax
import jax.numpy as jnp
import numpy as np
from jax import lax
from jax.experimental import pallas as pl
from jax.experimental.pallas import tpu as pltpu
from jax.sharding import PartitionSpec as P

SEGS = 4
EPS_NORM = 1e-05
EPS_COS = 1e-06
LOSS_SCALE = 4096.0
NEG = -1e30
DEAD = 99

BF = jnp.bfloat16
F32 = jnp.float32
MIB = 1024 * 1024
SHARE = 0.3


def dot(a, b, ca, cb):
    return lax.dot_general(a, b, (((ca,), (cb,)), ((), ())), preferred_element_type=F32)


def nn(a, b):
    return dot(a, b, 1, 0)


def nt(a, b):
    return dot(a, b, 1, 1)


def tn(a, b):
    return dot(a, b, 0, 0)


def call(kernel, grid, ins, outs, scratch=(), cost=1.0, scalars=0, limit=16, after=()):
    def spec(shape, block, index):
        if block == "any":
            return pl.BlockSpec(memory_space=pl.ANY)
        if block is None:
            zeros = (0,) * len(shape)
            return pl.BlockSpec(shape, lambda *_: zeros)
        return pl.BlockSpec(block, index)

    in_specs = [spec(a.shape, b, m) for a, b, m in ins[scalars:]]
    out_specs = [spec(s, b, m) for s, _, b, m in outs]
    flops = int(cost * SHARE * 1.15e9)
    body, known = kernel, len(ins)
    if after:
        in_specs += [pl.BlockSpec(memory_space=pl.ANY)] * len(after)

        def body(*refs):
            return kernel(*refs[:known], *refs[known + len(after) :])

    return pl.pallas_call(
        body,
        grid_spec=pltpu.PrefetchScalarGridSpec(
            num_scalar_prefetch=scalars,
            grid=grid,
            in_specs=in_specs,
            out_specs=out_specs,
            scratch_shapes=list(scratch),
        ),
        out_shape=[jax.ShapeDtypeStruct(s, d) for s, d, _, _ in outs],
        compiler_params=pltpu.CompilerParams(
            dimension_semantics=("arbitrary",) * len(grid), vmem_limit_bytes=limit * MIB
        ),
        cost_estimate=pl.CostEstimate(flops=flops, bytes_accessed=1024, transcendentals=0),
    )(*[a for a, _, _ in ins], *after)


def gate(arrays, after):
    n = len(arrays)
    anywhere = pl.BlockSpec(memory_space=pl.ANY)
    return pl.pallas_call(
        lambda *refs: None,
        in_specs=[anywhere] * (n + len(after)),
        out_specs=[anywhere] * n,
        out_shape=[jax.ShapeDtypeStruct(a.shape, a.dtype) for a in arrays],
        input_output_aliases={i: i for i in range(n)},
        cost_estimate=pl.CostEstimate(flops=1, bytes_accessed=1, transcendentals=0),
    )(*arrays, *after)


def deal_kernel(t_ref, tok_ref, *out_refs):
    size = tok_ref.shape[0]
    parts = len(out_refs)
    rows, block = out_refs[0].shape[0], out_refs[0].shape[1]
    t = t_ref[0]
    m = lax.broadcasted_iota(jnp.int32, (size, size), 0)
    n = lax.broadcasted_iota(jnp.int32, (size, size), 1)
    part, row, place = m // (rows * block), (m // block) % rows, m % block
    source = place * (parts * rows) + jnp.bitwise_xor(part, t) * rows + row
    pick = jnp.where(source == n, 1.0, 0.0).astype(BF)
    moved = nn(pick, tok_ref[...]).astype(BF)
    for j, out in enumerate(out_refs):
        for r in range(rows):
            at = (j * rows + r) * block
            out[r] = moved[at : at + block]


def collect_kernel(t_ref, *refs):
    *in_refs, out_ref = refs
    size = out_ref.shape[0]
    parts = len(in_refs)
    rows, block = in_refs[0].shape[0], in_refs[0].shape[1]
    t = t_ref[0]
    m = lax.broadcasted_iota(jnp.int32, (size, size), 1)
    n = lax.broadcasted_iota(jnp.int32, (size, size), 0)
    part, row, place = m // (rows * block), (m // block) % rows, m % block
    target = place * (parts * rows) + jnp.bitwise_xor(part, t) * rows + row
    pick = jnp.where(target == n, 1.0, 0.0).astype(BF)
    joined = jnp.concatenate([ref[r] for ref in in_refs for r in range(rows)], axis=0)
    out_ref[...] = nn(pick, joined).astype(BF)


def stack_kernel(*refs):
    *ins, out_ref = refs
    for i, ref in enumerate(ins):
        out_ref[i] = ref[...]


def add_kernel(layout, *refs):
    ins, outs = list(refs[: sum(map(sum, layout))]), refs[sum(map(sum, layout)) :]
    for terms, out_ref in zip(layout, outs):
        at = 0
        for n in terms:
            group = [ins.pop(0) for _ in range(n)]
            value = group[0][...].astype(F32)
            for ref in group[1:]:
                value += ref[...].astype(F32)
            rows, columns = value.shape[-2:]
            out_ref[0, :, at : at + columns] = value.reshape(rows, columns).astype(BF)
            at += columns


def merge_kernel(here_ref, own_ref, other_ref, out_ref):
    depth, rows = own_ref.shape[0], own_ref.shape[1]
    lo = here_ref[0]
    for z in range(depth):
        at = lax.rem(z + depth - here_ref[1], depth)
        mine, theirs = own_ref[at], other_ref[at]
        for b in range(2):
            at = (2 * z + b) * rows
            out_ref[at : at + rows, :] = jnp.where(lo == b, mine, theirs)


def attn_fwd_kernel(parts, *refs):
    x_refs, refs = refs[:parts], refs[parts:]
    w_ref, sqv_ref, kc_ref, qc_ref, qkv_ref, p_ref, o_ref, *refs = refs
    *x_out, bias_ref, mask_ref = refs
    local = o_ref.shape[2]
    heads = p_ref.shape[1]
    hd = local // heads

    @pl.when(pl.program_id(0) == 0)
    def _():
        bias_ref[...] = tn(w_ref[:, 3 * local :][:, :8], sqv_ref[...])

    x = x_refs[0][0]
    if parts > 1:
        x = jnp.concatenate([ref[0] for ref in x_refs], axis=0)
        x_out[0][0] = x
    kc, qc = kc_ref[0], qc_ref[0]
    allowed = (kc == qc) | ((qc == DEAD) & (kc >= 0))
    mask_ref[...] = jnp.where(allowed, 0.0, NEG)

    projected = nn(x, w_ref[:, : 3 * local])
    q_all = ((projected[:, :local] + bias_ref[0:1, :local]) * 0.125).astype(BF)
    k_all = projected[:, local : 2 * local].astype(BF)
    v_all = (projected[:, 2 * local :] + bias_ref[0:1, local:]).astype(BF)
    qkv_ref[0, :, :local] = q_all
    qkv_ref[0, :, local : 2 * local] = k_all
    qkv_ref[0, :, 2 * local :] = v_all
    outs = []
    for h in range(heads):
        at = slice(h * hd, (h + 1) * hd)
        s = nt(q_all[:, at], k_all[:, at]) + mask_ref[...]
        top = jnp.max(s, axis=-1, keepdims=True)
        e = jnp.exp(s - top)
        total = jnp.sum(e, axis=-1, keepdims=True)
        p = (e * (1.0 / total)).astype(BF)
        p_ref[0, h] = p
        outs.append(nn(p, v_all[:, at]).astype(BF))
    o_ref[0] = jnp.concatenate(outs, axis=1)


def norm(z):
    centred = z - jnp.mean(z, axis=-1, keepdims=True)
    rstd = lax.rsqrt(jnp.mean(centred * centred, axis=-1, keepdims=True) + EPS_NORM)
    return centred * rstd, rstd


def norm_back(dy, xh, rstd, gain):
    dxh = dy * gain
    mean = jnp.mean(dxh, axis=-1, keepdims=True)
    proj = jnp.mean(dxh * xh, axis=-1, keepdims=True)
    return rstd * (dxh - mean - xh * proj)


def out_kernel(o0, o1, o2, o3, x_ref, sup_ref, w0, w1, w2, w3, xh_ref, rstd_ref, u_ref, small_ref, bup_ref):
    local = o0.shape[1]
    width = x_ref.shape[1]
    ws = (w0, w1, w2, w3)

    @pl.when(pl.program_id(0) == 0)
    def _():
        eye = (
            lax.broadcasted_iota(jnp.int32, (width, width), 0)
            == lax.broadcasted_iota(jnp.int32, (width, width), 1)
        ).astype(BF)
        small_ref[...] = tn(w0[:, local:][:, :8], eye)
        for j in range(4):
            bup_ref[j] = tn(ws[j][:, local:][:, :8], sup_ref[...])

    a = nt(o0[...], w0[:, :local])
    for w, o in ((w1, o1), (w2, o2), (w3, o3)):
        a += nt(o[...], w[:, :local])
    z = x_ref[...].astype(F32) + (a + small_ref[2:3])
    xh, rstd = norm(z)
    xh_ref[...] = xh
    rstd_ref[...] = rstd
    u_ref[...] = (xh * small_ref[0:1] + small_ref[3:4]).astype(BF)


def turned(a):
    rows = a.shape[1]
    eye = (
        lax.broadcasted_iota(jnp.int32, (rows, rows), 0) == lax.broadcasted_iota(jnp.int32, (rows, rows), 1)
    ).astype(BF)
    return nt(eye, a).astype(BF)


def pack_one_kernel(w_ref, extra_ref, piece_ref):
    piece_ref[...] = jnp.concatenate([w_ref[...], extra_ref[...]], axis=1)


def pack_two_kernel(up_ref, out_ref, extra_ref, piece_ref):
    hidden = up_ref.shape[1]
    piece_ref[0, :, :hidden] = up_ref[...]
    piece_ref[0, :, hidden:] = jnp.concatenate([turned(out_ref[...]), extra_ref[...]], axis=1)


def pack_three_kernel(a_ref, piece_ref):
    piece_ref[0] = turned(a_ref[...])


def gelu_parts(e):
    cdf = 0.5 + 0.5 * lax.erf(e * (1.0 / math.sqrt(2.0)))
    return e * cdf, cdf + e * (jnp.exp(-0.5 * e * e) * (1.0 / math.sqrt(2.0 * math.pi)))


def fetch(moves, step, sems, body):
    copies = [pltpu.make_async_copy(src, dst, sems.at[i]) for i, (src, dst) in enumerate(moves)]

    @pl.when(step == 0)
    def _():
        for copy in copies:
            copy.start()
        body(lambda i: copies[i].wait())

    @pl.when(step > 0)
    def _():
        body(lambda i: None)


def up_kernel(u_ref, bup_ref, w0, w1, w2, w3, h_ref, g_ref, w_ref, sems):
    width = w_ref.shape[2]

    def body(ready):
        u = u_ref[...]
        for j in range(4):
            ready(j)
            e = nn(u, w_ref[j]) + bup_ref[j, 6:7]
            h, g = gelu_parts(e)
            h_ref[j] = h.astype(BF)
            g_ref[j] = g.astype(BF)

    fetch([(w.at[:, :width], w_ref.at[j]) for j, w in enumerate((w0, w1, w2, w3))], pl.program_id(0), sems, body)


def split3(v):
    a = v.astype(BF)
    rest = v - a.astype(F32)
    b = rest.astype(BF)
    c = (rest - b.astype(F32)).astype(BF)
    return a, b, c


def down_kernel(
    h_ref, xh1_ref, small_ref, code_ref, inv_ref, w0, w1, w2, w3,
    xh_ref, rstd_ref, y0, y1, y2, y3, pool_ref, acc_ref, w_ref, sems,
):
    y_refs = (y0, y1, y2, y3)
    step = pl.program_id(0)

    @pl.when(step == 0)
    def _():
        acc_ref[...] = jnp.zeros_like(acc_ref)

    def body(ready):
        ready(0)
        f = nt(h_ref[0], w_ref[0])
        for j in range(1, 4):
            ready(j)
            f += nt(h_ref[j], w_ref[j])
        first = xh1_ref[...] * small_ref[0:1] + small_ref[3:4]
        xh, rstd = norm(first + (f + small_ref[4:5]))
        y2 = xh * small_ref[1:2] + small_ref[5:6]
        xh_ref[...] = xh
        rstd_ref[...] = rstd
        low = y2.astype(BF)
        size = y_refs[0].shape[1]
        here = low.shape[0] // size
        for j, ref in enumerate(y_refs):

            @pl.when(lax.rem(step, 4 // here) == j // here)
            def _():
                ref[0] = low[(j % here) * size : (j % here + 1) * size]

        member = (lax.broadcasted_iota(jnp.int32, (8, y2.shape[0]), 0) == code_ref[...]).astype(BF)
        a, b, c = split3(y2)
        acc_ref[...] += nn(member, a) + nn(member, b) + nn(member, c)

    fetch([(w, w_ref.at[j]) for j, w in enumerate((w0, w1, w2, w3))], step, sems, body)

    @pl.when(step == pl.num_programs(0) - 1)
    def _():
        low = (acc_ref[...] * inv_ref[...]).astype(BF)

        def put(i, carry):
            pool_ref[i] = low
            return carry

        lax.fori_loop(0, pool_ref.shape[0], put, 0)


def loss_grad(pooled_ref, ids_ref, mate_ref, target_ref, inv_ref):
    pooled = pooled_ref[...]
    places = lax.broadcasted_iota(jnp.int32, (8, pooled.shape[0]), 1)
    first = nn((places == ids_ref[...]).astype(BF), pooled)
    second = nn((places == mate_ref[...]).astype(BF), pooled)
    inner = jnp.sum(first * second, axis=-1, keepdims=True)
    ra = lax.rsqrt(jnp.sum(first * first, axis=-1, keepdims=True) + EPS_COS)
    rb = lax.rsqrt(jnp.sum(second * second, axis=-1, keepdims=True) + EPS_COS)
    missed = inner * ra * rb - target_ref[...]
    grad = (2.0 * LOSS_SCALE) * missed * (second * (ra * rb) - first * (inner * rb * ra * ra * ra))
    return grad * inv_ref[...]


def rowsum(v):
    return jnp.sum(v, axis=0, keepdims=True)


def feed_back_kernel(
    blocks, here_ref, pooled_ref, ids_ref, mate_ref, target_ref, inv_ref, code_ref, xh_ref, rstd_ref, small_ref,
    g_ref, h_ref, w0, w1, w2, w3, df_ref, dz_ref, de_ref, send_ref, sum_ref, bup_ref, gp_ref, all_ref, w_ref, sems,
):
    step = pl.program_id(0)

    @pl.when(step == 0)
    def _():
        grad = loss_grad(pooled_ref, ids_ref, mate_ref, target_ref, inv_ref)
        for i, part in enumerate(split3(grad)):
            gp_ref[i] = part
        sum_ref[...] = jnp.zeros_like(sum_ref)
        bup_ref[...] = jnp.zeros_like(bup_ref)

    def body(ready):
        size = xh_ref.shape[0]
        member = (lax.broadcasted_iota(jnp.int32, (8, size), 0) == code_ref[...]).astype(BF)
        dy = tn(member, gp_ref[0]) + tn(member, gp_ref[1]) + tn(member, gp_ref[2])
        xh = xh_ref[...]
        dz = norm_back(dy, xh, rstd_ref[...], small_ref[1:2])
        sum_ref[0:1] += rowsum(dy * xh)
        sum_ref[1:2] += rowsum(dy)
        sum_ref[2:3] += rowsum(dz)
        df = dz.astype(BF)
        df_ref[...] = df
        dz_ref[...] = dz
        all_ref[pl.ds(pl.multiple_of(step * size, size), size), :] = df
        for j in range(4):
            ready(j)
            de = (nn(df, w_ref[j]) * g_ref[j].astype(F32)).astype(BF)
            de_ref[j] = de
            bup_ref[j, 0:1] += rowsum(de.astype(F32))

    @pl.when(step < blocks)
    def _():
        fetch([(w, w_ref.at[j]) for j, w in enumerate((w0, w1, w2, w3))], step, sems, body)

    @pl.when(step >= blocks)
    def _():
        pieces(tn(all_ref[...], h_ref[0]), here_ref, send_ref.at[0], slice(0, h_ref.shape[2]))


def norm_back_kernel(
    de_ref, dz2_ref, xh_ref, rstd_ref, small_ref, w0, w1, w2, w3,
    dz_ref, da_ref, do_ref, sum_ref, w_ref, wo_ref, sems,
):
    step = pl.program_id(0)
    hidden = w_ref.shape[2]
    ups = (w0, w1, w2, w3)
    moves = [(w.at[:, :hidden], w_ref.at[j]) for j, w in enumerate(ups)]
    moves += [(w.at[:, hidden:], wo_ref.at[j]) for j, w in enumerate(ups)]

    @pl.when(step == 0)
    def _():
        sum_ref[...] = jnp.zeros_like(sum_ref)

    def body(ready):
        dy = dz2_ref[...]
        for j in range(4):
            ready(j)
            dy = dy + nt(de_ref[j], w_ref[j])
        xh = xh_ref[...]
        dz = norm_back(dy, xh, rstd_ref[...], small_ref[0:1])
        sum_ref[0:1] += rowsum(dy * xh)
        sum_ref[1:2] += rowsum(dy)
        sum_ref[2:3] += rowsum(dz)
        da = dz.astype(BF)
        dz_ref[...] = dz
        da_ref[...] = da
        for j in range(4):
            ready(4 + j)
            do_ref[j] = nn(da, wo_ref[j, :, : do_ref.shape[2]]).astype(BF)

    fetch(moves, step, sems, body)


def pieces(grad, here_ref, ref, at):
    depth, rows = ref.shape[1], ref.shape[2]
    lo = here_ref[0]
    low = grad.astype(BF)
    for z in range(depth):
        first, second = (low[(2 * z + b) * rows : (2 * z + b + 1) * rows] for b in range(2))
        ref[0, z, :, at] = jnp.where(lo == 0, first, second)
        ref[1, z, :, at] = jnp.where(lo == 0, second, first)


def grad_send_kernel(here_ref, *refs):
    *ins, send_ref = refs
    at = 0
    for grad in (tn(a[...], b[0]) for a, b in zip(ins[::2], ins[1::2])):
        pieces(grad, here_ref, send_ref.at[0], slice(at, at + grad.shape[1]))
        at += grad.shape[1]


def grad_keep_kernel(by_row, here_ref, *refs):
    *ins, got_ref, stay_ref, fly_ref = refs
    depth, rows = got_ref.shape[2], got_ref.shape[3]
    lo = here_ref[0]
    j = pl.program_id(0)
    at = 0
    for grad in (tn(a[...], b[0]) for a, b in zip(ins[::2], ins[1::2])):
        cols = slice(at, at + grad.shape[1])
        for z in range(depth):
            first, second = (grad[(2 * z + b) * rows : (2 * z + b + 1) * rows] for b in range(2))
            mine, theirs = jnp.where(lo == 0, first, second), jnp.where(lo == 0, second, first)
            mine = (mine + got_ref[0, 0, z, :, cols].astype(F32)).astype(BF)
            theirs = (theirs + got_ref[0, 1, z, :, cols].astype(F32)).astype(BF)
            if by_row:
                stay_ref[0, z, :, cols] = mine
                fly_ref[0, z, :, cols] = theirs
            else:

                @pl.when(j == 0)
                def _():
                    stay_ref[0, z, :, cols] = mine
                    stay_ref[1, z, :, cols] = theirs

                @pl.when(j == 1)
                def _():
                    fly_ref[0, z, :, cols] = mine
                    fly_ref[1, z, :, cols] = theirs

        at += grad.shape[1]


def attn_bwd_kernel(keeps, here_ref, qkv_ref, p_ref, o_ref, do_ref, x_any, da_any, *refs):
    got_any, refs = refs[:keeps], refs[keeps:]
    piece_refs, refs = refs[: 1 + keeps], refs[1 + keeps :]
    sum_ref, dproj_ref, acc_ref, xs, das, sems = refs[: len(refs) - keeps]
    got_refs = refs[len(refs) - keeps :]
    r = pl.program_id(0)
    rows = xs.shape[0]
    local = o_ref.shape[2]
    heads = p_ref.shape[1]
    hd = local // heads

    def row_copies(i):
        pairs = ((x_any, xs), (da_any, das))
        return [pltpu.make_async_copy(src.at[i], dst.at[i], sems.at[2 * i + n]) for n, (src, dst) in enumerate(pairs)]

    others = [
        pltpu.make_async_copy(src, dst, sems.at[2 * rows + n]) for n, (src, dst) in enumerate(zip(got_any, got_refs))
    ]

    @pl.when(r == 0)
    def _():
        for i in range(rows):
            for copy in row_copies(i):
                copy.start()
        for copy in others:
            copy.start()

    q_all, k_all, v_all = (qkv_ref[0, :, i * local : (i + 1) * local] for i in range(3))
    o_all, do_all = o_ref[0], do_ref[0]
    prod = o_all.astype(F32) * do_all.astype(F32)
    dq, dk, dv = [], [], []
    for h in range(heads):
        at = slice(h * hd, (h + 1) * hd)
        p = p_ref[0, h]
        do = do_all[:, at]
        dv.append(tn(do, p))
        dp = nt(do, v_all[:, at])
        mid = jnp.sum(prod[:, at], axis=-1, keepdims=True)
        ds = (p.astype(F32) * (dp - mid)).astype(BF)
        dq.append(nn(ds, k_all[:, at]))
        dk.append(tn(q_all[:, at], ds))
    dq = (jnp.concatenate(dq, axis=1).astype(BF).astype(F32) * 0.125).astype(BF)
    dkv = jnp.transpose(jnp.concatenate(dk + dv, axis=0)).astype(BF)
    dproj = jnp.concatenate([dq, dkv], axis=1)
    sums = jnp.broadcast_to(rowsum(dproj.astype(F32)), sum_ref.shape)

    for copy in row_copies(r):
        copy.wait()

    @pl.when(r == 0)
    def _():
        acc_ref[...] = jnp.zeros_like(acc_ref)
        sum_ref[...] = jnp.zeros_like(sum_ref)

    sum_ref[...] += sums
    acc_ref[:, : 3 * local] += tn(xs[r], dproj)
    acc_ref[:, 3 * local :] += tn(das[r], o_all)
    dproj_ref[0] = dproj

    @pl.when(r == rows - 1)
    def _():
        if not keeps:
            pieces(acc_ref[...], here_ref, piece_refs[0], slice(0, acc_ref.shape[1]))
        else:
            others[0].wait()
            (got_ref,), (stay_ref, fly_ref) = got_refs, piece_refs
            depth, size = stay_ref.shape[0], stay_ref.shape[1]
            lo = here_ref[0]
            for z in range(depth):
                first, second = (acc_ref[(2 * z + b) * size : (2 * z + b + 1) * size] for b in range(2))
                mine, theirs = jnp.where(lo == 0, first, second), jnp.where(lo == 0, second, first)
                stay_ref[z] = (mine + got_ref[0, z].astype(F32)).astype(BF)
                fly_ref[z] = (theirs + got_ref[1, z].astype(F32)).astype(BF)


def small_kernel(norm1_ref, norm2_ref, up_ref, s1, s2, s3, keep_ref, send_ref):
    local = s1.shape[1] // 3
    parts = {1: s1, 2: s2, 3: s3}
    for ref, pair in ((keep_ref, (0, 2)), (send_ref, (1, 3))):
        ref[...] = jnp.zeros_like(ref)
        for i, (src, row) in enumerate(
            ((norm1_ref, 0), (norm2_ref, 0), (norm1_ref, 2), (norm1_ref, 1), (norm2_ref, 2), (norm2_ref, 1))
        ):
            ref[i : i + 1] = src[row : row + 1]
        for n, j in enumerate(pair):
            ref[8 + 8 * n : 9 + 8 * n] = up_ref[j, 0:1]
            if j in parts:
                ref[9 + 8 * n : 10 + 8 * n, :local] = parts[j][0:1, :local]
                ref[9 + 8 * n : 10 + 8 * n, local : 2 * local] = parts[j][0:1, 2 * local :]


def input_back_kernel(p0, p1, p2, p3, dz_ref, w0, w1, w2, w3, y0, y1, y2, y3, w_ref, sems):
    step = pl.program_id(0)
    y_refs = (y0, y1, y2, y3)

    def body(ready):
        dx = dz_ref[...]
        for j, p in enumerate((p0, p1, p2, p3)):
            ready(j)
            dx = dx + nt(p[...], w_ref[j, :, : p.shape[1]])
        low = dx.astype(BF)
        size = y_refs[0].shape[1]
        here = low.shape[0] // size
        for j, ref in enumerate(y_refs):

            @pl.when(lax.rem(step, 4 // here) == j // here)
            def _():
                ref[0] = low[(j % here) * size : (j % here + 1) * size]

    fetch([(w, w_ref.at[j]) for j, w in enumerate((w0, w1, w2, w3))], step, sems, body)


def make(mesh):
    nd, ntens = mesh.shape["dp"], mesh.shape["tensor"]
    nh = nd // 2
    groups = [[2 * z + b for z in range(nh)] for b in range(2)]

    def across(array, axis, bit):
        size = nd if axis == "dp" else ntens
        return lax.ppermute(array, axis, [(i, i ^ bit) for i in range(size)])

    def along(array):
        return lax.all_to_all(array, "dp", 0, 0, tiled=True, axis_index_groups=groups)

    def turn(array, k):
        return lax.ppermute(array, "dp", [(2 * ((z + k) % nh) + b, 2 * z + b) for z in range(nh) for b in range(2)])

    def swap(array):
        return across(array, "tensor", 1)

    def summed(*outs):
        layout, ins, shapes = [], [], []
        for ranges in outs:
            layout.append([len(terms) for terms in ranges])
            columns = 0
            for terms in ranges:
                for array, lead in terms:
                    block = (1,) * (len(lead) + 1) + array.shape[-2:]
                    ins.append((array, block, lambda z, lead=lead: (*lead, z, 0, 0)))
                columns += array.shape[-1]
            shape = (nh, array.shape[-2], columns)
            shapes.append((shape, BF, (1,) + shape[1:], lambda z: (z, 0, 0)))
        return call(functools.partial(add_kernel, layout), (nh,), ins, shapes, limit=63, cost=60.0)

    def turn(array, k):
        return lax.ppermute(array, "dp", [(2 * ((z + k) % nh) + b, 2 * z + b) for z in range(nh) for b in range(2)])

    def swap(array):
        return across(array, "tensor", 1)

    def total(*arrays):
        out = arrays[0].astype(F32)
        for a in arrays[1:]:
            out = out + a.astype(F32)
        return out

    def settle(array):
        return jnp.sum(array.astype(F32), axis=0)

    def shards(
        tokens, w_qkv, b_qv, w_out, w_up, b_up, w_down, ln_gains, shifts, lengths, segments, pair_ids, targets
    ):
        part_len, row_count, width = tokens.shape
        rb = w_up.shape[0]
        hidden = w_up.shape[1]
        local = w_qkv.shape[2]
        hb = b_up.shape[1]
        hd = hb * nd
        heads = local // hd
        seq = segments.shape[1]
        rows = row_count // ntens
        count = rows * seq
        sents = rows * SEGS
        blk = 256
        steps = count // blk
        t = lax.axis_index("tensor")
        d = lax.axis_index("dp")
        fused = rb % 16 == 0
        depth, rbk = (nh, rb) if fused else (1, width // 2)
        lo_bit = (d % 2 if fused else d * 0).astype(jnp.int32)
        turned_by = (d // 2 if nh <= 4 else d * 0).astype(jnp.int32)
        here, here_first = jnp.stack([lo_bit, lo_bit * 0]), jnp.stack([lo_bit, turned_by])
        t_arr = t.astype(jnp.int32).reshape(1)

        def merged(own, other, after=(), place=here):
            if not fused:
                first = jnp.where(d % 2 == 0, own, other)
                second = jnp.where(d % 2 == 0, other, own)
                return jnp.stack([first, second], axis=1).reshape(width, own.shape[2])
            columns = own.shape[2]
            return call(
                merge_kernel,
                (1,),
                [(place, None, None), (own, None, None), (other, None, None)],
                [((width, columns), BF, None, None)],
                scalars=1,
                after=after,
                cost=1.0,
                limit=63,
            )[0]

        def pack(kernel, arrays, columns, after):
            return call(
                kernel,
                (nh,),
                [(a, None, None) for a in arrays],
                [((nh, rb, columns), BF, (1, rb, columns), lambda i: (i, 0, 0))],
                after=after,
            )[0]

        def cut(array):
            if fused:
                return array
            lead = array.shape[:-4]
            full = array.reshape(*lead, nh, 2, rb, array.shape[-1])
            first, second = full[..., 0, :, :], full[..., 1, :, :]
            return jnp.stack(
                [jnp.where(d % 2 == 0, first, second), jnp.where(d % 2 == 0, second, first)], axis=len(lead)
            )

        def uncut(array):
            if fused:
                return array
            mine, theirs = array[..., 0, :, :, :], array[..., 1, :, :, :]
            first, second = jnp.where(d % 2 == 0, mine, theirs), jnp.where(d % 2 == 0, theirs, mine)
            return jnp.stack([first, second], axis=-3).reshape(*array.shape[:-4], 2, 1, width // 2, array.shape[-1])

        deal_block = blk // row_count
        dealt = call(
            deal_kernel,
            (part_len // deal_block,),
            [(t_arr, None, None), (tokens.reshape(part_len * row_count, width), (blk, width), lambda i, *_: (i, 0))],
            [((rows, part_len, width), BF, (rows, deal_block, width), lambda i, *_: (0, i, 0))] * ntens,
            scalars=1,
            cost=2.0,
        )
        x_parts = [dealt[0]] + [across(dealt[j], "tensor", j) for j in range(1, ntens)]

        qv_col = jnp.pad(b_qv.reshape(-1, 1), ((0, rb - b_qv.size), (0, 63)))
        wide = 3 * local + 64
        (first_piece,) = call(
            pack_one_kernel,
            (1,),
            [(w_qkv.reshape(rb, 3 * local), None, None), (qv_col, None, None)],
            [((rb, wide), BF, None, None)],
        )
        if nh <= 4:
            pieces1 = [first_piece] + [turn(first_piece, k) for k in range(1, nh)]
            own1 = call(
                stack_kernel,
                (1,),
                [(p, None, None) for p in pieces1],
                [((nh, rb, wide), BF, None, None)],
                after=[dealt[1]],
            )[0]
        else:
            own1 = along(jnp.broadcast_to(first_piece[None], (nh, rb, wide)))
        lo1 = across(own1, "dp", 1)
        w1 = {0: merged(own1, lo1, place=here_first)}
        w1[1] = swap(w1[0])
        w1[2] = across(w1[0], "tensor", 2)
        extra = jnp.concatenate([ln_gains.T, shifts.T, b_up.reshape(-1, 1), jnp.zeros((rb, 57), BF)], axis=1)
        second_piece = pack(pack_two_kernel, [w_up, w_out, extra], hidden + 256, [dealt[1]])
        (second_piece,) = gate([second_piece], [own1])
        own2 = along(second_piece)
        third_piece = pack(pack_three_kernel, [w_down], hidden, [dealt[1]])

        mine = lax.dynamic_slice_in_dim(segments, t * rows, rows, 0).reshape(rows, ntens, part_len)
        own_len = lax.dynamic_slice_in_dim(lengths, t * rows, rows, 0)
        seg = jnp.stack([lax.dynamic_index_in_dim(mine, t ^ j, 1, False) for j in range(ntens)], axis=1)
        place = jnp.stack([(t ^ j) * part_len + jnp.arange(part_len) for j in range(ntens)])
        live = (place[None] < own_len[:, None, None]).reshape(rows, seq)
        seg = seg.reshape(rows, seq)
        key_code = jnp.where(live, seg, -1)
        query_code = jnp.where(live, seg, DEAD)
        sent_code = jnp.where(live, seg + SEGS * jnp.arange(rows)[:, None], -1).reshape(1, count)
        member = (key_code[:, None, :] == jnp.arange(SEGS)[None, :, None]).astype(F32)
        inv_count = (1.0 / jnp.sum(member, axis=2)).reshape(sents, 1)
        own_ids = (d * row_count + t * rows) * SEGS + jnp.arange(sents, dtype=jnp.int32)
        is_mine = pair_ids[None, :] == own_ids[:, None]
        mates = pair_ids.reshape(-1, 2)[:, ::-1].reshape(-1)
        mate = jnp.sum(jnp.where(is_mine, mates[None, :], 0), axis=1, keepdims=True)
        goal = jnp.sum(jnp.where(is_mine, jnp.repeat(targets, 2)[None, :], 0.0), axis=1, keepdims=True)
        own_ids = own_ids[:, None]

        k = np.arange(width)
        dd, within = k // rb, k % rb
        up_at = (within // hb) * hd + dd * hb + within % hb
        sup = np.zeros((width, width), np.float32)
        sup[k, up_at] = 1.0
        qv = within < 2 * heads * hb
        qv_at = (within // (heads * hb)) * local + ((within // hb) % heads) * hd + dd * hb + within % hb
        sqv = np.zeros((width, 2 * local), np.float32)
        sqv[k[qv], qv_at[qv]] = 1.0
        sup, sqv = jnp.asarray(sup, BF), jnp.asarray(sqv, BF)

        def whole(array):
            return (array, None, None)

        def whole_out(shape, dtype):
            return (shape, dtype, None, None)

        by_row = lambda r, *_: (r, 0, 0)

        def attend(xs, w, before):
            outs = [
                ((rows, seq, 3 * local), BF, (1, seq, 3 * local), by_row),
                ((rows, heads, seq, seq), BF, (1, heads, seq, seq), lambda r, *_: (r, 0, 0, 0)),
                ((rows, seq, local), BF, (1, seq, local), by_row),
            ]
            if len(xs) > 1:
                outs.append(((rows, seq, width), BF, (1, seq, width), by_row))
            return call(
                functools.partial(attn_fwd_kernel, len(xs)),
                (rows,),
                [(a, (1,) + a.shape[1:], by_row) for a in xs]
                + [
                    whole(w),
                    whole(sqv),
                    (key_code.reshape(rows, 1, seq), (1, 1, seq), by_row),
                    (query_code.reshape(rows, seq, 1), (1, seq, 1), by_row),
                ],
                outs,
                scratch=[pltpu.VMEM((8, 2 * local), F32), pltpu.VMEM((seq, seq), F32)],
                after=before,
                limit=63,
                cost=9.0,
            )

        kept = {}
        *kept[0], x = attend(x_parts, w1[0], [second_piece])
        (own2,) = gate([own2], [kept[0][2]])
        lo2, far2 = across(own2, "dp", 1), across(own2, "tensor", 2)
        (third_piece,) = gate([third_piece], [own2])
        own3 = along(third_piece)
        kept[1] = attend([x], w1[1], [own2])
        (w1[2],) = gate([w1[2]], [kept[1][2]])
        w1[3] = swap(w1[2])
        kept[2] = attend([x], w1[2], [])
        lo2, far2 = gate([lo2, far2], [kept[2][2]])
        far_lo2 = across(far2, "dp", 1)
        w2 = {0: merged(own2, lo2)}
        w2[1] = swap(w2[0])
        (own3,) = gate([own3], [w2[0]])
        far3, lo3 = across(own3, "tensor", 2), across(own3, "dp", 1)
        kept[3] = attend([x], w1[3], [own3])
        far3, far_lo2 = gate([far3, far_lo2], [kept[3][2]])
        far_lo3 = across(far3, "dp", 1)
        w2[2] = merged(far2, far_lo2)
        w2[3] = swap(w2[2])
        ws2 = [w2[j] for j in range(4)]
        o_parts = [kept[j][2].reshape(count, local) for j in range(4)]
        x_flat = x.reshape(count, width)

        def rows_of(array, *lead):
            if array.ndim == 3:
                return (array, (array.shape[0], blk, array.shape[2]), lambda i, *_: (0, i, 0))
            return (array, (blk, array.shape[1]), lambda i, *_: (i, 0))

        def rows_out(shape, dtype):
            if len(shape) == 3:
                return (shape, dtype, (shape[0], blk, shape[2]), lambda i, *_: (0, i, 0))
            return (shape, dtype, (blk, shape[1]), lambda i, *_: (i, 0))

        ups = [(w, "any", None) for w in ws2]
        all_w = pltpu.VMEM((4, width, hidden), BF)
        sems = lambda n: pltpu.SemaphoreType.DMA((n,))
        outs_w = [(w, (width, 256), lambda i, *_: (0, hidden // 256)) for w in ws2]
        xh1, rstd1, u, small, bup_rows = call(
            out_kernel,
            (steps,),
            [rows_of(o) for o in o_parts] + [rows_of(x_flat), whole(sup)] + outs_w,
            [
                rows_out((count, width), F32),
                rows_out((count, 1), F32),
                rows_out((count, width), BF),
                whole_out((8, width), F32),
                whole_out((4, 8, hidden), F32),
            ],
            limit=63,
            cost=8.0,
        )
        (lo3,) = gate([lo3], [u])
        w3 = {0: merged(own3, lo3)}
        w3[1] = swap(w3[0])
        h, g = call(
            up_kernel,
            (steps,),
            [rows_of(u), whole(bup_rows)] + ups,
            [rows_out((4, count, hidden), BF), rows_out((4, count, hidden), BF)],
            after=[w3[0]],
            scratch=[all_w, sems(4)],
            limit=63,
            cost=20.0,
        )
        (far_lo3,) = gate([far_lo3], [h])
        w3[2] = merged(far3, far_lo3)
        w3[3] = swap(w3[2])
        downs = [(w3[j], "any", None) for j in range(4)]
        code_spec = (sent_code, (1, blk), lambda i, *_: (0, i))
        span = blk // part_len
        part_out = lambda i, *_: (i * span // ntens, 0, 0)
        xh2, rstd2, y0, y1, y2, y3, pooled = call(
            down_kernel,
            (steps,),
            [rows_of(h), rows_of(xh1), whole(small), code_spec, whole(inv_count)] + downs,
            [rows_out((count, width), F32), rows_out((count, 1), F32)]
            + [((rows, part_len, width), BF, (1, part_len, width), part_out)] * ntens
            + [whole_out((nd * ntens, sents, width), BF)],
            scratch=[pltpu.VMEM((sents, width), F32), all_w, sems(4)],
            limit=63,
            cost=14.0,
        )

        def send_back(parts):
            return [parts[0]] + [across(parts[j], "tensor", j) for j in range(1, ntens)]

        def collected(parts, after=()):
            (out,) = call(
                collect_kernel,
                (part_len // deal_block,),
                [whole(t_arr)] + [(a, (rows, deal_block, width), lambda i, *_: (0, i, 0)) for a in parts],
                [((part_len * row_count, width), BF, (blk, width), lambda i, *_: (i, 0))],
                scalars=1,
                after=after,
                cost=30.0,
            )
            return out.reshape(part_len, row_count, width)

        every = lax.all_to_all(pooled, ("dp", "tensor"), 0, 0, tiled=True).reshape(nd * ntens * sents, width)

        shape = (2, 2, depth, rbk, hidden)
        half = (2,) + shape[2:]

        def blocked(array):
            at = lambda i, *_: jnp.minimum(i, steps - 1)
            if len(array.shape) == 3:
                return (array.shape[0], blk, array.shape[2]), lambda i, *_: (0, at(i), 0)
            return (blk, array.shape[1]), lambda i, *_: (at(i), 0)

        def blocked_out(shape, dtype):
            return (shape, dtype, *blocked(jax.ShapeDtypeStruct(shape, dtype)))

        late = lambda i: jnp.maximum(i - steps, 0)
        df, dz2, de, send3, sums2, dbup = call(
            functools.partial(feed_back_kernel, steps),
            (steps + 2,),
            [whole(here), whole(every), whole(own_ids), whole(mate), whole(goal), whole(inv_count)]
            + [(sent_code, (1, blk), lambda i, *_: (0, jnp.minimum(i, steps - 1)))]
            + [(a, *blocked(a)) for a in (xh2, rstd2)]
            + [whole(small), (g, *blocked(g))]
            + [(h, (1, count, hidden), lambda i, *_: (2 * late(i) + 1, 0, 0))]
            + downs,
            [
                blocked_out((count, width), BF),
                blocked_out((count, width), F32),
                blocked_out((4, count, hidden), BF),
                (shape, BF, (1,) + shape[1:], lambda i, *_: (late(i), 0, 0, 0, 0)),
                whole_out((8, width), F32),
                whole_out((4, 8, hidden), F32),
            ],
            scratch=[pltpu.VMEM((3, sents, width), BF), pltpu.VMEM((count, width), BF), all_w, sems(4)],
            scalars=1,
            limit=63,
            cost=32.0,
        )

        hidden_parts = send_back([y0, y1, y2, y3])

        def grad_part(a, b, odd, kernel, got, outs, after):
            return call(
                kernel,
                (2,),
                [whole(here), whole(a), (b, (1,) + b.shape[1:], lambda j, *_: (2 * j + odd, 0, 0))]
                + [(v, (1,) + v.shape[1:], lambda j, *_: (j, 0, 0, 0, 0)) for v in got],
                outs,
                scalars=1,
                after=after,
                limit=63,
                cost=40.0,
            )

        both_out = [(shape, BF, (1,) + shape[1:], lambda j, *_: (j, 0, 0, 0, 0))]
        hidden_out = collected(hidden_parts, [send3])
        (sendu,) = grad_part(u, de, 1, grad_send_kernel, [], both_out, [send3, hidden_out])
        got = uncut(swap(cut(send3)))
        stay3, fly3 = grad_part(
            df, h, 0, functools.partial(grad_keep_kernel, True), [got],
            [(half, BF, (1,) + half[1:], lambda j, *_: (j, 0, 0, 0))] * 2, [sendu],
        )
        if not fused:
            both = cut(jnp.stack([stay3, fly3], axis=1))
            stay3, fly3 = both[:, 0], both[:, 1]
        got = uncut(swap(cut(sendu)))
        stayu, flyu = grad_part(
            u, de, 0, functools.partial(grad_keep_kernel, False), [got], [whole_out(half, BF)] * 2, [fly3]
        )
        stayu, flyu = cut(stayu), cut(flyu)
        got3x = across(fly3, "dp", 1)
        gotuy = across(flyu, "tensor", 2)

        dz1, da, do, sums1 = call(
            norm_back_kernel,
            (steps,),
            [rows_of(de), rows_of(dz2), rows_of(xh1), rows_of(rstd1), whole(small)] + ups,
            [
                rows_out((count, width), F32),
                rows_out((count, width), BF),
                rows_out((4, count, local), BF),
                whole_out((8, width), F32),
            ],
            scratch=[all_w, pltpu.VMEM((4, width, 256), BF), sems(8)],
            after=[flyu],
            limit=63,
            cost=14.0,
        )
        da_rows = da.reshape(rows, seq, width)
        grad_cols = 4 * local

        def attend_back(j, got, after):
            qkv, p, o = kept[j]
            half = (depth, rbk, grad_cols)
            kinds = [whole_out((2,) + half, BF)] if got is None else [whole_out(half, BF)] * 2
            keeps = 0 if got is None else 1
            whole_row = pltpu.VMEM((rows, seq, width), BF)
            *outs, sums, dproj = call(
                functools.partial(attn_bwd_kernel, keeps),
                (rows,),
                [
                    whole(here),
                    (qkv, (1, seq, 3 * local), by_row),
                    (p, (1, heads, seq, seq), lambda r, *_: (r, 0, 0, 0)),
                    (o, (1, seq, local), by_row),
                    (do, (1, seq, local), lambda r, *_: (j, r, 0)),
                    (x, "any", None),
                    (da_rows, "any", None),
                ]
                + ([] if got is None else [(uncut(got), "any", None)]),
                kinds
                + [whole_out((8, 3 * local), F32), ((rows, seq, 3 * local), BF, (1, seq, 3 * local), by_row)],
                scratch=[pltpu.VMEM((width, grad_cols), F32), whole_row, whole_row, sems(2 * rows + keeps)]
                + [pltpu.VMEM((2,) + half, BF)] * keeps,
                scalars=1,
                after=after,
                limit=63,
                cost=11.0,
            )
            if got is None:
                out = cut(outs[0])
            elif fused:
                out = tuple(outs)
            else:
                both = cut(jnp.stack(outs))
                out = both[0], both[1]
            sums_of[j], dprojs[j] = sums, dproj.reshape(count, 3 * local)
            return out

        sums_of, dprojs = {}, {}
        back3 = attend_back(3, None, [flyu])
        got_far = swap(back3)
        got3x, gotuy = gate([got3x, gotuy], [back3])
        turn3, turnu = summed([[(stay3, (1,)), (got3x, (1,))]], [[(stayu, (1,)), (gotuy, (1,))]])
        got3y, gotux = across(turn3, "tensor", 2), across(turnu, "dp", 1)
        stay_far, fly_far = attend_back(2, got_far, [turn3, turnu])
        got_fly = across(fly_far, "dp", 1)
        got3y, gotux = gate([got3y, gotux], [stay_far])
        (end,) = summed([[(stay3, (0,)), (got3x, (0,)), (got3y, ())], [(stayu, (0,)), (gotuy, (0,)), (gotux, ())]])
        end_sent = end
        end = along(end)
        back1 = attend_back(1, None, [end_sent])
        got_near = swap(back1)
        small_keep, small_send = call(
            small_kernel,
            (1,),
            [whole(a) for a in (sums1, sums2, dbup, sums_of[1], sums_of[2], sums_of[3])],
            [whole_out((24, width), F32)] * 2,
            after=[back1],
        )
        small_keep = small_keep + swap(small_send)
        small_got = across(jnp.concatenate([small_keep[:8], small_keep[16:]], axis=0), "tensor", 2)
        (got_fly,) = gate([got_fly], [small_keep])
        (turn1,) = summed([[(stay_far, ()), (got_fly, ())]])
        got_turn1 = across(turn1, "tensor", 2)
        stay_near, fly_near = attend_back(0, got_near, [turn1])
        got1 = across(fly_near, "dp", 1)
        span_out = lambda i, *_: (i * span // ntens, 0, 0)
        dx_parts = call(
            input_back_kernel,
            (steps,),
            [rows_of(dprojs[j]) for j in range(4)] + [rows_of(dz1)] + [(w1[j], "any", None) for j in range(4)],
            [((rows, part_len, width), BF, (1, part_len, width), span_out)] * ntens,
            scratch=[pltpu.VMEM((4, width, wide), BF), sems(4)],
            limit=63,
            after=[stay_near],
            cost=8.0,
        )
        token_parts = send_back(dx_parts)

        got1, got_turn1, end = gate([got1, got_turn1, end], [dx_parts[0]])
        (last1,) = summed([[(stay_near, ()), (got1, ()), (got_turn1, ())]])
        small_got, near_sums = gate([small_got, sums_of[0]], [last1])
        near_sums = jnp.concatenate([near_sums[:1, :local], near_sums[:1, 2 * local :]], axis=1)
        own = small_keep[:16] + small_got + jnp.pad(near_sums, ((9, 6), (0, width - 2 * local)))
        bit = 1
        while bit < nd:
            own = own + across(own, "dp", bit)
            bit *= 2
        rest = lax.dynamic_slice_in_dim(own[:6], (d * ntens + t) * (width // (nd * ntens)), width // (nd * ntens), 1)
        grad_b_up = lax.dynamic_slice_in_dim(own[8].reshape(hidden // hd, hd), d * hb, hb, 1)
        grad_b_qv = lax.dynamic_slice_in_dim(own[9, : 2 * local].reshape(2, heads, hd), d * hb, hb, 2)
        grad_one = settle(along(last1))
        grad_tokens = collected(token_parts, [last1])
        end = settle(end)
        grad_down, grad_up = end[:, :hidden], end[:, hidden:]
        return (
            hidden_out,
            grad_tokens,
            grad_one[:, : 3 * local].reshape(rb, 3, local),
            grad_b_qv,
            grad_one[:, 3 * local :].T,
            grad_up,
            grad_b_up,
            grad_down.T,
            rest[:2],
            rest[2:],
        )

    return shards


def solution(mesh):
    return jax.shard_map(
        make(mesh),
        mesh=mesh,
        in_specs=(
            P("tensor", "dp", None),
            P("dp", None, "tensor"),
            P(None, "tensor", "dp"),
            P("tensor", "dp"),
            P("dp", "tensor"),
            P("tensor", "dp"),
            P("tensor", "dp"),
            P(None, "dp"),
            P(None, "dp"),
            P("dp"),
            P("dp", None),
            P(),
            P(),
        ),
        out_specs=(
            P("tensor", "dp", None),
            P("tensor", "dp", None),
            P("dp", None, "tensor"),
            P(None, "tensor", "dp"),
            P("tensor", "dp"),
            P("dp", "tensor"),
            P("tensor", "dp"),
            P("tensor", "dp"),
            P(None, ("dp", "tensor")),
            P(None, ("dp", "tensor")),
        ),
        check_vma=False,
    )
```

```python
import functools
import math

import jax
import jax.numpy as jnp
import numpy as np
from jax import lax
from jax.experimental import pallas as pl
from jax.experimental.pallas import tpu as pltpu
from jax.sharding import PartitionSpec as P

SEGS = 4
EPS_NORM = 1e-05
EPS_COS = 1e-06
LOSS_SCALE = 4096.0
NEG = -1e30
DEAD = 99

BF = jnp.bfloat16
F32 = jnp.float32
MIB = 1024 * 1024
SHARE = 0.3


def dot(a, b, ca, cb):
    return lax.dot_general(a, b, (((ca,), (cb,)), ((), ())), preferred_element_type=F32)


def nn(a, b):
    return dot(a, b, 1, 0)


def nt(a, b):
    return dot(a, b, 1, 1)


def tn(a, b):
    return dot(a, b, 0, 0)


def call(kernel, grid, ins, outs, scratch=(), cost=1.0, scalars=0, limit=16, after=()):
    def spec(shape, block, index):
        if isinstance(block, str):
            return pl.BlockSpec(memory_space=pl.ANY)
        if block is None:
            zeros = (0,) * len(shape)
            return pl.BlockSpec(shape, lambda *_: zeros)
        return pl.BlockSpec(block, index)

    in_specs = [spec(a.shape, b, m) for a, b, m in ins[scalars:]]
    out_specs = [spec(s, b, m) for s, _, b, m in outs]
    flops = int(cost * SHARE * 1.15e9)
    body, known = kernel, len(ins)
    if after:
        in_specs += [pl.BlockSpec(memory_space=pl.ANY)] * len(after)

        def body(*refs):
            return kernel(*refs[:known], *refs[known + len(after) :])

    return pl.pallas_call(
        body,
        grid_spec=pltpu.PrefetchScalarGridSpec(
            num_scalar_prefetch=scalars,
            grid=grid,
            in_specs=in_specs,
            out_specs=out_specs,
            scratch_shapes=list(scratch),
        ),
        out_shape=[jax.ShapeDtypeStruct(s, d) for s, d, _, _ in outs],
        compiler_params=pltpu.CompilerParams(
            dimension_semantics=("arbitrary",) * len(grid), vmem_limit_bytes=limit * MIB
        ),
        cost_estimate=pl.CostEstimate(flops=flops, bytes_accessed=1024, transcendentals=0),
    )(*[a for a, _, _ in ins], *after)


def gate(arrays, after):
    n = len(arrays)
    anywhere = pl.BlockSpec(memory_space=pl.ANY)
    return pl.pallas_call(
        lambda *refs: None,
        in_specs=[anywhere] * (n + len(after)),
        out_specs=[anywhere] * n,
        out_shape=[jax.ShapeDtypeStruct(a.shape, a.dtype) for a in arrays],
        input_output_aliases={i: i for i in range(n)},
        cost_estimate=pl.CostEstimate(flops=1, bytes_accessed=1, transcendentals=0),
    )(*arrays, *after)


def deal_kernel(t_ref, tok_ref, *out_refs):
    size = tok_ref.shape[0]
    parts = len(out_refs)
    rows, block = out_refs[0].shape[0], out_refs[0].shape[1]
    t = t_ref[0]
    m = lax.broadcasted_iota(jnp.int32, (size, size), 0)
    n = lax.broadcasted_iota(jnp.int32, (size, size), 1)
    part, row, place = m // (rows * block), (m // block) % rows, m % block
    source = place * (parts * rows) + jnp.bitwise_xor(part, t) * rows + row
    pick = jnp.where(source == n, 1.0, 0.0).astype(BF)
    moved = nn(pick, tok_ref[...]).astype(BF)
    for j, out in enumerate(out_refs):
        for r in range(rows):
            at = (j * rows + r) * block
            out[r] = moved[at : at + block]


def collect_kernel(t_ref, *refs):
    *in_refs, out_ref = refs
    size = out_ref.shape[0]
    parts = len(in_refs)
    rows, block = in_refs[0].shape[0], in_refs[0].shape[1]
    t = t_ref[0]
    m = lax.broadcasted_iota(jnp.int32, (size, size), 1)
    n = lax.broadcasted_iota(jnp.int32, (size, size), 0)
    part, row, place = m // (rows * block), (m // block) % rows, m % block
    target = place * (parts * rows) + jnp.bitwise_xor(part, t) * rows + row
    pick = jnp.where(target == n, 1.0, 0.0).astype(BF)
    joined = jnp.concatenate([ref[r] for ref in in_refs for r in range(rows)], axis=0)
    out_ref[...] = nn(pick, joined).astype(BF)


def stack_kernel(*refs):
    *ins, out_ref = refs
    for i, ref in enumerate(ins):
        out_ref[i] = ref[...]


def add_kernel(layout, *refs):
    ins, outs = list(refs[: sum(map(sum, layout))]), refs[sum(map(sum, layout)) :]
    for terms, out_ref in zip(layout, outs):
        at = 0
        for n in terms:
            value = 0.0
            for ref in [ins.pop(0) for _ in range(n)]:
                value = value + ref[...].astype(F32).reshape(out_ref.shape[:2] + ref.shape[-1:])
            columns = value.shape[-1]
            out_ref[:, :, at : at + columns] = value.astype(BF)
            at += columns


def merge_kernel(here_ref, own_ref, other_ref, out_ref):
    depth, rows = own_ref.shape[0], own_ref.shape[1]
    lo = here_ref[0]
    for z in range(depth):
        at = lax.rem(z + depth - here_ref[1], depth)
        mine, theirs = own_ref[at], other_ref[at]
        for b in range(2):
            at = (2 * z + b) * rows
            out_ref[at : at + rows, :] = jnp.where(lo == b, mine, theirs)


def weight_copies(pairs, here_ref, columns, dest, sems, first=0):
    groups = []
    n = first
    for j, (own, other) in enumerate(pairs):
        depth, rows = own.shape[0], own.shape[1]
        size = columns.stop - columns.start
        group = []
        for z in range(depth):
            src = lax.rem(z + depth - here_ref[1], depth)
            for ref, b in ((own, here_ref[0]), (other, 1 - here_ref[0])):
                to = dest.at[pl.ds(pl.multiple_of((2 * z + b) * rows, rows), rows), j * size : (j + 1) * size]
                group.append(pltpu.make_async_copy(ref.at[src, :, columns], to, sems.at[n]))
                n += 1
        groups.append(group)
    return groups


def paired(refs):
    return list(zip(refs[::2], refs[1::2]))


def attn_fwd_kernel(parts, *refs):
    x_refs, refs = refs[:parts], refs[parts:]
    w_ref, sqv_ref, kc_ref, qc_ref, qkv_ref, p_ref, o_ref, *refs = refs
    *x_out, bias_ref, mask_ref = refs
    local = qkv_ref.shape[2] // 3
    heads = p_ref.shape[1]
    hd = local // heads

    @pl.when(pl.program_id(0) == 0)
    def _():
        bias_ref[...] = tn(w_ref[:, 3 * local :][:, :8], sqv_ref[...])

    x = x_refs[0][0]
    if parts > 1:
        x = jnp.concatenate([ref[0] for ref in x_refs], axis=0)
        x_out[0][0] = x
    kc, qc = kc_ref[0], qc_ref[0]
    allowed = (kc == qc) | ((qc == DEAD) & (kc >= 0))
    mask_ref[...] = jnp.where(allowed, 0.0, NEG)

    projected = nn(x, w_ref[:, : 3 * local])
    q_all = ((projected[:, :local] + bias_ref[0:1, :local]) * 0.125).astype(BF)
    k_all = projected[:, local : 2 * local].astype(BF)
    v_all = (projected[:, 2 * local :] + bias_ref[0:1, local:]).astype(BF)
    qkv_ref[0, :, :local] = q_all
    qkv_ref[0, :, local : 2 * local] = k_all
    qkv_ref[0, :, 2 * local :] = v_all
    outs = []
    for h in range(heads):
        at = slice(h * hd, (h + 1) * hd)
        s = nt(q_all[:, at], k_all[:, at]) + mask_ref[...]
        top = jnp.max(s, axis=-1, keepdims=True)
        e = jnp.exp(s - top)
        total = jnp.sum(e, axis=-1, keepdims=True)
        p = (e * (1.0 / total)).astype(BF)
        p_ref[0, h] = p
        outs.append(nn(p, v_all[:, at]).astype(BF))
    pad = jnp.zeros((outs[0].shape[0], o_ref.shape[2] - local), BF)
    o_ref[0] = jnp.concatenate(outs + [pad], axis=1)


def norm(z):
    centred = z - jnp.mean(z, axis=-1, keepdims=True)
    rstd = lax.rsqrt(jnp.mean(centred * centred, axis=-1, keepdims=True) + EPS_NORM)
    return centred * rstd, rstd


def norm_back(dy, xh, rstd, gain):
    dxh = dy * gain
    mean = jnp.mean(dxh, axis=-1, keepdims=True)
    proj = jnp.mean(dxh * xh, axis=-1, keepdims=True)
    return rstd * (dxh - mean - xh * proj)


def turned(a):
    rows = a.shape[1]
    eye = (
        lax.broadcasted_iota(jnp.int32, (rows, rows), 0) == lax.broadcasted_iota(jnp.int32, (rows, rows), 1)
    ).astype(BF)
    return nt(eye, a).astype(BF)


def pack_one_kernel(w_ref, extra_ref, piece_ref):
    piece_ref[...] = jnp.concatenate([w_ref[...], extra_ref[...]], axis=1)


def pack_two_kernel(up_ref, out_ref, extra_ref, piece_ref):
    hidden = up_ref.shape[1]
    piece_ref[0, :, :hidden] = up_ref[...]
    piece_ref[0, :, hidden:] = jnp.concatenate([turned(out_ref[...]), extra_ref[...]], axis=1)


def pack_three_kernel(a_ref, piece_ref):
    piece_ref[0] = turned(a_ref[...])


def gelu_parts(e):
    cdf = 0.5 + 0.5 * lax.erf(e * (1.0 / math.sqrt(2.0)))
    return e * cdf, cdf + e * (jnp.exp(-0.5 * e * e) * (1.0 / math.sqrt(2.0 * math.pi)))


def fetch(groups, step, body):
    @pl.when(step == 0)
    def _():
        for group in groups:
            for copy in group:
                copy.start()

        def ready(i):
            for copy in groups[i]:
                copy.wait()

        body(ready)

    @pl.when(step > 0)
    def _():
        body(None)


def middle_kernel(here_ref, o0, o1, o2, o3, x_ref, sup_ref, *refs):
    ws, refs = paired(refs[:8]), refs[8:]
    xh_ref, rstd_ref, u_ref, h_ref, g_ref, small_ref, wo_ref, wu_ref, bup_ref, sems = refs
    width = x_ref.shape[1]
    hidden = wu_ref.shape[1] // 4
    wide = wo_ref.shape[1] // 4
    per = 2 * ws[0][0].shape[0]
    groups = weight_copies(ws, here_ref, slice(hidden, hidden + wide), wo_ref, sems)
    groups += weight_copies(ws, here_ref, slice(0, hidden), wu_ref, sems, 4 * per)

    def body(ready):
        if ready:
            for j in range(4):
                ready(j)
            eye = (
                lax.broadcasted_iota(jnp.int32, (width, width), 0)
                == lax.broadcasted_iota(jnp.int32, (width, width), 1)
            ).astype(BF)
            local = wide - 64
            small_ref[...] = tn(wo_ref[:, local:wide][:, :8], eye)
            for j in range(4):
                cols = wo_ref[:, j * wide + local : (j + 1) * wide][:, :8]
                bup_ref[:, j * hidden : (j + 1) * hidden] = tn(cols, sup_ref[...])
        o = jnp.concatenate([o0[...], o1[...], o2[...], o3[...]], axis=1)
        z = x_ref[...].astype(F32) + (nt(o, wo_ref[...]) + small_ref[2:3])
        xh, rstd = norm(z)
        xh_ref[...] = xh.astype(BF)
        rstd_ref[...] = rstd
        u = (xh * small_ref[0:1] + small_ref[3:4]).astype(BF)
        u_ref[...] = u
        for j in range(4 if ready else 1):
            at = slice(j * hidden, (j + 1) * hidden) if ready else slice(0, 4 * hidden)
            if ready:
                ready(4 + j)
            h, g = gelu_parts(nn(u, wu_ref[:, at]) + bup_ref[6:7, at])
            h_ref[:, at] = h.astype(BF)
            g_ref[:, at] = g.astype(BF)

    fetch(groups, pl.program_id(0), body)


def split3(v):
    a = v.astype(BF)
    rest = v - a.astype(F32)
    b = rest.astype(BF)
    c = (rest - b.astype(F32)).astype(BF)
    return a, b, c


def down_kernel(here_ref, h_ref, u_ref, small_ref, code_ref, inv_ref, *refs):
    ws, refs = paired(refs[:8]), refs[8:]
    xh_ref, rstd_ref, y0, y1, y2, y3, pool_ref, acc_ref, w_ref, sems = refs
    y_refs = (y0, y1, y2, y3)
    step = pl.program_id(0)
    hidden = w_ref.shape[1] // 4

    @pl.when(step == 0)
    def _():
        acc_ref[...] = jnp.zeros_like(acc_ref)

    def body(ready):
        if ready:
            ready(0)
            f = nt(h_ref[:, :hidden], w_ref[:, :hidden])
            for j in range(1, 4):
                ready(j)
                f += nt(h_ref[:, j * hidden : (j + 1) * hidden], w_ref[:, j * hidden : (j + 1) * hidden])
        else:
            f = nt(h_ref[...], w_ref[...])
        xh, rstd = norm(u_ref[...].astype(F32) + (f + small_ref[4:5]))
        y2 = xh * small_ref[1:2] + small_ref[5:6]
        xh_ref[...] = xh.astype(BF)
        rstd_ref[...] = rstd
        low = y2.astype(BF)
        size = y_refs[0].shape[1]
        here = low.shape[0] // size
        for j, ref in enumerate(y_refs):

            @pl.when(lax.rem(step, 4 // here) == j // here)
            def _():
                ref[0] = low[(j % here) * size : (j % here + 1) * size]

        member = (lax.broadcasted_iota(jnp.int32, (8, y2.shape[0]), 0) == code_ref[...]).astype(BF)
        a, b, c = split3(y2)
        acc_ref[...] += nn(member, a) + nn(member, b) + nn(member, c)

    fetch(weight_copies(ws, here_ref, slice(0, hidden), w_ref, sems), step, body)

    @pl.when(step == pl.num_programs(0) - 1)
    def _():
        low = (acc_ref[...] * inv_ref[...]).astype(BF)

        def put(i, carry):
            pool_ref[i] = low
            return carry

        lax.fori_loop(0, pool_ref.shape[0], put, 0)


def loss_grad(pooled_ref, ids_ref, mate_ref, target_ref, inv_ref):
    pooled = pooled_ref[...]
    places = lax.broadcasted_iota(jnp.int32, (8, pooled.shape[0]), 1)
    first = nn((places == ids_ref[...]).astype(BF), pooled)
    second = nn((places == mate_ref[...]).astype(BF), pooled)
    inner = jnp.sum(first * second, axis=-1, keepdims=True)
    ra = lax.rsqrt(jnp.sum(first * first, axis=-1, keepdims=True) + EPS_COS)
    rb = lax.rsqrt(jnp.sum(second * second, axis=-1, keepdims=True) + EPS_COS)
    missed = inner * ra * rb - target_ref[...]
    grad = (2.0 * LOSS_SCALE) * missed * (second * (ra * rb) - first * (inner * rb * ra * ra * ra))
    return grad * inv_ref[...]


def rowsum(v):
    return jnp.sum(v, axis=0, keepdims=True)


def feed_back_kernel(
    blocks, here_ref, pooled_ref, ids_ref, mate_ref, target_ref, inv_ref, code_ref, xh_ref, rstd_ref, small_ref,
    g_ref, h_ref, *refs,
):
    ws, refs = paired(refs[:8]), refs[8:]
    df_ref, de_ref, send_ref, sum_ref, bup_ref, gp_ref, all_ref, w_ref, sems = refs
    hidden = w_ref.shape[1] // 4
    step = pl.program_id(0)

    @pl.when(step == 0)
    def _():
        grad = loss_grad(pooled_ref, ids_ref, mate_ref, target_ref, inv_ref)
        for i, part in enumerate(split3(grad)):
            gp_ref[i] = part
        sum_ref[...] = jnp.zeros_like(sum_ref)
        bup_ref[...] = jnp.zeros_like(bup_ref)

    def body(ready):
        size = xh_ref.shape[0]
        member = (lax.broadcasted_iota(jnp.int32, (8, size), 0) == code_ref[...]).astype(BF)
        dy = tn(member, gp_ref[0]) + tn(member, gp_ref[1]) + tn(member, gp_ref[2])
        xh = xh_ref[...].astype(F32)
        dz = norm_back(dy, xh, rstd_ref[...], small_ref[1:2])
        sum_ref[0:1] += rowsum(dy * xh)
        sum_ref[1:2] += rowsum(dy)
        sum_ref[2:3] += rowsum(dz)
        df = dz.astype(BF)
        df_ref[...] = df
        all_ref[pl.ds(pl.multiple_of(step * size, size), size), :] = df
        for j in range(4 if ready else 1):
            at = slice(j * hidden, (j + 1) * hidden) if ready else slice(0, 4 * hidden)
            if ready:
                ready(j)
            de = (nn(df, w_ref[:, at]) * g_ref[:, at].astype(F32)).astype(BF)
            de_ref[:, at] = de
            bup_ref[0:1, at] += rowsum(de.astype(F32))

    @pl.when(step < blocks)
    def _():
        fetch(weight_copies(ws, here_ref, slice(0, hidden), w_ref, sems), step, body)

    @pl.when(step >= blocks)
    def _():
        pieces(tn(all_ref[...], h_ref[...]), here_ref, send_ref.at[0], slice(0, hidden))


def norm_back_kernel(here_ref, de_ref, df_ref, xh_ref, rstd_ref, small_ref, *refs):
    ws, refs = paired(refs[:8]), refs[8:]
    da_ref, do_ref, sum_ref, w_ref, wo_ref, sems = refs
    step = pl.program_id(0)
    hidden, wide = w_ref.shape[1] // 4, wo_ref.shape[1] // 4
    per = 2 * ws[0][0].shape[0]
    groups = weight_copies(ws, here_ref, slice(0, hidden), w_ref, sems)
    groups += weight_copies(ws, here_ref, slice(hidden, hidden + wide), wo_ref, sems, 4 * per)

    @pl.when(step == 0)
    def _():
        sum_ref[...] = jnp.zeros_like(sum_ref)

    def body(ready):
        dy = df_ref[...].astype(F32)
        for j in range(4 if ready else 1):
            at = slice(j * hidden, (j + 1) * hidden) if ready else slice(0, 4 * hidden)
            if ready:
                ready(j)
            dy = dy + nt(de_ref[:, at], w_ref[:, at])
        xh = xh_ref[...].astype(F32)
        dz = norm_back(dy, xh, rstd_ref[...], small_ref[0:1])
        sum_ref[0:1] += rowsum(dy * xh)
        sum_ref[1:2] += rowsum(dy)
        sum_ref[2:3] += rowsum(dz)
        da = dz.astype(BF)
        da_ref[...] = da
        if ready:
            for j in range(4):
                ready(4 + j)
        do_ref[...] = nn(da, wo_ref[...]).astype(BF)

    fetch(groups, step, body)


def pieces(grad, here_ref, ref, at):
    depth, rows = ref.shape[1], ref.shape[2]
    low = grad.astype(BF)
    for z in range(depth):
        for b in range(2):
            part = low[(2 * z + b) * rows : (2 * z + b + 1) * rows]
            ref[here_ref[0] if b == 0 else 1 - here_ref[0], z, :, at] = part


def grad_send_kernel(here_ref, *refs):
    *ins, send_ref = refs
    at = 0
    for grad in (tn(a[...], b[...]) for a, b in zip(ins[::2], ins[1::2])):
        pieces(grad, here_ref, send_ref.at[0], slice(at, at + grad.shape[1]))
        at += grad.shape[1]


def grad_keep_kernel(by_row, here_ref, *refs):
    *ins, got_ref, stay_ref, fly_ref = refs
    depth, rows = got_ref.shape[2], got_ref.shape[3]
    lo = here_ref[0]
    j = pl.program_id(0)
    at = 0
    for grad in (tn(a[...], b[...]) for a, b in zip(ins[::2], ins[1::2])):
        cols = slice(at, at + grad.shape[1])
        for z in range(depth):
            first, second = (grad[(2 * z + b) * rows : (2 * z + b + 1) * rows] for b in range(2))
            mine, theirs = jnp.where(lo == 0, first, second), jnp.where(lo == 0, second, first)
            mine = (mine + got_ref[0, 0, z, :, cols].astype(F32)).astype(BF)
            theirs = (theirs + got_ref[0, 1, z, :, cols].astype(F32)).astype(BF)
            if by_row:
                stay_ref[0, z, :, cols] = mine
                fly_ref[0, z, :, cols] = theirs
            else:

                @pl.when(j == 0)
                def _():
                    stay_ref[0, z, :, cols] = mine
                    stay_ref[1, z, :, cols] = theirs

                @pl.when(j == 1)
                def _():
                    fly_ref[0, z, :, cols] = mine
                    fly_ref[1, z, :, cols] = theirs

        at += grad.shape[1]


def attn_bwd_kernel(keeps, here_ref, qkv_ref, p_ref, o_ref, do_ref, x_any, da_any, *refs):
    got_any, refs = refs[:keeps], refs[keeps:]
    piece_refs, refs = refs[: 1 + keeps], refs[1 + keeps :]
    sum_ref, dproj_ref, acc_ref, xs, das, sems = refs[: len(refs) - keeps]
    got_refs = refs[len(refs) - keeps :]
    r = pl.program_id(0)
    rows = xs.shape[0]
    local = qkv_ref.shape[2] // 3
    heads = p_ref.shape[1]
    hd = local // heads

    def row_copies(i):
        pairs = ((x_any, xs), (da_any, das))
        return [pltpu.make_async_copy(src.at[i], dst.at[i], sems.at[2 * i + n]) for n, (src, dst) in enumerate(pairs)]

    others = [
        pltpu.make_async_copy(src, dst, sems.at[2 * rows + n]) for n, (src, dst) in enumerate(zip(got_any, got_refs))
    ]

    @pl.when(r == 0)
    def _():
        for i in range(rows):
            for copy in row_copies(i):
                copy.start()
        for copy in others:
            copy.start()

    q_all, k_all, v_all = (qkv_ref[0, :, i * local : (i + 1) * local] for i in range(3))
    o_all, do_all = o_ref[0, :, :local], do_ref[0, :, :local]
    prod = o_all.astype(F32) * do_all.astype(F32)
    dq, dk, dv = [], [], []
    for h in range(heads):
        at = slice(h * hd, (h + 1) * hd)
        p = p_ref[0, h]
        do = do_all[:, at]
        dv.append(tn(do, p))
        dp = nt(do, v_all[:, at])
        mid = jnp.sum(prod[:, at], axis=-1, keepdims=True)
        ds = (p.astype(F32) * (dp - mid)).astype(BF)
        dq.append(nn(ds, k_all[:, at]))
        dk.append(tn(q_all[:, at], ds))
    dq = (jnp.concatenate(dq, axis=1).astype(BF).astype(F32) * 0.125).astype(BF)
    dkv = jnp.transpose(jnp.concatenate(dk + dv, axis=0)).astype(BF)
    dproj = jnp.concatenate([dq, dkv], axis=1)
    sums = jnp.broadcast_to(rowsum(dproj.astype(F32)), sum_ref.shape)

    for copy in row_copies(r):
        copy.wait()

    @pl.when(r == 0)
    def _():
        acc_ref[...] = jnp.zeros_like(acc_ref)
        sum_ref[...] = jnp.zeros_like(sum_ref)

    sum_ref[...] += sums
    acc_ref[:, : 3 * local] += tn(xs[r], dproj)
    acc_ref[:, 3 * local :] += tn(das[r], o_all)
    dproj_ref[0] = jnp.concatenate([dproj, jnp.zeros((dproj.shape[0], 64), BF)], axis=1)

    @pl.when(r == rows - 1)
    def _():
        if not keeps:
            pieces(acc_ref[...], here_ref, piece_refs[0], slice(0, acc_ref.shape[1]))
        else:
            others[0].wait()
            (got_ref,), (stay_ref, fly_ref) = got_refs, piece_refs
            depth, size = stay_ref.shape[0], stay_ref.shape[1]
            lo = here_ref[0]
            for z in range(depth):
                first, second = (acc_ref[(2 * z + b) * size : (2 * z + b + 1) * size] for b in range(2))
                mine, theirs = jnp.where(lo == 0, first, second), jnp.where(lo == 0, second, first)
                stay_ref[z] = (mine + got_ref[0, z].astype(F32)).astype(BF)
                fly_ref[z] = (theirs + got_ref[1, z].astype(F32)).astype(BF)


def small_kernel(norm1_ref, norm2_ref, up_ref, s1, s2, s3, keep_ref, send_ref):
    local = s1.shape[1] // 3
    parts = {1: s1, 2: s2, 3: s3}
    for ref, pair in ((keep_ref, (0, 2)), (send_ref, (1, 3))):
        ref[...] = jnp.zeros_like(ref)
        for i, (src, row) in enumerate(
            ((norm1_ref, 0), (norm2_ref, 0), (norm1_ref, 2), (norm1_ref, 1), (norm2_ref, 2), (norm2_ref, 1))
        ):
            ref[i : i + 1] = src[row : row + 1]
        for n, j in enumerate(pair):
            ref[8 + 8 * n : 9 + 8 * n] = up_ref[0:1, j * ref.shape[1] : (j + 1) * ref.shape[1]]
            if j in parts:
                ref[9 + 8 * n : 10 + 8 * n, :local] = parts[j][0:1, :local]
                ref[9 + 8 * n : 10 + 8 * n, local : 2 * local] = parts[j][0:1, 2 * local :]


def input_back_kernel(p0, p1, p2, p3, da_ref, w0, w1, w2, w3, y0, y1, y2, y3, w_ref, sems):
    step = pl.program_id(0)
    y_refs, p_refs = (y0, y1, y2, y3), (p0, p1, p2, p3)
    wide = p0.shape[1]

    def body(ready):
        dx = da_ref[...].astype(F32)
        if ready:
            for j, p in enumerate(p_refs):
                ready(j)
                dx = dx + nt(p[...], w_ref[:, j * wide : (j + 1) * wide])
        else:
            dx = dx + nt(jnp.concatenate([p[...] for p in p_refs], axis=1), w_ref[...])
        low = dx.astype(BF)
        size = y_refs[0].shape[1]
        here = low.shape[0] // size
        for j, ref in enumerate(y_refs):

            @pl.when(lax.rem(step, 4 // here) == j // here)
            def _():
                ref[0] = low[(j % here) * size : (j % here + 1) * size]

    groups = []
    for j, w in enumerate((w0, w1, w2, w3)):
        groups.append([pltpu.make_async_copy(w, w_ref.at[:, j * wide : (j + 1) * wide], sems.at[j])])
    fetch(groups, step, body)


def make(mesh):
    nd, ntens = mesh.shape["dp"], mesh.shape["tensor"]
    nh = nd // 2
    groups = [[2 * z + b for z in range(nh)] for b in range(2)]

    def across(array, axis, bit):
        size = nd if axis == "dp" else ntens
        return lax.ppermute(array, axis, [(i, i ^ bit) for i in range(size)])

    def along(array):
        return lax.all_to_all(array, "dp", 0, 0, tiled=True, axis_index_groups=groups)

    def turn(array, k):
        return lax.ppermute(array, "dp", [(2 * ((z + k) % nh) + b, 2 * z + b) for z in range(nh) for b in range(2)])

    def swap(array):
        return across(array, "tensor", 1)

    def summed(*outs):
        layout, ins, shapes = [], [], []
        for ranges in outs:
            layout.append([len(terms) for terms in ranges])
            columns = 0
            for terms in ranges:
                for array, lead in terms:
                    block = (1,) * len(lead) + (nh // 2,) + array.shape[-2:]
                    ins.append((array, block, lambda z, lead=lead: (*lead, z, 0, 0)))
                columns += array.shape[-1]
            shape = (nh, array.shape[-2], columns)
            shapes.append((shape, BF, (nh // 2,) + shape[1:], lambda z: (z, 0, 0)))
        return call(functools.partial(add_kernel, layout), (2,), ins, shapes, limit=63, cost=60.0)

    def turn(array, k):
        return lax.ppermute(array, "dp", [(2 * ((z + k) % nh) + b, 2 * z + b) for z in range(nh) for b in range(2)])

    def swap(array):
        return across(array, "tensor", 1)

    def settle(array):
        return jnp.sum(array.astype(F32), axis=0)

    def shards(
        tokens, w_qkv, b_qv, w_out, w_up, b_up, w_down, ln_gains, shifts, lengths, segments, pair_ids, targets
    ):
        part_len, row_count, width = tokens.shape
        rb = w_up.shape[0]
        hidden = w_up.shape[1]
        local = w_qkv.shape[2]
        hb = b_up.shape[1]
        hd = hb * nd
        heads = local // hd
        seq = segments.shape[1]
        rows = row_count // ntens
        count = rows * seq
        sents = rows * SEGS
        blk = 256
        steps = count // blk
        t = lax.axis_index("tensor")
        d = lax.axis_index("dp")
        fused = rb % 16 == 0
        depth, rbk = (nh, rb) if fused else (1, width // 2)
        lo_bit = (d % 2 if fused else d * 0).astype(jnp.int32)
        turned_by = (d // 2 if nh <= 4 else d * 0).astype(jnp.int32)
        here, here_first = jnp.stack([lo_bit, lo_bit * 0]), jnp.stack([lo_bit, turned_by])
        t_arr = t.astype(jnp.int32).reshape(1)

        def ready(own, other):
            if fused:
                return [own, other]
            first = jnp.where(d % 2 == 0, own, other)
            second = jnp.where(d % 2 == 0, other, own)
            full = jnp.stack([first, second], axis=1).reshape(2, 1, width // 2, own.shape[2])
            return [full[0], full[1]]

        def merged(own, other, place, after):
            if not fused:
                first = jnp.where(d % 2 == 0, own, other)
                second = jnp.where(d % 2 == 0, other, own)
                return jnp.stack([first, second], axis=1).reshape(width, own.shape[2])
            return call(
                merge_kernel,
                (1,),
                [(place, None, None), (own, None, None), (other, None, None)],
                [((width, own.shape[2]), BF, None, None)],
                scalars=1,
                after=after,
            )[0]

        def weights(pairs):
            return [(a, "any", None) for pair in pairs for a in ready(*pair)]

        def sems(n):
            return pltpu.SemaphoreType.DMA((n,))

        def pack(kernel, arrays, columns, after):
            return call(
                kernel,
                (nh,),
                [(a, None, None) for a in arrays],
                [((nh, rb, columns), BF, (1, rb, columns), lambda i: (i, 0, 0))],
                after=after,
            )[0]

        def cut(array):
            if fused:
                return array
            lead = array.shape[:-4]
            full = array.reshape(*lead, nh, 2, rb, array.shape[-1])
            first, second = full[..., 0, :, :], full[..., 1, :, :]
            return jnp.stack(
                [jnp.where(d % 2 == 0, first, second), jnp.where(d % 2 == 0, second, first)], axis=len(lead)
            )

        def uncut(array):
            if fused:
                return array
            mine, theirs = array[..., 0, :, :, :], array[..., 1, :, :, :]
            first, second = jnp.where(d % 2 == 0, mine, theirs), jnp.where(d % 2 == 0, theirs, mine)
            return jnp.stack([first, second], axis=-3).reshape(*array.shape[:-4], 2, 1, width // 2, array.shape[-1])

        deal_size = min(512, part_len * row_count)
        deal_block = deal_size // row_count
        dealt = call(
            deal_kernel,
            (part_len // deal_block,),
            [(t_arr, None, None), (tokens.reshape(part_len * row_count, width), (deal_size, width), lambda i, *_: (i, 0))],
            [((rows, part_len, width), BF, (rows, deal_block, width), lambda i, *_: (0, i, 0))] * ntens,
            scalars=1,
            cost=2.0,
        )
        x_parts = [dealt[0]] + [across(dealt[j], "tensor", j) for j in range(1, ntens)]

        mine = lax.dynamic_slice_in_dim(segments, t * rows, rows, 0).reshape(rows, ntens, part_len)
        own_len = lax.dynamic_slice_in_dim(lengths, t * rows, rows, 0)
        seg = jnp.stack([lax.dynamic_index_in_dim(mine, t ^ j, 1, False) for j in range(ntens)], axis=1)
        place = jnp.stack([(t ^ j) * part_len + jnp.arange(part_len) for j in range(ntens)])
        live = (place[None] < own_len[:, None, None]).reshape(rows, seq)
        seg = seg.reshape(rows, seq)
        key_code = jnp.where(live, seg, -1)
        query_code = jnp.where(live, seg, DEAD)
        sent_code = jnp.where(live, seg + SEGS * jnp.arange(rows)[:, None], -1).reshape(1, count)
        member = (key_code[:, None, :] == jnp.arange(SEGS)[None, :, None]).astype(F32)
        key_codes, query_codes = key_code.reshape(rows, 1, seq), query_code.reshape(rows, seq, 1)
        inv_count = (1.0 / jnp.sum(member, axis=2)).reshape(sents, 1)
        own_ids = (d * row_count + t * rows) * SEGS + jnp.arange(sents, dtype=jnp.int32)
        is_mine = pair_ids[None, :] == own_ids[:, None]
        mates = pair_ids.reshape(-1, 2)[:, ::-1].reshape(-1)
        mate = jnp.sum(jnp.where(is_mine, mates[None, :], 0), axis=1, keepdims=True)
        goal = jnp.sum(jnp.where(is_mine, jnp.repeat(targets, 2)[None, :], 0.0), axis=1, keepdims=True)
        own_ids = own_ids[:, None]

        qv_col = jnp.pad(b_qv.reshape(-1, 1), ((0, rb - b_qv.size), (0, 63)))
        wide = 3 * local + 64
        (first_piece,) = call(
            pack_one_kernel,
            (1,),
            [(w_qkv.reshape(rb, 3 * local), None, None), (qv_col, None, None)],
            [((rb, wide), BF, None, None)],
        )
        if nh <= 4:
            pieces1 = [first_piece] + [turn(first_piece, k) for k in range(1, nh)]
            own1 = call(
                stack_kernel,
                (1,),
                [(p, None, None) for p in pieces1],
                [((nh, rb, wide), BF, None, None)],
                after=[dealt[1]],
            )[0]
        else:
            own1 = along(jnp.broadcast_to(first_piece[None], (nh, rb, wide)))
        lo1 = across(own1, "dp", 1)
        w1 = {0: merged(own1, lo1, here_first, [key_codes, query_codes])}
        w1[1] = swap(w1[0])
        w1[2] = across(w1[0], "tensor", 2)
        extra = jnp.concatenate([ln_gains.T, shifts.T, b_up.reshape(-1, 1), jnp.zeros((rb, 57), BF)], axis=1)
        second_piece = pack(pack_two_kernel, [w_up, w_out, extra], hidden + 256, [dealt[1]])
        (second_piece,) = gate([second_piece], [own1])
        own2 = along(second_piece)
        third_piece = pack(pack_three_kernel, [w_down], hidden, [dealt[1]])

        k = np.arange(width)
        dd, within = k // rb, k % rb
        up_at = (within // hb) * hd + dd * hb + within % hb
        sup = np.zeros((width, width), np.float32)
        sup[k, up_at] = 1.0
        qv = within < 2 * heads * hb
        qv_at = (within // (heads * hb)) * local + ((within // hb) % heads) * hd + dd * hb + within % hb
        sqv = np.zeros((width, 2 * local), np.float32)
        sqv[k[qv], qv_at[qv]] = 1.0
        sup, sqv = jnp.asarray(sup, BF), jnp.asarray(sqv, BF)

        def whole(array):
            return (array, None, None)

        def whole_out(shape, dtype):
            return (shape, dtype, None, None)

        by_row = lambda r, *_: (r, 0, 0)

        def attend(xs, w, before, cost=9.0):
            outs = [
                ((rows, seq, 3 * local), BF, (1, seq, 3 * local), by_row),
                ((rows, heads, seq, seq), BF, (1, heads, seq, seq), lambda r, *_: (r, 0, 0, 0)),
                ((rows, seq, 256), BF, (1, seq, 256), by_row),
            ]
            if len(xs) > 1:
                outs.append(((rows, seq, width), BF, (1, seq, width), by_row))
            return call(
                functools.partial(attn_fwd_kernel, len(xs)),
                (rows,),
                [(a, (1,) + a.shape[1:], by_row) for a in xs]
                + [
                    whole(w),
                    whole(sqv),
                    (key_codes, (1, 1, seq), by_row),
                    (query_codes, (1, seq, 1), by_row),
                ],
                outs,
                scratch=[pltpu.VMEM((8, 2 * local), F32), pltpu.VMEM((seq, seq), F32)],
                after=before,
                limit=63,
                cost=cost,
            )

        kept = {}
        *kept[0], x = attend(x_parts, w1[0], [second_piece], 25.0)
        (own2,) = gate([own2], [kept[0][2]])
        lo2, far2 = across(own2, "dp", 1), across(own2, "tensor", 2)
        (third_piece,) = gate([third_piece], [own2])
        own3 = along(third_piece)
        kept[1] = attend([x], w1[1], [own2])
        w1[2], lo2 = gate([w1[2], lo2], [kept[1][2]])
        w1[3] = swap(w1[2])
        far_lo2 = across(lo2, "tensor", 2)
        kept[2] = attend([x], w1[2], [lo2])
        own3, far2 = gate([own3, far2], [kept[2][2]])
        lo3, far3 = across(own3, "dp", 1), across(own3, "tensor", 2)
        kept[3] = attend([x], w1[3], [own3, far2])
        far_lo2, lo3 = gate([far_lo2, lo3], [kept[3][2]])
        far_lo3 = across(lo3, "tensor", 2)
        w2 = [(own2, lo2), (swap(own2), swap(lo2)), (far2, far_lo2), (swap(far2), swap(far_lo2))]
        o_parts = [kept[j][2].reshape(count, 256) for j in range(4)]
        x_flat = x.reshape(count, width)

        def rows_of(array):
            return (array, (blk, array.shape[1]), lambda i, *_: (i, 0))

        def rows_out(shape, dtype):
            return (shape, dtype, (blk, shape[1]), lambda i, *_: (i, 0))

        all_w, all_o = pltpu.VMEM((width, 4 * hidden), BF), pltpu.VMEM((width, 4 * 256), BF)
        xh1, rstd1, u, h, g, small = call(
            middle_kernel,
            (steps,),
            [whole(here)] + [rows_of(o) for o in o_parts] + [rows_of(x_flat), whole(sup)] + weights(w2),
            [
                rows_out((count, width), BF),
                rows_out((count, 1), F32),
                rows_out((count, width), BF),
                rows_out((count, 4 * hidden), BF),
                rows_out((count, 4 * hidden), BF),
                whole_out((8, width), F32),
            ],
            scratch=[all_o, all_w, pltpu.VMEM((8, 4 * hidden), F32), sems(16 * depth)],
            scalars=1,
            after=[lo3],
            limit=63,
            cost=20.0,
        )
        far3, far_lo3 = gate([far3, far_lo3], [u])
        w3 = [(own3, lo3), (swap(own3), swap(lo3)), (far3, far_lo3), (swap(far3), swap(far_lo3))]
        code_spec = (sent_code, (1, blk), lambda i, *_: (0, i))
        span = blk // part_len
        part_out = lambda i, *_: (i * span // ntens, 0, 0)
        xh2, rstd2, y0, y1, y2, y3, pooled = call(
            down_kernel,
            (steps,),
            [whole(here), rows_of(h), rows_of(u), whole(small), code_spec, whole(inv_count)] + weights(w3),
            [rows_out((count, width), BF), rows_out((count, 1), F32)]
            + [((rows, part_len, width), BF, (1, part_len, width), part_out)] * ntens
            + [whole_out((nd * ntens, sents, width), BF)],
            scratch=[pltpu.VMEM((sents, width), F32), all_w, sems(8 * depth)],
            scalars=1,
            limit=63,
            cost=14.0,
        )

        def send_back(parts):
            return [parts[0]] + [across(parts[j], "tensor", j) for j in range(1, ntens)]

        def collected(parts, after=()):
            (out,) = call(
                collect_kernel,
                (part_len // deal_block,),
                [whole(t_arr)] + [(a, (rows, deal_block, width), lambda i, *_: (0, i, 0)) for a in parts],
                [((part_len * row_count, width), BF, (deal_size, width), lambda i, *_: (i, 0))],
                scalars=1,
                after=after,
                limit=63,
                cost=30.0,
            )
            return out.reshape(part_len, row_count, width)

        every = lax.all_to_all(pooled, ("dp", "tensor"), 0, 0, tiled=True).reshape(nd * ntens * sents, width)

        shape = (2, 2, depth, rbk, hidden)
        half = (2,) + shape[2:]

        def blocked(array):
            return (blk, array.shape[1]), lambda i, *_: (jnp.minimum(i, steps - 1), 0)

        def blocked_out(shape, dtype):
            return (shape, dtype, *blocked(jax.ShapeDtypeStruct(shape, dtype)))

        late = lambda i: jnp.maximum(i - steps, 0)
        df, de, send3, sums2, dbup = call(
            functools.partial(feed_back_kernel, steps),
            (steps + 2,),
            [whole(here), whole(every), whole(own_ids), whole(mate), whole(goal), whole(inv_count)]
            + [(sent_code, (1, blk), lambda i, *_: (0, jnp.minimum(i, steps - 1)))]
            + [(a, *blocked(a)) for a in (xh2, rstd2)]
            + [whole(small), (g, *blocked(g))]
            + [(h, (count, hidden), lambda i, *_: (0, 2 * late(i) + 1))]
            + weights(w3),
            [
                blocked_out((count, width), BF),
                blocked_out((count, 4 * hidden), BF),
                (shape, BF, (1,) + shape[1:], lambda i, *_: (late(i), 0, 0, 0, 0)),
                whole_out((8, width), F32),
                whole_out((8, 4 * hidden), F32),
            ],
            scratch=[pltpu.VMEM((3, sents, width), BF), pltpu.VMEM((count, width), BF), all_w, sems(8 * depth)],
            scalars=1,
            limit=63,
            cost=32.0,
        )

        hidden_parts = send_back([y0, y1, y2, y3])

        def grad_part(a, b, odd, kernel, got, outs, after):
            return call(
                kernel,
                (2,),
                [whole(here), whole(a), (b, (count, hidden), lambda j, *_: (0, 2 * j + odd))]
                + [(v, (1,) + v.shape[1:], lambda j, *_: (j, 0, 0, 0, 0)) for v in got],
                outs,
                scalars=1,
                after=after,
                limit=63,
                cost=40.0,
            )

        both_out = [(shape, BF, (1,) + shape[1:], lambda j, *_: (j, 0, 0, 0, 0))]
        hidden_out = collected(hidden_parts, [send3])
        (sendu,) = grad_part(u, de, 1, grad_send_kernel, [], both_out, [send3, hidden_out])
        got = uncut(swap(cut(send3)))
        stay3, fly3 = grad_part(
            df, h, 0, functools.partial(grad_keep_kernel, True), [got],
            [(half, BF, (1,) + half[1:], lambda j, *_: (j, 0, 0, 0))] * 2, [sendu],
        )
        if not fused:
            both = cut(jnp.stack([stay3, fly3], axis=1))
            stay3, fly3 = both[:, 0], both[:, 1]
        got = uncut(swap(cut(sendu)))
        stayu, flyu = grad_part(
            u, de, 0, functools.partial(grad_keep_kernel, False), [got], [whole_out(half, BF)] * 2, [fly3]
        )
        stayu, flyu = cut(stayu), cut(flyu)
        got3x = across(fly3, "dp", 1)
        gotuy = across(flyu, "tensor", 2)

        da, do, sums1 = call(
            norm_back_kernel,
            (steps,),
            [whole(here), rows_of(de), rows_of(df), rows_of(xh1), rows_of(rstd1), whole(small)] + weights(w2),
            [
                rows_out((count, width), BF),
                rows_out((count, 4 * 256), BF),
                whole_out((8, width), F32),
            ],
            scratch=[all_w, all_o, sems(16 * depth)],
            scalars=1,
            after=[flyu],
            limit=63,
            cost=14.0,
        )
        da_rows, do_rows = da.reshape(rows, seq, width), do.reshape(rows, seq, 4 * 256)
        grad_cols = 4 * local

        def attend_back(j, got, after):
            qkv, p, o = kept[j]
            half = (depth, rbk, grad_cols)
            kinds = [whole_out((2,) + half, BF)] if got is None else [whole_out(half, BF)] * 2
            keeps = 0 if got is None else 1
            whole_row = pltpu.VMEM((rows, seq, width), BF)
            *outs, sums, dproj = call(
                functools.partial(attn_bwd_kernel, keeps),
                (rows,),
                [
                    whole(here),
                    (qkv, (1, seq, 3 * local), by_row),
                    (p, (1, heads, seq, seq), lambda r, *_: (r, 0, 0, 0)),
                    (o, (1, seq, 256), by_row),
                    (do_rows, (1, seq, 256), lambda r, *_: (r, 0, j)),
                    (x, "any", None),
                    (da_rows, "any", None),
                ]
                + ([] if got is None else [(uncut(got), "any", None)]),
                kinds
                + [whole_out((8, 3 * local), F32), ((rows, seq, wide), BF, (1, seq, wide), by_row)],
                scratch=[pltpu.VMEM((width, grad_cols), F32), whole_row, whole_row, sems(2 * rows + keeps)]
                + [pltpu.VMEM((2,) + half, BF)] * keeps,
                scalars=1,
                after=after,
                limit=63,
                cost=11.0,
            )
            if got is None:
                out = cut(outs[0])
            elif fused:
                out = tuple(outs)
            else:
                both = cut(jnp.stack(outs))
                out = both[0], both[1]
            sums_of[j], dprojs[j] = sums, dproj.reshape(count, wide)
            return out

        sums_of, dprojs = {}, {}
        back3 = attend_back(3, None, [flyu])
        got_far = swap(back3)
        got3x, gotuy = gate([got3x, gotuy], [back3])
        turn3, turnu = summed([[(stay3, (1,)), (got3x, (1,))]], [[(stayu, (1,)), (gotuy, (1,))]])
        got3y, gotux = across(turn3, "tensor", 2), across(turnu, "dp", 1)
        stay_far, fly_far = attend_back(2, got_far, [turn3, turnu])
        got_fly = across(fly_far, "dp", 1)
        got3y, gotux = gate([got3y, gotux], [stay_far])
        (end,) = summed([[(stay3, (0,)), (got3x, (0,)), (got3y, ())], [(stayu, (0,)), (gotuy, (0,)), (gotux, ())]])
        end_sent = end
        end = along(end)
        back1 = attend_back(1, None, [end_sent])
        got_near = swap(back1)
        small_keep, small_send = call(
            small_kernel,
            (1,),
            [whole(a) for a in (sums1, sums2, dbup, sums_of[1], sums_of[2], sums_of[3])],
            [whole_out((24, width), F32)] * 2,
            after=[back1],
        )
        small_keep = small_keep + swap(small_send)
        small_got = across(jnp.concatenate([small_keep[:8], small_keep[16:]], axis=0), "tensor", 2)
        (got_fly,) = gate([got_fly], [small_keep])
        (turn1,) = summed([[(stay_far, ()), (got_fly, ())]])
        got_turn1 = across(turn1, "tensor", 2)
        stay_near, fly_near = attend_back(0, got_near, [turn1])
        got1 = across(fly_near, "dp", 1)
        span_out = lambda i, *_: (i * span // ntens, 0, 0)
        dx_parts = call(
            input_back_kernel,
            (steps,),
            [rows_of(dprojs[j]) for j in range(4)] + [rows_of(da)] + [(w1[j], "any", None) for j in range(4)],
            [((rows, part_len, width), BF, (1, part_len, width), span_out)] * ntens,
            scratch=[pltpu.VMEM((width, 4 * wide), BF), sems(4)],
            limit=63,
            after=[stay_near],
            cost=8.0,
        )
        token_parts = send_back(dx_parts)

        got1, got_turn1, end = gate([got1, got_turn1, end], [dx_parts[0]])
        (last1,) = summed([[(stay_near, ()), (got1, ()), (got_turn1, ())]])
        small_got, near_sums = gate([small_got, sums_of[0]], [last1])
        near_sums = jnp.concatenate([near_sums[:1, :local], near_sums[:1, 2 * local :]], axis=1)
        own = small_keep[:16] + small_got + jnp.pad(near_sums, ((9, 6), (0, width - 2 * local)))
        bit = 1
        while bit < nd:
            own = own + across(own, "dp", bit)
            bit *= 2
        rest = lax.dynamic_slice_in_dim(own[:6], (d * ntens + t) * (width // (nd * ntens)), width // (nd * ntens), 1)
        grad_b_up = lax.dynamic_slice_in_dim(own[8].reshape(hidden // hd, hd), d * hb, hb, 1)
        grad_b_qv = lax.dynamic_slice_in_dim(own[9, : 2 * local].reshape(2, heads, hd), d * hb, hb, 2)
        grad_one = settle(along(last1))
        grad_tokens = collected(token_parts, [last1])
        end = settle(end)
        grad_down, grad_up = end[:, :hidden], end[:, hidden:]
        return (
            hidden_out,
            grad_tokens,
            grad_one[:, : 3 * local].reshape(rb, 3, local),
            grad_b_qv,
            grad_one[:, 3 * local :].T,
            grad_up,
            grad_b_up,
            grad_down.T,
            rest[:2],
            rest[2:],
        )

    return shards


def solution(mesh):
    return jax.shard_map(
        make(mesh),
        mesh=mesh,
        in_specs=(
            P("tensor", "dp", None),
            P("dp", None, "tensor"),
            P(None, "tensor", "dp"),
            P("tensor", "dp"),
            P("dp", "tensor"),
            P("tensor", "dp"),
            P("tensor", "dp"),
            P(None, "dp"),
            P(None, "dp"),
            P("dp"),
            P("dp", None),
            P(),
            P(),
        ),
        out_specs=(
            P("tensor", "dp", None),
            P("tensor", "dp", None),
            P("dp", None, "tensor"),
            P(None, "tensor", "dp"),
            P("tensor", "dp"),
            P("dp", "tensor"),
            P("tensor", "dp"),
            P("tensor", "dp"),
            P(None, ("dp", "tensor")),
            P(None, ("dp", "tensor")),
        ),
        check_vma=False,
    )
```

```python
import functools
import math

import jax
import jax.numpy as jnp
import numpy as np
from jax import lax
from jax.experimental import pallas as pl
from jax.experimental.pallas import tpu as pltpu
from jax.sharding import PartitionSpec as P

SEGS = 4
EPS_NORM = 1e-05
EPS_COS = 1e-06
LOSS_SCALE = 4096.0
NEG = -1e30

BF = jnp.bfloat16
F32 = jnp.float32
MIB = 1024 * 1024
SHARE = 0.3


def dot(a, b, ca, cb):
    return lax.dot_general(a, b, (((ca,), (cb,)), ((), ())), preferred_element_type=F32)


def nn(a, b):
    return dot(a, b, 1, 0)


def nt(a, b):
    return dot(a, b, 1, 1)


def tn(a, b):
    return dot(a, b, 0, 0)


def call(kernel, grid, ins, outs, scratch=(), cost=1.0, scalars=0, limit=16, after=()):
    def spec(shape, block, index):
        if isinstance(block, str):
            return pl.BlockSpec(memory_space=pl.ANY)
        if block is None:
            zeros = (0,) * len(shape)
            return pl.BlockSpec(shape, lambda *_: zeros)
        return pl.BlockSpec(block, index)

    in_specs = [spec(a.shape, b, m) for a, b, m in ins[scalars:]]
    out_specs = [spec(s, b, m) for s, _, b, m in outs]
    flops = int(cost * SHARE * 1.15e9)
    body, known = kernel, len(ins)
    if after:
        in_specs += [pl.BlockSpec(memory_space=pl.ANY)] * len(after)

        def body(*refs):
            return kernel(*refs[:known], *refs[known + len(after) :])

    return pl.pallas_call(
        body,
        grid_spec=pltpu.PrefetchScalarGridSpec(
            num_scalar_prefetch=scalars,
            grid=grid,
            in_specs=in_specs,
            out_specs=out_specs,
            scratch_shapes=list(scratch),
        ),
        out_shape=[jax.ShapeDtypeStruct(s, d) for s, d, _, _ in outs],
        compiler_params=pltpu.CompilerParams(
            dimension_semantics=("arbitrary",) * len(grid), vmem_limit_bytes=limit * MIB
        ),
        cost_estimate=pl.CostEstimate(flops=flops, bytes_accessed=1024, transcendentals=0),
    )(*[a for a, _, _ in ins], *after)


def gate(arrays, after):
    n = len(arrays)
    anywhere = pl.BlockSpec(memory_space=pl.ANY)
    return pl.pallas_call(
        lambda *refs: None,
        in_specs=[anywhere] * (n + len(after)),
        out_specs=[anywhere] * n,
        out_shape=[jax.ShapeDtypeStruct(a.shape, a.dtype) for a in arrays],
        input_output_aliases={i: i for i in range(n)},
        cost_estimate=pl.CostEstimate(flops=1, bytes_accessed=1, transcendentals=0),
    )(*arrays, *after)


def deal_kernel(t_ref, tok_ref, *out_refs):
    size = tok_ref.shape[0]
    parts = len(out_refs)
    rows, block = out_refs[0].shape[0], out_refs[0].shape[1]
    t = t_ref[0]
    m = lax.broadcasted_iota(jnp.int32, (size, size), 0)
    n = lax.broadcasted_iota(jnp.int32, (size, size), 1)
    part, row, place = m // (rows * block), (m // block) % rows, m % block
    source = place * (parts * rows) + jnp.bitwise_xor(part, t) * rows + row
    pick = jnp.where(source == n, 1.0, 0.0).astype(BF)
    moved = nn(pick, tok_ref[...]).astype(BF)
    for j, out in enumerate(out_refs):
        for r in range(rows):
            at = (j * rows + r) * block
            out[r] = moved[at : at + block]


def collect_kernel(t_ref, *refs):
    *in_refs, out_ref = refs
    size = out_ref.shape[0]
    parts = len(in_refs)
    rows, block = in_refs[0].shape[0], in_refs[0].shape[1]
    t = t_ref[0]
    m = lax.broadcasted_iota(jnp.int32, (size, size), 1)
    n = lax.broadcasted_iota(jnp.int32, (size, size), 0)
    part, row, place = m // (rows * block), (m // block) % rows, m % block
    target = place * (parts * rows) + jnp.bitwise_xor(part, t) * rows + row
    pick = jnp.where(target == n, 1.0, 0.0).astype(BF)
    joined = jnp.concatenate([ref[r] for ref in in_refs for r in range(rows)], axis=0)
    out_ref[...] = nn(pick, joined).astype(BF)


def stack_kernel(*refs):
    *ins, out_ref = refs
    for i, ref in enumerate(ins):
        out_ref[i] = ref[...]


def add_kernel(layout, *refs):
    ins, outs = list(refs[: sum(map(sum, layout))]), refs[sum(map(sum, layout)) :]
    for terms, out_ref in zip(layout, outs):
        at = 0
        for n in terms:
            value = 0.0
            for ref in [ins.pop(0) for _ in range(n)]:
                value = value + ref[...].astype(F32).reshape(out_ref.shape[:2] + ref.shape[-1:])
            columns = value.shape[-1]
            out_ref[:, :, at : at + columns] = value.astype(BF)
            at += columns


def merge_kernel(here_ref, own_ref, other_ref, out_ref):
    depth, rows = own_ref.shape[0], own_ref.shape[1]
    lo = here_ref[0]
    for z in range(depth):
        at = lax.rem(z + depth - here_ref[1], depth)
        mine, theirs = own_ref[at], other_ref[at]
        for b in range(2):
            at = (2 * z + b) * rows
            out_ref[at : at + rows, :] = jnp.where(lo == b, mine, theirs)


def weight_copies(pairs, here_ref, columns, dest, sems, first=0):
    groups = []
    n = first
    for j, (own, other) in enumerate(pairs):
        depth, rows = own.shape[0], own.shape[1]
        size = columns.stop - columns.start
        group = []
        for z in range(depth):
            src = lax.rem(z + depth - here_ref[1], depth)
            for ref, b in ((own, here_ref[0]), (other, 1 - here_ref[0])):
                to = dest.at[pl.ds(pl.multiple_of((2 * z + b) * rows, rows), rows), j * size : (j + 1) * size]
                group.append(pltpu.make_async_copy(ref.at[src, :, columns], to, sems.at[n]))
                n += 1
        groups.append(group)
    return groups


def paired(refs):
    return list(zip(refs[::2], refs[1::2]))


def attn_fwd_kernel(parts, *refs):
    x_refs, refs = refs[:parts], refs[parts:]
    w_ref, sqv_ref, kf_ref, qf_ref, qkv_ref, p_ref, o_ref, *refs = refs
    *x_out, bias_ref = refs
    local = qkv_ref.shape[2] // 3
    heads = p_ref.shape[1]
    hd = local // heads

    @pl.when(pl.program_id(0) == 0)
    def _():
        bias_ref[...] = tn(w_ref[:, 3 * local :][:, :8], sqv_ref[...])

    x = x_refs[0][0]
    if parts > 1:
        x = jnp.concatenate([ref[0] for ref in x_refs], axis=0)
        x_out[0][0] = x
    projected = nn(x, w_ref[:, : 3 * local])
    q_all = ((projected[:, :local] + bias_ref[0:1, :local]) * 0.125).astype(BF)
    k_all = projected[:, local : 2 * local].astype(BF)
    v_all = (projected[:, 2 * local :] + bias_ref[0:1, local:]).astype(BF)
    qkv_ref[0, :, :local] = q_all
    qkv_ref[0, :, local : 2 * local] = k_all
    qkv_ref[0, :, 2 * local :] = v_all
    outs = []
    for h in range(heads):
        at = slice(h * hd, (h + 1) * hd)
        q = jnp.concatenate([q_all[:, at], qf_ref[0]], axis=1)
        k = jnp.concatenate([k_all[:, at], kf_ref[0]], axis=1)
        s = nt(q, k)
        top = jnp.max(s, axis=-1, keepdims=True)
        e = jnp.exp(s - top)
        total = jnp.sum(e, axis=-1, keepdims=True)
        p = (e * (1.0 / total)).astype(BF)
        p_ref[0, h] = p
        outs.append(nn(p, v_all[:, at]).astype(BF))
    pad = jnp.zeros((outs[0].shape[0], o_ref.shape[2] - local), BF)
    o_ref[0] = jnp.concatenate(outs + [pad], axis=1)


def norm(z):
    centred = z - jnp.mean(z, axis=-1, keepdims=True)
    rstd = lax.rsqrt(jnp.mean(centred * centred, axis=-1, keepdims=True) + EPS_NORM)
    return centred * rstd, rstd


def norm_back(dy, xh, rstd, gain):
    dxh = dy * gain
    mean = jnp.mean(dxh, axis=-1, keepdims=True)
    proj = jnp.mean(dxh * xh, axis=-1, keepdims=True)
    return rstd * (dxh - mean - xh * proj)


def turned(a):
    rows = a.shape[1]
    eye = (
        lax.broadcasted_iota(jnp.int32, (rows, rows), 0) == lax.broadcasted_iota(jnp.int32, (rows, rows), 1)
    ).astype(BF)
    return nt(eye, a).astype(BF)


def pack_one_kernel(w_ref, extra_ref, piece_ref):
    piece_ref[...] = jnp.concatenate([w_ref[...], extra_ref[...]], axis=1)


def pack_two_kernel(up_ref, out_ref, extra_ref, piece_ref):
    hidden = up_ref.shape[1]
    piece_ref[0, :, :hidden] = up_ref[...]
    piece_ref[0, :, hidden:] = jnp.concatenate([turned(out_ref[...]), extra_ref[...]], axis=1)


def pack_three_kernel(a_ref, piece_ref):
    piece_ref[0] = turned(a_ref[...])


def gelu_parts(e):
    cdf = 0.5 + 0.5 * lax.erf(e * (1.0 / math.sqrt(2.0)))
    return e * cdf, cdf + e * (jnp.exp(-0.5 * e * e) * (1.0 / math.sqrt(2.0 * math.pi)))


def fetch(groups, step, body):
    @pl.when(step == 0)
    def _():
        for group in groups:
            for copy in group:
                copy.start()

        def ready(i):
            for copy in groups[i]:
                copy.wait()

        body(ready)

    @pl.when(step > 0)
    def _():
        body(None)


def middle_kernel(here_ref, o0, o1, o2, o3, x_ref, sup_ref, *refs):
    ws, refs = paired(refs[:8]), refs[8:]
    xh_ref, rstd_ref, u_ref, h_ref, g_ref, small_ref, wo_ref, wu_ref, bup_ref, sems = refs
    width = x_ref.shape[1]
    hidden = wu_ref.shape[1] // 4
    wide = wo_ref.shape[1] // 4
    per = 2 * ws[0][0].shape[0]
    groups = weight_copies(ws, here_ref, slice(hidden, hidden + wide), wo_ref, sems)
    groups += weight_copies(ws, here_ref, slice(0, hidden), wu_ref, sems, 4 * per)

    def body(ready):
        if ready:
            for j in range(4):
                ready(j)
            eye = (
                lax.broadcasted_iota(jnp.int32, (width, width), 0)
                == lax.broadcasted_iota(jnp.int32, (width, width), 1)
            ).astype(BF)
            local = wide - 64
            small_ref[...] = tn(wo_ref[:, local:wide][:, :8], eye)
            cols = [wo_ref[:, j * wide + local : (j + 1) * wide][:, :8] for j in range(4)]
            rows = tn(jnp.concatenate(cols, axis=1), sup_ref[...])
            for j in range(4):
                bup_ref[:, j * hidden : (j + 1) * hidden] = rows[8 * j : 8 * j + 8]
        o = jnp.concatenate([o0[...], o1[...], o2[...], o3[...]], axis=1)
        z = x_ref[...].astype(F32) + (nt(o, wo_ref[...]) + small_ref[2:3])
        xh, rstd = norm(z)
        xh_ref[...] = xh.astype(BF)
        rstd_ref[...] = rstd
        u = (xh * small_ref[0:1] + small_ref[3:4]).astype(BF)
        u_ref[...] = u
        for j in range(4 if ready else 1):
            at = slice(j * hidden, (j + 1) * hidden) if ready else slice(0, 4 * hidden)
            if ready:
                ready(4 + j)
            h, g = gelu_parts(nn(u, wu_ref[:, at]) + bup_ref[6:7, at])
            h_ref[:, at] = h.astype(BF)
            g_ref[:, at] = g.astype(BF)

    fetch(groups, pl.program_id(0), body)


def split3(v):
    a = v.astype(BF)
    rest = v - a.astype(F32)
    b = rest.astype(BF)
    c = (rest - b.astype(F32)).astype(BF)
    return a, b, c


def down_kernel(here_ref, h_ref, u_ref, small_ref, code_ref, inv_ref, *refs):
    ws, refs = paired(refs[:8]), refs[8:]
    xh_ref, rstd_ref, y0, y1, y2, y3, pool_ref, acc_ref, w_ref, sems = refs
    y_refs = (y0, y1, y2, y3)
    step = pl.program_id(0)
    hidden = w_ref.shape[1] // 4

    @pl.when(step == 0)
    def _():
        acc_ref[...] = jnp.zeros_like(acc_ref)

    def body(ready):
        if ready:
            ready(0)
            f = nt(h_ref[:, :hidden], w_ref[:, :hidden])
            for j in range(1, 4):
                ready(j)
                f += nt(h_ref[:, j * hidden : (j + 1) * hidden], w_ref[:, j * hidden : (j + 1) * hidden])
        else:
            f = nt(h_ref[...], w_ref[...])
        xh, rstd = norm(u_ref[...].astype(F32) + (f + small_ref[4:5]))
        y2 = xh * small_ref[1:2] + small_ref[5:6]
        xh_ref[...] = xh.astype(BF)
        rstd_ref[...] = rstd
        low = y2.astype(BF)
        size = y_refs[0].shape[1]
        here = low.shape[0] // size
        for j, ref in enumerate(y_refs):

            @pl.when(lax.rem(step, 4 // here) == j // here)
            def _():
                ref[0] = low[(j % here) * size : (j % here + 1) * size]

        member = (lax.broadcasted_iota(jnp.int32, (8, y2.shape[0]), 0) == code_ref[...]).astype(BF)
        a, b, c = split3(y2)
        acc_ref[...] += nn(member, a) + nn(member, b) + nn(member, c)

    fetch(weight_copies(ws, here_ref, slice(0, hidden), w_ref, sems), step, body)

    @pl.when(step == pl.num_programs(0) - 1)
    def _():
        low = (acc_ref[...] * inv_ref[...]).astype(BF)

        def put(i, carry):
            pool_ref[i] = low
            return carry

        lax.fori_loop(0, pool_ref.shape[0], put, 0)


def loss_grad(pooled_ref, ids_ref, mate_ref, target_ref, inv_ref):
    pooled = pooled_ref[...]
    places = lax.broadcasted_iota(jnp.int32, (8, pooled.shape[0]), 1)
    first = nn((places == ids_ref[...]).astype(BF), pooled)
    second = nn((places == mate_ref[...]).astype(BF), pooled)
    inner = jnp.sum(first * second, axis=-1, keepdims=True)
    ra = lax.rsqrt(jnp.sum(first * first, axis=-1, keepdims=True) + EPS_COS)
    rb = lax.rsqrt(jnp.sum(second * second, axis=-1, keepdims=True) + EPS_COS)
    missed = inner * ra * rb - target_ref[...]
    grad = (2.0 * LOSS_SCALE) * missed * (second * (ra * rb) - first * (inner * rb * ra * ra * ra))
    return grad * inv_ref[...]


def rowsum(v):
    return jnp.sum(v, axis=0, keepdims=True)


def feed_back_kernel(
    blocks, here_ref, pooled_ref, ids_ref, mate_ref, target_ref, inv_ref, code_ref, xh_ref, rstd_ref, small_ref,
    g_ref, h_ref, *refs,
):
    ws, refs = paired(refs[:8]), refs[8:]
    df_ref, de_ref, send_ref, sum_ref, bup_ref, gp_ref, all_ref, w_ref, sems = refs
    hidden = w_ref.shape[1] // 4
    step = pl.program_id(0)

    @pl.when(step == 0)
    def _():
        grad = loss_grad(pooled_ref, ids_ref, mate_ref, target_ref, inv_ref)
        for i, part in enumerate(split3(grad)):
            gp_ref[i] = part
        sum_ref[...] = jnp.zeros_like(sum_ref)
        bup_ref[...] = jnp.zeros_like(bup_ref)

    def body(ready):
        size = xh_ref.shape[0]
        member = (lax.broadcasted_iota(jnp.int32, (8, size), 0) == code_ref[...]).astype(BF)
        dy = tn(member, gp_ref[0]) + tn(member, gp_ref[1]) + tn(member, gp_ref[2])
        xh = xh_ref[...].astype(F32)
        dz = norm_back(dy, xh, rstd_ref[...], small_ref[1:2])
        sum_ref[0:1] += rowsum(dy * xh)
        sum_ref[1:2] += rowsum(dy)
        sum_ref[2:3] += rowsum(dz)
        df = dz.astype(BF)
        df_ref[...] = df
        all_ref[pl.ds(pl.multiple_of(step * size, size), size), :] = df
        for j in range(4 if ready else 1):
            at = slice(j * hidden, (j + 1) * hidden) if ready else slice(0, 4 * hidden)
            if ready:
                ready(j)
            de = (nn(df, w_ref[:, at]) * g_ref[:, at].astype(F32)).astype(BF)
            de_ref[:, at] = de
            bup_ref[0:1, at] += rowsum(de.astype(F32))

    @pl.when(step < blocks)
    def _():
        fetch(weight_copies(ws, here_ref, slice(0, hidden), w_ref, sems), step, body)

    @pl.when(step >= blocks)
    def _():
        pieces(tn(all_ref[...], h_ref[...]), here_ref, send_ref.at[0], slice(0, hidden))


def norm_back_kernel(here_ref, de_ref, df_ref, xh_ref, rstd_ref, small_ref, *refs):
    ws, refs = paired(refs[:8]), refs[8:]
    da_ref, do_ref, sum_ref, w_ref, wo_ref, sems = refs
    step = pl.program_id(0)
    hidden, wide = w_ref.shape[1] // 4, wo_ref.shape[1] // 4
    per = 2 * ws[0][0].shape[0]
    groups = weight_copies(ws, here_ref, slice(0, hidden), w_ref, sems)
    groups += weight_copies(ws, here_ref, slice(hidden, hidden + wide), wo_ref, sems, 4 * per)

    @pl.when(step == 0)
    def _():
        sum_ref[...] = jnp.zeros_like(sum_ref)

    def body(ready):
        dy = df_ref[...].astype(F32)
        for j in range(4 if ready else 1):
            at = slice(j * hidden, (j + 1) * hidden) if ready else slice(0, 4 * hidden)
            if ready:
                ready(j)
            dy = dy + nt(de_ref[:, at], w_ref[:, at])
        xh = xh_ref[...].astype(F32)
        dz = norm_back(dy, xh, rstd_ref[...], small_ref[0:1])
        sum_ref[0:1] += rowsum(dy * xh)
        sum_ref[1:2] += rowsum(dy)
        sum_ref[2:3] += rowsum(dz)
        da = dz.astype(BF)
        da_ref[...] = da
        if ready:
            for j in range(4):
                ready(4 + j)
        do_ref[...] = nn(da, wo_ref[...]).astype(BF)

    fetch(groups, step, body)


def pieces(grad, here_ref, ref, at):
    depth, rows = ref.shape[1], ref.shape[2]
    low = grad.astype(BF)
    for z in range(depth):
        for b in range(2):
            part = low[(2 * z + b) * rows : (2 * z + b + 1) * rows]
            ref[here_ref[0] if b == 0 else 1 - here_ref[0], z, :, at] = part


def grad_send_kernel(here_ref, *refs):
    *ins, send_ref = refs
    at = 0
    for grad in (tn(a[...], b[...]) for a, b in zip(ins[::2], ins[1::2])):
        pieces(grad, here_ref, send_ref.at[0], slice(at, at + grad.shape[1]))
        at += grad.shape[1]


def grad_keep_kernel(by_row, here_ref, *refs):
    *ins, got_ref, stay_ref, fly_ref = refs
    depth, rows = got_ref.shape[2], got_ref.shape[3]
    lo = here_ref[0]
    j = pl.program_id(0)
    at = 0
    for grad in (tn(a[...], b[...]) for a, b in zip(ins[::2], ins[1::2])):
        cols = slice(at, at + grad.shape[1])
        for z in range(depth):
            first, second = (grad[(2 * z + b) * rows : (2 * z + b + 1) * rows] for b in range(2))
            mine, theirs = jnp.where(lo == 0, first, second), jnp.where(lo == 0, second, first)
            mine = (mine + got_ref[0, 0, z, :, cols].astype(F32)).astype(BF)
            theirs = (theirs + got_ref[0, 1, z, :, cols].astype(F32)).astype(BF)
            if by_row:
                stay_ref[0, z, :, cols] = mine
                fly_ref[0, z, :, cols] = theirs
            else:

                @pl.when(j == 0)
                def _():
                    stay_ref[0, z, :, cols] = mine
                    stay_ref[1, z, :, cols] = theirs

                @pl.when(j == 1)
                def _():
                    fly_ref[0, z, :, cols] = mine
                    fly_ref[1, z, :, cols] = theirs

        at += grad.shape[1]


def attn_bwd_kernel(keeps, here_ref, qkv_ref, p_ref, o_ref, do_ref, x_any, da_any, *refs):
    got_any, refs = refs[:keeps], refs[keeps:]
    piece_refs, refs = refs[: 1 + keeps], refs[1 + keeps :]
    sum_ref, dproj_ref, acc_ref, xs, das, sems = refs[: len(refs) - keeps]
    got_refs = refs[len(refs) - keeps :]
    r = pl.program_id(0)
    rows = xs.shape[0]
    local = qkv_ref.shape[2] // 3
    heads = p_ref.shape[1]
    hd = local // heads

    def row_copies(i):
        pairs = ((x_any, xs), (da_any, das))
        return [pltpu.make_async_copy(src.at[i], dst.at[i], sems.at[2 * i + n]) for n, (src, dst) in enumerate(pairs)]

    others = [
        pltpu.make_async_copy(src, dst, sems.at[2 * rows + n]) for n, (src, dst) in enumerate(zip(got_any, got_refs))
    ]

    @pl.when(r == 0)
    def _():
        for i in range(rows):
            for copy in row_copies(i):
                copy.start()
        for copy in others:
            copy.start()

    q_all, k_all, v_all = (qkv_ref[0, :, i * local : (i + 1) * local] for i in range(3))
    o_all, do_all = o_ref[0, :, :local], do_ref[0, :, :local]
    prod = o_all.astype(F32) * do_all.astype(F32)
    dq, dk, dv = [], [], []
    for h in range(heads):
        at = slice(h * hd, (h + 1) * hd)
        p = p_ref[0, h]
        do = do_all[:, at]
        dv.append(tn(do, p))
        dp = nt(do, v_all[:, at])
        mid = jnp.sum(prod[:, at], axis=-1, keepdims=True)
        ds = (p.astype(F32) * (dp - mid)).astype(BF)
        dq.append(nn(ds, k_all[:, at]))
        dk.append(tn(q_all[:, at], ds))
    dq = (jnp.concatenate(dq, axis=1).astype(BF).astype(F32) * 0.125).astype(BF)
    dkv = jnp.transpose(jnp.concatenate(dk + dv, axis=0)).astype(BF)
    dproj = jnp.concatenate([dq, dkv], axis=1)
    sums = jnp.broadcast_to(rowsum(dproj.astype(F32)), sum_ref.shape)

    for copy in row_copies(r):
        copy.wait()

    @pl.when(r == 0)
    def _():
        acc_ref[...] = jnp.zeros_like(acc_ref)
        sum_ref[...] = jnp.zeros_like(sum_ref)

    sum_ref[...] += sums
    acc_ref[:, : 3 * local] += tn(xs[r], dproj)
    acc_ref[:, 3 * local :] += tn(das[r], o_all)
    dproj_ref[0] = jnp.concatenate([dproj, jnp.zeros((dproj.shape[0], 64), BF)], axis=1)

    @pl.when(r == rows - 1)
    def _():
        if not keeps:
            pieces(acc_ref[...], here_ref, piece_refs[0], slice(0, acc_ref.shape[1]))
        else:
            others[0].wait()
            (got_ref,), (stay_ref, fly_ref) = got_refs, piece_refs
            depth, size = stay_ref.shape[0], stay_ref.shape[1]
            lo = here_ref[0]
            for z in range(depth):
                first, second = (acc_ref[(2 * z + b) * size : (2 * z + b + 1) * size] for b in range(2))
                mine, theirs = jnp.where(lo == 0, first, second), jnp.where(lo == 0, second, first)
                stay_ref[z] = (mine + got_ref[0, z].astype(F32)).astype(BF)
                fly_ref[z] = (theirs + got_ref[1, z].astype(F32)).astype(BF)


def small_kernel(norm1_ref, norm2_ref, up_ref, s2, s3, keep_ref, send_ref):
    local = s2.shape[1] // 3
    parts = {2: s2, 3: s3}
    for ref, pair in ((keep_ref, (0, 2)), (send_ref, (1, 3))):
        ref[...] = jnp.zeros_like(ref)
        for i, (src, row) in enumerate(
            ((norm1_ref, 0), (norm2_ref, 0), (norm1_ref, 2), (norm1_ref, 1), (norm2_ref, 2), (norm2_ref, 1))
        ):
            ref[i : i + 1] = src[row : row + 1]
        for n, j in enumerate(pair):
            ref[8 + 8 * n : 9 + 8 * n] = up_ref[0:1, j * ref.shape[1] : (j + 1) * ref.shape[1]]
            if j in parts:
                ref[9 + 8 * n : 10 + 8 * n, :local] = parts[j][0:1, :local]
                ref[9 + 8 * n : 10 + 8 * n, local : 2 * local] = parts[j][0:1, 2 * local :]


def split_small(own):
    rows = jnp.concatenate([own[0:6], own[8:10]], axis=0)
    high = rows.astype(BF)
    return jnp.concatenate([high, (rows - high.astype(F32)).astype(BF)], axis=0)


def last_kernel(here_ref, a_ref, b_ref, c_ref, own_ref, got_ref, *out_refs):
    depth, rows = a_ref.shape[0], a_ref.shape[1]
    small = split_small(own_ref[...] + got_ref[...])
    for k, out_ref in enumerate(out_refs):
        z = lax.rem(here_ref[1] + k, depth)
        total = a_ref[z].astype(F32) + b_ref[z].astype(F32) + c_ref[z].astype(F32)
        out_ref[:rows, :] = total.astype(BF)
        out_ref[rows:, :] = small


def final_kernel(place_ref, *refs):
    *parts, qkv_ref, out_ref, gains_ref, shifts_ref, up_ref, qv_ref = refs
    rows = qkv_ref.shape[0]
    total = parts[0][...].astype(F32)
    for ref in parts[1:]:
        total += ref[...].astype(F32)
    local = qkv_ref.shape[2]
    for i in range(3):
        qkv_ref[:, i, :] = total[:rows, i * local : (i + 1) * local]
    out_ref[...] = jnp.transpose(total[:rows, 3 * local :])
    small = total[rows : rows + 8] + total[rows + 8 :]
    width = small.shape[1]
    hd = width // up_ref.shape[0]
    lane = lax.broadcasted_iota(jnp.int32, (width, 128), 0)
    column = lax.broadcasted_iota(jnp.int32, (width, 128), 1)

    def pick(values, ones):
        ones = ones.astype(BF)
        a, b, c = split3(values)
        return nn(a, ones) + nn(b, ones) + nn(c, ones)

    size = gains_ref.shape[1]
    norms = pick(small, (lane == place_ref[0] + column) & (column < size))
    gains_ref[...] = norms[0:2, :size]
    shifts_ref[...] = norms[2:6, :size]
    group = up_ref.shape[1]
    ones = (lane % hd == place_ref[1] + column) & (column < group)
    head = lax.broadcasted_iota(jnp.int32, (16, width), 1) // hd
    row = lax.broadcasted_iota(jnp.int32, (16, width), 0)
    ups = pick(jnp.where(head == row, small[6:7], 0.0), ones)
    up_ref[...] = ups[: up_ref.shape[0], :group]
    qvs = pick(jnp.where(head == row, small[7:8], 0.0), ones)
    heads = qv_ref.shape[1]
    for i in range(2):
        qv_ref[i] = qvs[i * heads : (i + 1) * heads, :group]


def input_back_kernel(p0, p1, p2, p3, da_ref, w0, w1, w2, w3, y0, y1, y2, y3, w_ref, sems):
    step = pl.program_id(0)
    y_refs, p_refs = (y0, y1, y2, y3), (p0, p1, p2, p3)
    wide = p0.shape[1]

    def body(ready):
        dx = da_ref[...].astype(F32)
        if ready:
            for j, p in enumerate(p_refs):
                ready(j)
                dx = dx + nt(p[...], w_ref[:, j * wide : (j + 1) * wide])
        else:
            dx = dx + nt(jnp.concatenate([p[...] for p in p_refs], axis=1), w_ref[...])
        low = dx.astype(BF)
        size = y_refs[0].shape[1]
        here = low.shape[0] // size
        for j, ref in enumerate(y_refs):

            @pl.when(lax.rem(step, 4 // here) == j // here)
            def _():
                ref[0] = low[(j % here) * size : (j % here + 1) * size]

    groups = []
    for j, w in enumerate((w0, w1, w2, w3)):
        groups.append([pltpu.make_async_copy(w, w_ref.at[:, j * wide : (j + 1) * wide], sems.at[j])])
    fetch(groups, step, body)


def make(mesh):
    nd, ntens = mesh.shape["dp"], mesh.shape["tensor"]
    nh = nd // 2
    groups = [[2 * z + b for z in range(nh)] for b in range(2)]

    def across(array, axis, bit):
        size = nd if axis == "dp" else ntens
        return lax.ppermute(array, axis, [(i, i ^ bit) for i in range(size)])

    def along(array):
        return lax.all_to_all(array, "dp", 0, 0, tiled=True, axis_index_groups=groups)

    def summed(*outs):
        layout, ins, shapes = [], [], []
        for ranges in outs:
            layout.append([len(terms) for terms in ranges])
            columns = 0
            for terms in ranges:
                for array, lead in terms:
                    block = (1,) * len(lead) + (nh // 2,) + array.shape[-2:]
                    ins.append((array, block, lambda z, lead=lead: (*lead, z, 0, 0)))
                columns += array.shape[-1]
            shape = (nh, array.shape[-2], columns)
            shapes.append((shape, BF, (nh // 2,) + shape[1:], lambda z: (z, 0, 0)))
        return call(functools.partial(add_kernel, layout), (2,), ins, shapes, limit=63, cost=60.0)

    def turn(array, k):
        return lax.ppermute(array, "dp", [(2 * ((z + k) % nh) + b, 2 * z + b) for z in range(nh) for b in range(2)])

    def swap(array):
        return across(array, "tensor", 1)

    def settle(array):
        return jnp.sum(array.astype(F32), axis=0)

    def shards(
        tokens, w_qkv, b_qv, w_out, w_up, b_up, w_down, ln_gains, shifts, lengths, segments, pair_ids, targets
    ):
        part_len, row_count, width = tokens.shape
        rb = w_up.shape[0]
        hidden = w_up.shape[1]
        local = w_qkv.shape[2]
        hb = b_up.shape[1]
        hd = hb * nd
        heads = local // hd
        seq = segments.shape[1]
        rows = row_count // ntens
        count = rows * seq
        sents = rows * SEGS
        blk = 256
        steps = count // blk
        t = lax.axis_index("tensor")
        d = lax.axis_index("dp")
        fused = rb % 16 == 0
        depth, rbk = (nh, rb) if fused else (1, width // 2)
        lo_bit = (d % 2 if fused else d * 0).astype(jnp.int32)
        turned_by = (d // 2 if nh <= 4 else d * 0).astype(jnp.int32)
        here, here_first = jnp.stack([lo_bit, lo_bit * 0]), jnp.stack([lo_bit, turned_by])
        t_arr = t.astype(jnp.int32).reshape(1)

        def ready(own, other):
            if fused:
                return [own, other]
            first = jnp.where(d % 2 == 0, own, other)
            second = jnp.where(d % 2 == 0, other, own)
            full = jnp.stack([first, second], axis=1).reshape(2, 1, width // 2, own.shape[2])
            return [full[0], full[1]]

        def merged(own, other, place, after):
            if not fused:
                first = jnp.where(d % 2 == 0, own, other)
                second = jnp.where(d % 2 == 0, other, own)
                return jnp.stack([first, second], axis=1).reshape(width, own.shape[2])
            return call(
                merge_kernel,
                (1,),
                [(place, None, None), (own, None, None), (other, None, None)],
                [((width, own.shape[2]), BF, None, None)],
                scalars=1,
                after=after,
            )[0]

        def weights(pairs):
            return [(a, "any", None) for pair in pairs for a in ready(*pair)]

        def sems(n):
            return pltpu.SemaphoreType.DMA((n,))

        def pack(kernel, arrays, columns, after):
            return call(
                kernel,
                (nh,),
                [(a, None, None) for a in arrays],
                [((nh, rb, columns), BF, (1, rb, columns), lambda i: (i, 0, 0))],
                after=after,
            )[0]

        def cut(array):
            if fused:
                return array
            lead = array.shape[:-4]
            full = array.reshape(*lead, nh, 2, rb, array.shape[-1])
            first, second = full[..., 0, :, :], full[..., 1, :, :]
            return jnp.stack(
                [jnp.where(d % 2 == 0, first, second), jnp.where(d % 2 == 0, second, first)], axis=len(lead)
            )

        def uncut(array):
            if fused:
                return array
            mine, theirs = array[..., 0, :, :, :], array[..., 1, :, :, :]
            first, second = jnp.where(d % 2 == 0, mine, theirs), jnp.where(d % 2 == 0, theirs, mine)
            return jnp.stack([first, second], axis=-3).reshape(*array.shape[:-4], 2, 1, width // 2, array.shape[-1])

        deal_size = min(512, part_len * row_count)
        deal_block = deal_size // row_count
        dealt = call(
            deal_kernel,
            (part_len // deal_block,),
            [(t_arr, None, None), (tokens.reshape(part_len * row_count, width), (deal_size, width), lambda i, *_: (i, 0))],
            [((rows, part_len, width), BF, (rows, deal_block, width), lambda i, *_: (0, i, 0))] * ntens,
            scalars=1,
            cost=2.0,
        )
        x_parts = [dealt[0]] + [across(dealt[j], "tensor", j) for j in range(1, ntens)]

        mine = lax.dynamic_slice_in_dim(segments, t * rows, rows, 0).reshape(rows, ntens, part_len)
        own_len = lax.dynamic_slice_in_dim(lengths, t * rows, rows, 0)
        seg = jnp.stack([lax.dynamic_index_in_dim(mine, t ^ j, 1, False) for j in range(ntens)], axis=1)
        place = jnp.stack([(t ^ j) * part_len + jnp.arange(part_len) for j in range(ntens)])
        live = (place[None] < own_len[:, None, None]).reshape(rows, seq)
        seg = seg.reshape(rows, seq)
        key_code = jnp.where(live, seg, -1)
        classes = jnp.arange(hd)
        query_features = (jnp.where(live, seg, SEGS)[:, :, None] == classes).astype(BF)
        open_key = live[:, :, None] & ((seg[:, :, None] == classes) | (classes == SEGS))
        key_features = jnp.where(open_key | (classes > SEGS), 0.0, NEG).astype(BF)
        sent_code = jnp.where(live, seg + SEGS * jnp.arange(rows)[:, None], -1).reshape(1, count)
        member = (key_code[:, None, :] == jnp.arange(SEGS)[None, :, None]).astype(F32)
        inv_count = (1.0 / jnp.sum(member, axis=2)).reshape(sents, 1)
        own_ids = (d * row_count + t * rows) * SEGS + jnp.arange(sents, dtype=jnp.int32)
        is_mine = pair_ids[None, :] == own_ids[:, None]
        mates = pair_ids.reshape(-1, 2)[:, ::-1].reshape(-1)
        mate = jnp.sum(jnp.where(is_mine, mates[None, :], 0), axis=1, keepdims=True)
        goal = jnp.sum(jnp.where(is_mine, jnp.repeat(targets, 2)[None, :], 0.0), axis=1, keepdims=True)
        own_ids = own_ids[:, None]

        qv_col = jnp.pad(b_qv.reshape(-1, 1), ((0, rb - b_qv.size), (0, 63)))
        wide = 3 * local + 64
        (first_piece,) = call(
            pack_one_kernel,
            (1,),
            [(w_qkv.reshape(rb, 3 * local), None, None), (qv_col, None, None)],
            [((rb, wide), BF, None, None)],
        )
        if nh <= 4:
            pieces1 = [first_piece] + [turn(first_piece, k) for k in range(1, nh)]
            own1 = call(
                stack_kernel,
                (1,),
                [(p, None, None) for p in pieces1],
                [((nh, rb, wide), BF, None, None)],
                after=[dealt[1]],
            )[0]
        else:
            own1 = along(jnp.broadcast_to(first_piece[None], (nh, rb, wide)))
        lo1 = across(own1, "dp", 1)
        w1 = {0: merged(own1, lo1, here_first, [key_features, query_features])}
        w1[1] = swap(w1[0])
        w1[2] = across(w1[0], "tensor", 2)
        extra = jnp.concatenate([ln_gains.T, shifts.T, b_up.reshape(-1, 1), jnp.zeros((rb, 57), BF)], axis=1)
        second_piece = pack(pack_two_kernel, [w_up, w_out, extra], hidden + 256, [dealt[1]])
        (second_piece,) = gate([second_piece], [own1])
        own2 = along(second_piece)
        third_piece = pack(pack_three_kernel, [w_down], hidden, [dealt[1]])

        k = np.arange(width)
        dd, within = k // rb, k % rb
        up_at = (within // hb) * hd + dd * hb + within % hb
        sup = np.zeros((width, width), np.float32)
        sup[k, up_at] = 1.0
        qv = within < 2 * heads * hb
        qv_at = (within // (heads * hb)) * local + ((within // hb) % heads) * hd + dd * hb + within % hb
        sqv = np.zeros((width, 2 * local), np.float32)
        sqv[k[qv], qv_at[qv]] = 1.0
        sup, sqv = jnp.asarray(sup, BF), jnp.asarray(sqv, BF)

        def whole(array):
            return (array, None, None)

        def whole_out(shape, dtype):
            return (shape, dtype, None, None)

        by_row = lambda r, *_: (r, 0, 0)

        def attend(xs, w, before, cost=9.0):
            outs = [
                ((rows, seq, 3 * local), BF, (1, seq, 3 * local), by_row),
                ((rows, heads, seq, seq), BF, (1, heads, seq, seq), lambda r, *_: (r, 0, 0, 0)),
                ((rows, seq, 256), BF, (1, seq, 256), by_row),
            ]
            if len(xs) > 1:
                outs.append(((rows, seq, width), BF, (1, seq, width), by_row))
            return call(
                functools.partial(attn_fwd_kernel, len(xs)),
                (rows,),
                [(a, (1,) + a.shape[1:], by_row) for a in xs]
                + [
                    whole(w),
                    whole(sqv),
                    (key_features, (1, seq, hd), by_row),
                    (query_features, (1, seq, hd), by_row),
                ],
                outs,
                scratch=[pltpu.VMEM((8, 2 * local), F32)],
                after=before,
                limit=63,
                cost=cost,
            )

        kept = {}
        *kept[0], x = attend(x_parts, w1[0], [second_piece], 25.0)
        (own2,) = gate([own2], [kept[0][2]])
        lo2, far2 = across(own2, "dp", 1), across(own2, "tensor", 2)
        (third_piece,) = gate([third_piece], [own2])
        own3 = along(third_piece)
        kept[1] = attend([x], w1[1], [own2])
        w1[2], lo2 = gate([w1[2], lo2], [kept[1][2]])
        w1[3] = swap(w1[2])
        far_lo2 = across(lo2, "tensor", 2)
        kept[2] = attend([x], w1[2], [lo2])
        own3, far2 = gate([own3, far2], [kept[2][2]])
        lo3, far3 = across(own3, "dp", 1), across(own3, "tensor", 2)
        kept[3] = attend([x], w1[3], [own3, far2])
        far_lo2, lo3 = gate([far_lo2, lo3], [kept[3][2]])
        far_lo3 = across(lo3, "tensor", 2)
        w2 = [(own2, lo2), (swap(own2), swap(lo2)), (far2, far_lo2), (swap(far2), swap(far_lo2))]
        o_parts = [kept[j][2].reshape(count, 256) for j in range(4)]
        x_flat = x.reshape(count, width)

        def rows_of(array):
            return (array, (blk, array.shape[1]), lambda i, *_: (i, 0))

        def rows_out(shape, dtype):
            return (shape, dtype, (blk, shape[1]), lambda i, *_: (i, 0))

        all_w, all_o = pltpu.VMEM((width, 4 * hidden), BF), pltpu.VMEM((width, 4 * 256), BF)
        xh1, rstd1, u, h, g, small = call(
            middle_kernel,
            (steps,),
            [whole(here)] + [rows_of(o) for o in o_parts] + [rows_of(x_flat), whole(sup)] + weights(w2),
            [
                rows_out((count, width), BF),
                rows_out((count, 1), F32),
                rows_out((count, width), BF),
                rows_out((count, 4 * hidden), BF),
                rows_out((count, 4 * hidden), BF),
                whole_out((8, width), F32),
            ],
            scratch=[all_o, all_w, pltpu.VMEM((8, 4 * hidden), F32), sems(16 * depth)],
            scalars=1,
            after=[lo3],
            limit=63,
            cost=20.0,
        )
        far3, far_lo3 = gate([far3, far_lo3], [u])
        w3 = [(own3, lo3), (swap(own3), swap(lo3)), (far3, far_lo3), (swap(far3), swap(far_lo3))]
        code_spec = (sent_code, (1, blk), lambda i, *_: (0, i))
        span = blk // part_len
        part_out = lambda i, *_: (i * span // ntens, 0, 0)
        xh2, rstd2, y0, y1, y2, y3, pooled = call(
            down_kernel,
            (steps,),
            [whole(here), rows_of(h), rows_of(u), whole(small), code_spec, whole(inv_count)] + weights(w3),
            [rows_out((count, width), BF), rows_out((count, 1), F32)]
            + [((rows, part_len, width), BF, (1, part_len, width), part_out)] * ntens
            + [whole_out((nd * ntens, sents, width), BF)],
            scratch=[pltpu.VMEM((sents, width), F32), all_w, sems(8 * depth)],
            scalars=1,
            limit=63,
            cost=14.0,
        )

        def send_back(parts):
            return [parts[0]] + [across(parts[j], "tensor", j) for j in range(1, ntens)]

        def collected(parts, after=()):
            (out,) = call(
                collect_kernel,
                (part_len // deal_block,),
                [whole(t_arr)] + [(a, (rows, deal_block, width), lambda i, *_: (0, i, 0)) for a in parts],
                [((part_len * row_count, width), BF, (deal_size, width), lambda i, *_: (i, 0))],
                scalars=1,
                after=after,
                limit=63,
                cost=30.0,
            )
            return out.reshape(part_len, row_count, width)

        every = lax.all_to_all(pooled, ("dp", "tensor"), 0, 0, tiled=True).reshape(nd * ntens * sents, width)

        shape = (2, 2, depth, rbk, hidden)
        half = (2,) + shape[2:]

        def blocked(array):
            return (blk, array.shape[1]), lambda i, *_: (jnp.minimum(i, steps - 1), 0)

        def blocked_out(shape, dtype):
            return (shape, dtype, *blocked(jax.ShapeDtypeStruct(shape, dtype)))

        late = lambda i: jnp.maximum(i - steps, 0)
        df, de, send3, sums2, dbup = call(
            functools.partial(feed_back_kernel, steps),
            (steps + 2,),
            [whole(here), whole(every), whole(own_ids), whole(mate), whole(goal), whole(inv_count)]
            + [(sent_code, (1, blk), lambda i, *_: (0, jnp.minimum(i, steps - 1)))]
            + [(a, *blocked(a)) for a in (xh2, rstd2)]
            + [whole(small), (g, *blocked(g))]
            + [(h, (count, hidden), lambda i, *_: (0, 2 * late(i) + 1))]
            + weights(w3),
            [
                blocked_out((count, width), BF),
                blocked_out((count, 4 * hidden), BF),
                (shape, BF, (1,) + shape[1:], lambda i, *_: (late(i), 0, 0, 0, 0)),
                whole_out((8, width), F32),
                whole_out((8, 4 * hidden), F32),
            ],
            scratch=[pltpu.VMEM((3, sents, width), BF), pltpu.VMEM((count, width), BF), all_w, sems(8 * depth)],
            scalars=1,
            limit=63,
            cost=32.0,
        )

        hidden_parts = send_back([y0, y1, y2, y3])

        def grad_part(a, b, odd, kernel, got, outs, after):
            return call(
                kernel,
                (2,),
                [whole(here), whole(a), (b, (count, hidden), lambda j, *_: (0, 2 * j + odd))]
                + [(v, (1,) + v.shape[1:], lambda j, *_: (j, 0, 0, 0, 0)) for v in got],
                outs,
                scalars=1,
                after=after,
                limit=63,
                cost=40.0,
            )

        both_out = [(shape, BF, (1,) + shape[1:], lambda j, *_: (j, 0, 0, 0, 0))]
        hidden_out = collected(hidden_parts, [send3])
        (sendu,) = grad_part(u, de, 1, grad_send_kernel, [], both_out, [send3, hidden_out])
        got = uncut(swap(cut(send3)))
        stay3, fly3 = grad_part(
            df, h, 0, functools.partial(grad_keep_kernel, True), [got],
            [(half, BF, (1,) + half[1:], lambda j, *_: (j, 0, 0, 0))] * 2, [sendu],
        )
        if not fused:
            both = cut(jnp.stack([stay3, fly3], axis=1))
            stay3, fly3 = both[:, 0], both[:, 1]
        got = uncut(swap(cut(sendu)))
        stayu, flyu = grad_part(
            u, de, 0, functools.partial(grad_keep_kernel, False), [got], [whole_out(half, BF)] * 2, [fly3]
        )
        stayu, flyu = cut(stayu), cut(flyu)
        got3x = across(fly3, "dp", 1)
        gotuy = across(flyu, "tensor", 2)

        da, do, sums1 = call(
            norm_back_kernel,
            (steps,),
            [whole(here), rows_of(de), rows_of(df), rows_of(xh1), rows_of(rstd1), whole(small)] + weights(w2),
            [
                rows_out((count, width), BF),
                rows_out((count, 4 * 256), BF),
                whole_out((8, width), F32),
            ],
            scratch=[all_w, all_o, sems(16 * depth)],
            scalars=1,
            after=[flyu],
            limit=63,
            cost=14.0,
        )
        da_rows, do_rows = da.reshape(rows, seq, width), do.reshape(rows, seq, 4 * 256)
        grad_cols = 4 * local

        def attend_back(j, got, after):
            qkv, p, o = kept[j]
            half = (depth, rbk, grad_cols)
            kinds = [whole_out((2,) + half, BF)] if got is None else [whole_out(half, BF)] * 2
            keeps = 0 if got is None else 1
            whole_row = pltpu.VMEM((rows, seq, width), BF)
            *outs, sums, dproj = call(
                functools.partial(attn_bwd_kernel, keeps),
                (rows,),
                [
                    whole(here),
                    (qkv, (1, seq, 3 * local), by_row),
                    (p, (1, heads, seq, seq), lambda r, *_: (r, 0, 0, 0)),
                    (o, (1, seq, 256), by_row),
                    (do_rows, (1, seq, 256), lambda r, *_: (r, 0, j)),
                    (x, "any", None),
                    (da_rows, "any", None),
                ]
                + ([] if got is None else [(uncut(got), "any", None)]),
                kinds
                + [whole_out((8, 3 * local), F32), ((rows, seq, wide), BF, (1, seq, wide), by_row)],
                scratch=[pltpu.VMEM((width, grad_cols), F32), whole_row, whole_row, sems(2 * rows + keeps)]
                + [pltpu.VMEM((2,) + half, BF)] * keeps,
                scalars=1,
                after=after,
                limit=63,
                cost=11.0,
            )
            if got is None:
                out = cut(outs[0])
            elif fused:
                out = tuple(outs)
            else:
                both = cut(jnp.stack(outs))
                out = both[0], both[1]
            sums_of[j], dprojs[j] = sums, dproj.reshape(count, wide)
            return out

        sums_of, dprojs = {}, {}
        back3 = attend_back(3, None, [flyu])
        got_far = swap(back3)
        got3x, gotuy = gate([got3x, gotuy], [back3])
        turn3, turnu = summed([[(stay3, (1,)), (got3x, (1,))]], [[(stayu, (1,)), (gotuy, (1,))]])
        got3y, gotux = across(turn3, "tensor", 2), across(turnu, "dp", 1)
        stay_far, fly_far = attend_back(2, got_far, [turn3, turnu])
        got_fly = across(fly_far, "dp", 1)
        small_keep, small_send = call(
            small_kernel,
            (1,),
            [whole(a) for a in (sums1, sums2, dbup, sums_of[2], sums_of[3])],
            [whole_out((24, width), F32)] * 2,
            limit=63,
            after=[stay_far],
        )
        small_keep = small_keep + swap(small_send)
        small_got = across(jnp.concatenate([small_keep[:8], small_keep[16:]], axis=0), "tensor", 2)
        got3y, gotux = gate([got3y, gotux], [small_keep])
        (end,) = summed([[(stay3, (0,)), (got3x, (0,)), (got3y, ())], [(stayu, (0,)), (gotuy, (0,)), (gotux, ())]])
        end_sent = end
        end = along(end)
        back1 = attend_back(1, None, [end_sent])
        got_near = swap(back1)
        got_sums = swap(sums_of[1])
        (got_fly,) = gate([got_fly], [back1])
        (turn1,) = summed([[(stay_far, ()), (got_fly, ())]])
        got_turn1 = across(turn1, "tensor", 2)
        stay_near, fly_near = attend_back(0, got_near, [turn1])
        got1 = across(fly_near, "dp", 1)
        span_out = lambda i, *_: (i * span // ntens, 0, 0)
        dx_parts = call(
            input_back_kernel,
            (steps,),
            [rows_of(dprojs[j]) for j in range(4)] + [rows_of(da)] + [(w1[j], "any", None) for j in range(4)],
            [((rows, part_len, width), BF, (1, part_len, width), span_out)] * ntens,
            scratch=[pltpu.VMEM((width, 4 * wide), BF), sems(4)],
            limit=63,
            after=[stay_near],
            cost=8.0,
        )
        token_parts = send_back(dx_parts)

        got1, got_turn1, end = gate([got1, got_turn1, end], [dx_parts[0]])
        near_sums = sums_of[0] + got_sums
        near_sums = jnp.concatenate([near_sums[:1, :local], near_sums[:1, 2 * local :]], axis=1)
        own = small_keep[:16] + small_got + jnp.pad(near_sums, ((9, 6), (0, width - 2 * local)))
        got = across(own, "dp", 1)
        if fused and nh <= 4:
            last = call(
                last_kernel,
                (1,),
                [whole(here_first)] + [whole(v) for v in (stay_near, got1, got_turn1, own, got)],
                [whole_out((rb + 16, width), BF)] * nh,
                scalars=1,
                after=[token_parts[1]],
                limit=63,
                cost=60.0,
            )
            last_sent = last[0]
            mine = width // (nd * ntens)
            at = jnp.stack([(d * ntens + t) * mine, d * hb]).astype(jnp.int32)
            grad_qkv, grad_out, grad_gains, grad_shifts, grad_b_up, grad_b_qv = call(
                final_kernel,
                (1,),
                [whole(at)] + [whole(v) for v in [last[0]] + [turn(last[k], nh - k) for k in range(1, nh)]],
                [
                    whole_out((rb, 3, local), F32),
                    whole_out((local, rb), F32),
                    whole_out((2, mine), F32),
                    whole_out((4, mine), F32),
                    whole_out((hidden // hd, hb), F32),
                    whole_out((2, heads, hb), F32),
                ],
                scalars=1,
                limit=32,
            )
        else:
            (last_sent,) = summed([[(stay_near, ()), (got1, ()), (got_turn1, ())]])
            small = jnp.broadcast_to(split_small(own + got)[None], (nh, 16, width))
            total = settle(along(jnp.concatenate([last_sent, small], axis=1)))
            grad_qkv, grad_out = total[:rb, : 3 * local].reshape(rb, 3, local), total[:rb, 3 * local :].T
            small = total[rb : rb + 8] + total[rb + 8 :]
            rest = lax.dynamic_slice_in_dim(small[:6], (d * ntens + t) * (width // (nd * ntens)), width // (nd * ntens), 1)
            grad_b_up = lax.dynamic_slice_in_dim(small[6].reshape(hidden // hd, hd), d * hb, hb, 1)
            grad_b_qv = lax.dynamic_slice_in_dim(small[7, : 2 * local].reshape(2, heads, hd), d * hb, hb, 2)
            grad_gains, grad_shifts = rest[:2], rest[2:]
        grad_tokens = collected(token_parts, [last_sent])
        end = settle(end)
        grad_down, grad_up = end[:, :hidden], end[:, hidden:]
        return (
            hidden_out,
            grad_tokens,
            grad_qkv,
            grad_b_qv,
            grad_out,
            grad_up,
            grad_b_up,
            grad_down.T,
            grad_gains,
            grad_shifts,
        )

    return shards


def solution(mesh):
    return jax.shard_map(
        make(mesh),
        mesh=mesh,
        in_specs=(
            P("tensor", "dp", None),
            P("dp", None, "tensor"),
            P(None, "tensor", "dp"),
            P("tensor", "dp"),
            P("dp", "tensor"),
            P("tensor", "dp"),
            P("tensor", "dp"),
            P(None, "dp"),
            P(None, "dp"),
            P("dp"),
            P("dp", None),
            P(),
            P(),
        ),
        out_specs=(
            P("tensor", "dp", None),
            P("tensor", "dp", None),
            P("dp", None, "tensor"),
            P(None, "tensor", "dp"),
            P("tensor", "dp"),
            P("dp", "tensor"),
            P("tensor", "dp"),
            P("tensor", "dp"),
            P(None, ("dp", "tensor")),
            P(None, ("dp", "tensor")),
        ),
        check_vma=False,
    )
```

```python
import functools
import math

import jax
import jax.numpy as jnp
import numpy as np
from jax import lax
from jax.experimental import pallas as pl
from jax.experimental.pallas import tpu as pltpu
from jax.sharding import PartitionSpec as P

SEGS = 4
EPS_NORM = 1e-05
EPS_COS = 1e-06
LOSS_SCALE = 4096.0
NEG = -1e30

BF = jnp.bfloat16
F32 = jnp.float32
MIB = 1024 * 1024
SHARE = 0.2


def dot(a, b, ca, cb):
    return lax.dot_general(a, b, (((ca,), (cb,)), ((), ())), preferred_element_type=F32)


def nn(a, b):
    return dot(a, b, 1, 0)


def nt(a, b):
    return dot(a, b, 1, 1)


def tn(a, b):
    return dot(a, b, 0, 0)


def call(kernel, grid, ins, outs, scratch=(), cost=1.0, scalars=0, limit=16, after=()):
    def spec(shape, block, index):
        if isinstance(block, str):
            return pl.BlockSpec(memory_space=pl.ANY)
        if block is None:
            zeros = (0,) * len(shape)
            return pl.BlockSpec(shape, lambda *_: zeros)
        return pl.BlockSpec(block, index)

    in_specs = [spec(a.shape, b, m) for a, b, m in ins[scalars:]]
    out_specs = [spec(s, b, m) for s, _, b, m in outs]
    flops = int(cost * SHARE * 1.15e9)
    body, known = kernel, len(ins)
    if after:
        in_specs += [pl.BlockSpec(memory_space=pl.ANY)] * len(after)

        def body(*refs):
            return kernel(*refs[:known], *refs[known + len(after) :])

    return pl.pallas_call(
        body,
        grid_spec=pltpu.PrefetchScalarGridSpec(
            num_scalar_prefetch=scalars,
            grid=grid,
            in_specs=in_specs,
            out_specs=out_specs,
            scratch_shapes=list(scratch),
        ),
        out_shape=[jax.ShapeDtypeStruct(s, d) for s, d, _, _ in outs],
        compiler_params=pltpu.CompilerParams(
            dimension_semantics=("arbitrary",) * len(grid), vmem_limit_bytes=limit * MIB
        ),
        cost_estimate=pl.CostEstimate(flops=flops, bytes_accessed=1024, transcendentals=0),
    )(*[a for a, _, _ in ins], *after)


def gate(arrays, after):
    n = len(arrays)
    anywhere = pl.BlockSpec(memory_space=pl.ANY)
    return pl.pallas_call(
        lambda *refs: None,
        in_specs=[anywhere] * (n + len(after)),
        out_specs=[anywhere] * n,
        out_shape=[jax.ShapeDtypeStruct(a.shape, a.dtype) for a in arrays],
        input_output_aliases={i: i for i in range(n)},
        cost_estimate=pl.CostEstimate(flops=1, bytes_accessed=1, transcendentals=0),
    )(*arrays, *after)


def deal_kernel(t_ref, tok_ref, *out_refs):
    size = tok_ref.shape[0]
    parts = len(out_refs)
    rows, block = out_refs[0].shape[0], out_refs[0].shape[1]
    t = t_ref[0]
    m = lax.broadcasted_iota(jnp.int32, (size, size), 0)
    n = lax.broadcasted_iota(jnp.int32, (size, size), 1)
    part, row, place = m // (rows * block), (m // block) % rows, m % block
    source = place * (parts * rows) + jnp.bitwise_xor(part, t) * rows + row
    pick = jnp.where(source == n, 1.0, 0.0).astype(BF)
    moved = nn(pick, tok_ref[...]).astype(BF)
    for j, out in enumerate(out_refs):
        for r in range(rows):
            at = (j * rows + r) * block
            out[r] = moved[at : at + block]


def collect_kernel(t_ref, *refs):
    *in_refs, out_ref = refs
    size = out_ref.shape[0]
    parts = len(in_refs)
    rows, block = in_refs[0].shape[0], in_refs[0].shape[1]
    t = t_ref[0]
    m = lax.broadcasted_iota(jnp.int32, (size, size), 1)
    n = lax.broadcasted_iota(jnp.int32, (size, size), 0)
    part, row, place = m // (rows * block), (m // block) % rows, m % block
    target = place * (parts * rows) + jnp.bitwise_xor(part, t) * rows + row
    pick = jnp.where(target == n, 1.0, 0.0).astype(BF)
    joined = jnp.concatenate([ref[r] for ref in in_refs for r in range(rows)], axis=0)
    out_ref[...] = nn(pick, joined).astype(BF)


def stack_kernel(*refs):
    *ins, out_ref = refs
    for i, ref in enumerate(ins):
        out_ref[i] = ref[...]


def add_kernel(layout, *refs):
    ins, outs = list(refs[: sum(map(sum, layout))]), refs[sum(map(sum, layout)) :]
    for terms, out_ref in zip(layout, outs):
        at = 0
        for n in terms:
            value = 0.0
            for ref in [ins.pop(0) for _ in range(n)]:
                value = value + ref[...].astype(F32).reshape(out_ref.shape[:2] + ref.shape[-1:])
            columns = value.shape[-1]
            out_ref[:, :, at : at + columns] = value.astype(BF)
            at += columns


def merge_kernel(here_ref, own_ref, other_ref, out_ref):
    depth, rows = own_ref.shape[0], own_ref.shape[1]
    lo = here_ref[0]
    for z in range(depth):
        at = lax.rem(z + depth - here_ref[1], depth)
        mine, theirs = own_ref[at], other_ref[at]
        for b in range(2):
            at = (2 * z + b) * rows
            out_ref[at : at + rows, :] = jnp.where(lo == b, mine, theirs)


def weight_copies(pairs, here_ref, columns, dest, sems, first=0):
    groups = []
    n = first
    for j, (own, other) in enumerate(pairs):
        depth, rows = own.shape[0], own.shape[1]
        size = columns.stop - columns.start
        group = []
        for z in range(depth):
            src = lax.rem(z + depth - here_ref[1], depth)
            for ref, b in ((own, here_ref[0]), (other, 1 - here_ref[0])):
                to = dest.at[pl.ds(pl.multiple_of((2 * z + b) * rows, rows), rows), j * size : (j + 1) * size]
                group.append(pltpu.make_async_copy(ref.at[src, :, columns], to, sems.at[n]))
                n += 1
        groups.append(group)
    return groups


def paired(refs):
    return list(zip(refs[::2], refs[1::2]))


def attn_fwd_kernel(parts, *refs):
    x_refs, refs = refs[:parts], refs[parts:]
    w_ref, sqv_ref, kf_ref, qf_ref, qkv_ref, p_ref, o_ref, *refs = refs
    *x_out, bias_ref = refs
    local = qkv_ref.shape[2] // 3
    heads = p_ref.shape[1]
    hd = local // heads

    @pl.when(pl.program_id(0) == 0)
    def _():
        bias_ref[...] = tn(w_ref[:, 3 * local :][:, :8], sqv_ref[...])

    x = x_refs[0][0]
    if parts > 1:
        x = jnp.concatenate([ref[0] for ref in x_refs], axis=0)
        x_out[0][0] = x
    projected = nn(x, w_ref[:, : 3 * local])
    q_all = ((projected[:, :local] + bias_ref[0:1, :local]) * 0.125).astype(BF)
    k_all = projected[:, local : 2 * local].astype(BF)
    v_all = (projected[:, 2 * local :] + bias_ref[0:1, local:]).astype(BF)
    qkv_ref[0, :, :local] = q_all
    qkv_ref[0, :, local : 2 * local] = k_all
    qkv_ref[0, :, 2 * local :] = v_all
    outs = []
    for h in range(heads):
        at = slice(h * hd, (h + 1) * hd)
        q = jnp.concatenate([q_all[:, at], qf_ref[0]], axis=1)
        k = jnp.concatenate([k_all[:, at], kf_ref[0]], axis=1)
        s = nt(q, k)
        top = jnp.max(s, axis=-1, keepdims=True)
        e = jnp.exp(s - top)
        total = jnp.sum(e, axis=-1, keepdims=True)
        p = (e * (1.0 / total)).astype(BF)
        p_ref[0, h] = p
        outs.append(nn(p, v_all[:, at]).astype(BF))
    pad = jnp.zeros((outs[0].shape[0], o_ref.shape[2] - local), BF)
    o_ref[0] = jnp.concatenate(outs + [pad], axis=1)


def norm(z):
    centred = z - jnp.mean(z, axis=-1, keepdims=True)
    rstd = lax.rsqrt(jnp.mean(centred * centred, axis=-1, keepdims=True) + EPS_NORM)
    return centred * rstd, rstd


def norm_back(dy, xh, rstd, gain):
    dxh = dy * gain
    mean = jnp.mean(dxh, axis=-1, keepdims=True)
    proj = jnp.mean(dxh * xh, axis=-1, keepdims=True)
    return rstd * (dxh - mean - xh * proj)


def turned(a):
    rows = a.shape[1]
    eye = (
        lax.broadcasted_iota(jnp.int32, (rows, rows), 0) == lax.broadcasted_iota(jnp.int32, (rows, rows), 1)
    ).astype(BF)
    return nt(eye, a).astype(BF)


def pack_one_kernel(w_ref, extra_ref, piece_ref):
    piece_ref[...] = jnp.concatenate([w_ref[...], extra_ref[...]], axis=1)


def pack_two_kernel(up_ref, out_ref, extra_ref, piece_ref):
    hidden = up_ref.shape[1]
    piece_ref[0, :, :hidden] = up_ref[...]
    piece_ref[0, :, hidden:] = jnp.concatenate([turned(out_ref[...]), extra_ref[...]], axis=1)


def pack_three_kernel(a_ref, piece_ref):
    piece_ref[0] = turned(a_ref[...])


def gelu_parts(e):
    cdf = 0.5 + 0.5 * lax.erf(e * (1.0 / math.sqrt(2.0)))
    return e * cdf, cdf + e * (jnp.exp(-0.5 * e * e) * (1.0 / math.sqrt(2.0 * math.pi)))


def fetch(groups, step, body):
    @pl.when(step == 0)
    def _():
        for group in groups:
            for copy in group:
                copy.start()

        def ready(i):
            for copy in groups[i]:
                copy.wait()

        body(ready)

    @pl.when(step > 0)
    def _():
        body(None)


def middle_kernel(here_ref, o0, o1, o2, o3, x_ref, sup_ref, *refs):
    ws, refs = paired(refs[:8]), refs[8:]
    xh_ref, rstd_ref, u_ref, h_ref, g_ref, small_ref, wo_ref, wu_ref, bup_ref, sems = refs
    width = x_ref.shape[1]
    hidden = wu_ref.shape[1] // 4
    wide = wo_ref.shape[1] // 4
    per = 2 * ws[0][0].shape[0]
    groups = weight_copies(ws, here_ref, slice(hidden, hidden + wide), wo_ref, sems)
    groups += weight_copies(ws, here_ref, slice(0, hidden), wu_ref, sems, 4 * per)

    def body(ready):
        if ready:
            for j in range(4):
                ready(j)
            eye = (
                lax.broadcasted_iota(jnp.int32, (width, width), 0)
                == lax.broadcasted_iota(jnp.int32, (width, width), 1)
            ).astype(BF)
            local = wide - 64
            small_ref[...] = tn(wo_ref[:, local:wide][:, :8], eye)
            cols = [wo_ref[:, j * wide + local : (j + 1) * wide][:, :8] for j in range(4)]
            rows = tn(jnp.concatenate(cols, axis=1), sup_ref[...])
            for j in range(4):
                bup_ref[:, j * hidden : (j + 1) * hidden] = rows[8 * j : 8 * j + 8]
        o = jnp.concatenate([o0[...], o1[...], o2[...], o3[...]], axis=1)
        z = x_ref[...].astype(F32) + (nt(o, wo_ref[...]) + small_ref[2:3])
        xh, rstd = norm(z)
        xh_ref[...] = xh.astype(BF)
        rstd_ref[...] = rstd
        u = (xh * small_ref[0:1] + small_ref[3:4]).astype(BF)
        u_ref[...] = u
        for j in range(4 if ready else 1):
            at = slice(j * hidden, (j + 1) * hidden) if ready else slice(0, 4 * hidden)
            if ready:
                ready(4 + j)
            h, g = gelu_parts(nn(u, wu_ref[:, at]) + bup_ref[6:7, at])
            h_ref[:, at] = h.astype(BF)
            g_ref[:, at] = g.astype(BF)

    fetch(groups, pl.program_id(0), body)


def split3(v):
    a = v.astype(BF)
    rest = v - a.astype(F32)
    b = rest.astype(BF)
    c = (rest - b.astype(F32)).astype(BF)
    return a, b, c


def down_kernel(here_ref, h_ref, u_ref, small_ref, code_ref, inv_ref, *refs):
    ws, refs = paired(refs[:8]), refs[8:]
    xh_ref, rstd_ref, y0, y1, y2, y3, pool_ref, acc_ref, w_ref, sems = refs
    y_refs = (y0, y1, y2, y3)
    step = pl.program_id(0)
    hidden = w_ref.shape[1] // 4

    @pl.when(step == 0)
    def _():
        acc_ref[...] = jnp.zeros_like(acc_ref)

    def body(ready):
        if ready:
            ready(0)
            f = nt(h_ref[:, :hidden], w_ref[:, :hidden])
            for j in range(1, 4):
                ready(j)
                f += nt(h_ref[:, j * hidden : (j + 1) * hidden], w_ref[:, j * hidden : (j + 1) * hidden])
        else:
            f = nt(h_ref[...], w_ref[...])
        xh, rstd = norm(u_ref[...].astype(F32) + (f + small_ref[4:5]))
        y2 = xh * small_ref[1:2] + small_ref[5:6]
        xh_ref[...] = xh.astype(BF)
        rstd_ref[...] = rstd
        low = y2.astype(BF)
        size = y_refs[0].shape[1]
        here = low.shape[0] // size
        for j, ref in enumerate(y_refs):

            @pl.when(lax.rem(step, 4 // here) == j // here)
            def _():
                ref[0] = low[(j % here) * size : (j % here + 1) * size]

        member = (lax.broadcasted_iota(jnp.int32, (8, y2.shape[0]), 0) == code_ref[...]).astype(BF)
        a, b, c = split3(y2)
        acc_ref[...] += nn(member, a) + nn(member, b) + nn(member, c)

    fetch(weight_copies(ws, here_ref, slice(0, hidden), w_ref, sems), step, body)

    @pl.when(step == pl.num_programs(0) - 1)
    def _():
        low = (acc_ref[...] * inv_ref[...]).astype(BF)

        def put(i, carry):
            pool_ref[i] = low
            return carry

        lax.fori_loop(0, pool_ref.shape[0], put, 0)


def loss_grad(pooled_ref, ids_ref, mate_ref, target_ref, inv_ref):
    pooled = pooled_ref[...]
    places = lax.broadcasted_iota(jnp.int32, (8, pooled.shape[0]), 1)
    first = nn((places == ids_ref[...]).astype(BF), pooled)
    second = nn((places == mate_ref[...]).astype(BF), pooled)
    inner = jnp.sum(first * second, axis=-1, keepdims=True)
    ra = lax.rsqrt(jnp.sum(first * first, axis=-1, keepdims=True) + EPS_COS)
    rb = lax.rsqrt(jnp.sum(second * second, axis=-1, keepdims=True) + EPS_COS)
    missed = inner * ra * rb - target_ref[...]
    grad = (2.0 * LOSS_SCALE) * missed * (second * (ra * rb) - first * (inner * rb * ra * ra * ra))
    return grad * inv_ref[...]


def rowsum(v):
    return jnp.sum(v, axis=0, keepdims=True)


def feed_back_kernel(
    blocks, here_ref, pooled_ref, ids_ref, mate_ref, target_ref, inv_ref, code_ref, xh_ref, rstd_ref, small_ref,
    g_ref, h_ref, *refs,
):
    ws, refs = paired(refs[:8]), refs[8:]
    df_ref, de_ref, send_ref, sum_ref, bup_ref, gp_ref, all_ref, w_ref, sems = refs
    hidden = w_ref.shape[1] // 4
    step = pl.program_id(0)

    @pl.when(step == 0)
    def _():
        grad = loss_grad(pooled_ref, ids_ref, mate_ref, target_ref, inv_ref)
        for i, part in enumerate(split3(grad)):
            gp_ref[i] = part
        sum_ref[...] = jnp.zeros_like(sum_ref)
        bup_ref[...] = jnp.zeros_like(bup_ref)

    def body(ready):
        size = xh_ref.shape[0]
        member = (lax.broadcasted_iota(jnp.int32, (8, size), 0) == code_ref[...]).astype(BF)
        dy = tn(member, gp_ref[0]) + tn(member, gp_ref[1]) + tn(member, gp_ref[2])
        xh = xh_ref[...].astype(F32)
        dz = norm_back(dy, xh, rstd_ref[...], small_ref[1:2])
        sum_ref[0:1] += rowsum(dy * xh)
        sum_ref[1:2] += rowsum(dy)
        sum_ref[2:3] += rowsum(dz)
        df = dz.astype(BF)
        df_ref[...] = df
        all_ref[pl.ds(pl.multiple_of(step * size, size), size), :] = df
        for j in range(4 if ready else 1):
            at = slice(j * hidden, (j + 1) * hidden) if ready else slice(0, 4 * hidden)
            if ready:
                ready(j)
            de = (nn(df, w_ref[:, at]) * g_ref[:, at].astype(F32)).astype(BF)
            de_ref[:, at] = de
            bup_ref[0:1, at] += rowsum(de.astype(F32))

    @pl.when(step < blocks)
    def _():
        fetch(weight_copies(ws, here_ref, slice(0, hidden), w_ref, sems), step, body)

    @pl.when(step >= blocks)
    def _():
        pieces(tn(all_ref[...], h_ref[...]), here_ref, send_ref.at[0], slice(0, hidden))


def norm_back_kernel(here_ref, de_ref, df_ref, xh_ref, rstd_ref, small_ref, *refs):
    ws, refs = paired(refs[:8]), refs[8:]
    da_ref, do_ref, sum_ref, w_ref, wo_ref, sems = refs
    step = pl.program_id(0)
    hidden, wide = w_ref.shape[1] // 4, wo_ref.shape[1] // 4
    per = 2 * ws[0][0].shape[0]
    groups = weight_copies(ws, here_ref, slice(0, hidden), w_ref, sems)
    groups += weight_copies(ws, here_ref, slice(hidden, hidden + wide), wo_ref, sems, 4 * per)

    @pl.when(step == 0)
    def _():
        sum_ref[...] = jnp.zeros_like(sum_ref)

    def body(ready):
        dy = df_ref[...].astype(F32)
        for j in range(4 if ready else 1):
            at = slice(j * hidden, (j + 1) * hidden) if ready else slice(0, 4 * hidden)
            if ready:
                ready(j)
            dy = dy + nt(de_ref[:, at], w_ref[:, at])
        xh = xh_ref[...].astype(F32)
        dz = norm_back(dy, xh, rstd_ref[...], small_ref[0:1])
        sum_ref[0:1] += rowsum(dy * xh)
        sum_ref[1:2] += rowsum(dy)
        sum_ref[2:3] += rowsum(dz)
        da = dz.astype(BF)
        da_ref[...] = da
        if ready:
            for j in range(4):
                ready(4 + j)
        do_ref[...] = nn(da, wo_ref[...]).astype(BF)

    fetch(groups, step, body)


def pieces(grad, here_ref, ref, at):
    depth, rows = ref.shape[1], ref.shape[2]
    low = grad.astype(BF)
    for z in range(depth):
        for b in range(2):
            part = low[(2 * z + b) * rows : (2 * z + b + 1) * rows]
            ref[here_ref[0] if b == 0 else 1 - here_ref[0], z, :, at] = part


def grad_send_kernel(here_ref, *refs):
    *ins, send_ref = refs
    at = 0
    for grad in (tn(a[...], b[...]) for a, b in zip(ins[::2], ins[1::2])):
        pieces(grad, here_ref, send_ref.at[0], slice(at, at + grad.shape[1]))
        at += grad.shape[1]


def grad_keep_kernel(by_row, here_ref, *refs):
    *ins, got_ref, stay_ref, fly_ref = refs
    depth, rows = got_ref.shape[2], got_ref.shape[3]
    lo = here_ref[0]
    j = pl.program_id(0)
    at = 0
    for grad in (tn(a[...], b[...]) for a, b in zip(ins[::2], ins[1::2])):
        cols = slice(at, at + grad.shape[1])
        for z in range(depth):
            first, second = (grad[(2 * z + b) * rows : (2 * z + b + 1) * rows] for b in range(2))
            mine, theirs = jnp.where(lo == 0, first, second), jnp.where(lo == 0, second, first)
            mine = (mine + got_ref[0, 0, z, :, cols].astype(F32)).astype(BF)
            theirs = (theirs + got_ref[0, 1, z, :, cols].astype(F32)).astype(BF)
            if by_row:
                stay_ref[0, z, :, cols] = mine
                fly_ref[0, z, :, cols] = theirs
            else:

                @pl.when(j == 0)
                def _():
                    stay_ref[0, z, :, cols] = mine
                    stay_ref[1, z, :, cols] = theirs

                @pl.when(j == 1)
                def _():
                    fly_ref[0, z, :, cols] = mine
                    fly_ref[1, z, :, cols] = theirs

        at += grad.shape[1]


def attn_bwd_kernel(keeps, here_ref, qkv_ref, p_ref, o_ref, do_ref, x_any, da_any, *refs):
    got_any, refs = refs[:keeps], refs[keeps:]
    piece_refs, refs = refs[: 1 + keeps], refs[1 + keeps :]
    sum_ref, dproj_ref, acc_ref, xs, das, sems = refs[: len(refs) - keeps]
    got_refs = refs[len(refs) - keeps :]
    r = pl.program_id(0)
    rows = xs.shape[0]
    local = qkv_ref.shape[2] // 3
    heads = p_ref.shape[1]
    hd = local // heads

    def row_copies(i):
        pairs = ((x_any, xs), (da_any, das))
        return [pltpu.make_async_copy(src.at[i], dst.at[i], sems.at[2 * i + n]) for n, (src, dst) in enumerate(pairs)]

    others = [
        pltpu.make_async_copy(src, dst, sems.at[2 * rows + n]) for n, (src, dst) in enumerate(zip(got_any, got_refs))
    ]

    @pl.when(r == 0)
    def _():
        for i in range(rows):
            for copy in row_copies(i):
                copy.start()
        for copy in others:
            copy.start()

    q_all, k_all, v_all = (qkv_ref[0, :, i * local : (i + 1) * local] for i in range(3))
    o_all, do_all = o_ref[0, :, :local], do_ref[0, :, :local]
    prod = o_all.astype(F32) * do_all.astype(F32)
    dq, dk, dv = [], [], []
    for h in range(heads):
        at = slice(h * hd, (h + 1) * hd)
        p = p_ref[0, h]
        do = do_all[:, at]
        dv.append(tn(do, p))
        dp = nt(do, v_all[:, at])
        mid = jnp.sum(prod[:, at], axis=-1, keepdims=True)
        ds = (p.astype(F32) * (dp - mid)).astype(BF)
        dq.append(nn(ds, k_all[:, at]))
        dk.append(tn(q_all[:, at], ds))
    dq = (jnp.concatenate(dq, axis=1).astype(BF).astype(F32) * 0.125).astype(BF)
    dkv = jnp.transpose(jnp.concatenate(dk + dv, axis=0)).astype(BF)
    dproj = jnp.concatenate([dq, dkv], axis=1)
    sums = jnp.broadcast_to(rowsum(dproj.astype(F32)), sum_ref.shape)

    for copy in row_copies(r):
        copy.wait()

    @pl.when(r == 0)
    def _():
        acc_ref[...] = jnp.zeros_like(acc_ref)
        sum_ref[...] = jnp.zeros_like(sum_ref)

    sum_ref[...] += sums
    acc_ref[:, : 3 * local] += tn(xs[r], dproj)
    acc_ref[:, 3 * local :] += tn(das[r], o_all)
    dproj_ref[0] = jnp.concatenate([dproj, jnp.zeros((dproj.shape[0], 64), BF)], axis=1)

    @pl.when(r == rows - 1)
    def _():
        if not keeps:
            pieces(acc_ref[...], here_ref, piece_refs[0], slice(0, acc_ref.shape[1]))
        else:
            others[0].wait()
            (got_ref,), (stay_ref, fly_ref) = got_refs, piece_refs
            depth, size = stay_ref.shape[0], stay_ref.shape[1]
            lo = here_ref[0]
            for z in range(depth):
                first, second = (acc_ref[(2 * z + b) * size : (2 * z + b + 1) * size] for b in range(2))
                mine, theirs = jnp.where(lo == 0, first, second), jnp.where(lo == 0, second, first)
                stay_ref[z] = (mine + got_ref[0, z].astype(F32)).astype(BF)
                fly_ref[z] = (theirs + got_ref[1, z].astype(F32)).astype(BF)


def small_kernel(norm1_ref, norm2_ref, up_ref, s2, s3, keep_ref, send_ref):
    local = s2.shape[1] // 3
    parts = {2: s2, 3: s3}
    for ref, pair in ((keep_ref, (0, 2)), (send_ref, (1, 3))):
        ref[...] = jnp.zeros_like(ref)
        for i, (src, row) in enumerate(
            ((norm1_ref, 0), (norm2_ref, 0), (norm1_ref, 2), (norm1_ref, 1), (norm2_ref, 2), (norm2_ref, 1))
        ):
            ref[i : i + 1] = src[row : row + 1]
        for n, j in enumerate(pair):
            ref[8 + 8 * n : 9 + 8 * n] = up_ref[0:1, j * ref.shape[1] : (j + 1) * ref.shape[1]]
            if j in parts:
                ref[9 + 8 * n : 10 + 8 * n, :local] = parts[j][0:1, :local]
                ref[9 + 8 * n : 10 + 8 * n, local : 2 * local] = parts[j][0:1, 2 * local :]


def split_small(own):
    rows = jnp.concatenate([own[0:6], own[8:10]], axis=0)
    high = rows.astype(BF)
    return jnp.concatenate([high, (rows - high.astype(F32)).astype(BF)], axis=0)


def last_kernel(here_ref, a_ref, b_ref, c_ref, own_ref, got_ref, *out_refs):
    depth, rows = a_ref.shape[0], a_ref.shape[1]
    small = split_small(own_ref[...] + got_ref[...])
    for k, out_ref in enumerate(out_refs):
        z = lax.rem(here_ref[1] + k, depth)
        total = a_ref[z].astype(F32) + b_ref[z].astype(F32) + c_ref[z].astype(F32)
        out_ref[:rows, :] = total.astype(BF)
        out_ref[rows:, :] = small


def final_kernel(place_ref, *refs):
    *parts, qkv_ref, out_ref, gains_ref, shifts_ref, up_ref, qv_ref = refs
    rows = qkv_ref.shape[0]
    total = parts[0][...].astype(F32)
    for ref in parts[1:]:
        total += ref[...].astype(F32)
    local = qkv_ref.shape[2]
    for i in range(3):
        qkv_ref[:, i, :] = total[:rows, i * local : (i + 1) * local]
    out_ref[...] = jnp.transpose(total[:rows, 3 * local :])
    small = total[rows : rows + 8] + total[rows + 8 :]
    width = small.shape[1]
    hd = width // up_ref.shape[0]
    lane = lax.broadcasted_iota(jnp.int32, (width, 128), 0)
    column = lax.broadcasted_iota(jnp.int32, (width, 128), 1)

    def pick(values, ones):
        ones = ones.astype(BF)
        a, b, c = split3(values)
        return nn(a, ones) + nn(b, ones) + nn(c, ones)

    size = gains_ref.shape[1]
    norms = pick(small, (lane == place_ref[0] + column) & (column < size))
    gains_ref[...] = norms[0:2, :size]
    shifts_ref[...] = norms[2:6, :size]
    group = up_ref.shape[1]
    ones = (lane % hd == place_ref[1] + column) & (column < group)
    head = lax.broadcasted_iota(jnp.int32, (16, width), 1) // hd
    row = lax.broadcasted_iota(jnp.int32, (16, width), 0)
    ups = pick(jnp.where(head == row, small[6:7], 0.0), ones)
    up_ref[...] = ups[: up_ref.shape[0], :group]
    qvs = pick(jnp.where(head == row, small[7:8], 0.0), ones)
    heads = qv_ref.shape[1]
    for i in range(2):
        qv_ref[i] = qvs[i * heads : (i + 1) * heads, :group]


def input_back_kernel(p0, p1, p2, p3, da_ref, w0, w1, w2, w3, y0, y1, y2, y3, w_ref, sems):
    step = pl.program_id(0)
    y_refs, p_refs = (y0, y1, y2, y3), (p0, p1, p2, p3)
    wide = p0.shape[1]

    def body(ready):
        dx = da_ref[...].astype(F32)
        if ready:
            for j, p in enumerate(p_refs):
                ready(j)
                dx = dx + nt(p[...], w_ref[:, j * wide : (j + 1) * wide])
        else:
            dx = dx + nt(jnp.concatenate([p[...] for p in p_refs], axis=1), w_ref[...])
        low = dx.astype(BF)
        size = y_refs[0].shape[1]
        here = low.shape[0] // size
        for j, ref in enumerate(y_refs):

            @pl.when(lax.rem(step, 4 // here) == j // here)
            def _():
                ref[0] = low[(j % here) * size : (j % here + 1) * size]

    groups = []
    for j, w in enumerate((w0, w1, w2, w3)):
        groups.append([pltpu.make_async_copy(w, w_ref.at[:, j * wide : (j + 1) * wide], sems.at[j])])
    fetch(groups, step, body)


def make(mesh):
    nd, ntens = mesh.shape["dp"], mesh.shape["tensor"]
    nh = nd // 2
    groups = [[2 * z + b for z in range(nh)] for b in range(2)]

    def across(array, axis, bit):
        size = nd if axis == "dp" else ntens
        return lax.ppermute(array, axis, [(i, i ^ bit) for i in range(size)])

    def along(array):
        return lax.all_to_all(array, "dp", 0, 0, tiled=True, axis_index_groups=groups)

    def summed(*outs):
        layout, ins, shapes = [], [], []
        for ranges in outs:
            layout.append([len(terms) for terms in ranges])
            columns = 0
            for terms in ranges:
                for array, lead in terms:
                    block = (1,) * len(lead) + (nh // 2,) + array.shape[-2:]
                    ins.append((array, block, lambda z, lead=lead: (*lead, z, 0, 0)))
                columns += array.shape[-1]
            shape = (nh, array.shape[-2], columns)
            shapes.append((shape, BF, (nh // 2,) + shape[1:], lambda z: (z, 0, 0)))
        return call(functools.partial(add_kernel, layout), (2,), ins, shapes, limit=63, cost=60.0)

    def turn(array, k):
        return lax.ppermute(array, "dp", [(2 * ((z + k) % nh) + b, 2 * z + b) for z in range(nh) for b in range(2)])

    def swap(array):
        return across(array, "tensor", 1)

    def settle(array):
        return jnp.sum(array.astype(F32), axis=0)

    def shards(
        tokens, w_qkv, b_qv, w_out, w_up, b_up, w_down, ln_gains, shifts, lengths, segments, pair_ids, targets
    ):
        part_len, row_count, width = tokens.shape
        rb = w_up.shape[0]
        hidden = w_up.shape[1]
        local = w_qkv.shape[2]
        hb = b_up.shape[1]
        hd = hb * nd
        heads = local // hd
        seq = segments.shape[1]
        rows = row_count // ntens
        count = rows * seq
        sents = rows * SEGS
        blk = 256
        steps = count // blk
        t = lax.axis_index("tensor")
        d = lax.axis_index("dp")
        fused = rb % 16 == 0
        depth, rbk = (nh, rb) if fused else (1, width // 2)
        lo_bit = (d % 2 if fused else d * 0).astype(jnp.int32)
        turned_by = (d // 2 if nh <= 4 else d * 0).astype(jnp.int32)
        here, here_first = jnp.stack([lo_bit, lo_bit * 0]), jnp.stack([lo_bit, turned_by])
        t_arr = t.astype(jnp.int32).reshape(1)

        def ready(own, other):
            if fused:
                return [own, other]
            first = jnp.where(d % 2 == 0, own, other)
            second = jnp.where(d % 2 == 0, other, own)
            full = jnp.stack([first, second], axis=1).reshape(2, 1, width // 2, own.shape[2])
            return [full[0], full[1]]

        def merged(own, other, place, after):
            if not fused:
                first = jnp.where(d % 2 == 0, own, other)
                second = jnp.where(d % 2 == 0, other, own)
                return jnp.stack([first, second], axis=1).reshape(width, own.shape[2])
            return call(
                merge_kernel,
                (1,),
                [(place, None, None), (own, None, None), (other, None, None)],
                [((width, own.shape[2]), BF, None, None)],
                scalars=1,
                after=after,
            )[0]

        def weights(pairs):
            return [(a, "any", None) for pair in pairs for a in ready(*pair)]

        def sems(n):
            return pltpu.SemaphoreType.DMA((n,))

        def pack(kernel, arrays, columns, after):
            return call(
                kernel,
                (nh,),
                [(a, None, None) for a in arrays],
                [((nh, rb, columns), BF, (1, rb, columns), lambda i: (i, 0, 0))],
                after=after,
            )[0]

        def cut(array):
            if fused:
                return array
            lead = array.shape[:-4]
            full = array.reshape(*lead, nh, 2, rb, array.shape[-1])
            first, second = full[..., 0, :, :], full[..., 1, :, :]
            return jnp.stack(
                [jnp.where(d % 2 == 0, first, second), jnp.where(d % 2 == 0, second, first)], axis=len(lead)
            )

        def uncut(array):
            if fused:
                return array
            mine, theirs = array[..., 0, :, :, :], array[..., 1, :, :, :]
            first, second = jnp.where(d % 2 == 0, mine, theirs), jnp.where(d % 2 == 0, theirs, mine)
            return jnp.stack([first, second], axis=-3).reshape(*array.shape[:-4], 2, 1, width // 2, array.shape[-1])

        deal_size = min(512, part_len * row_count)
        deal_block = deal_size // row_count
        dealt = call(
            deal_kernel,
            (part_len // deal_block,),
            [(t_arr, None, None), (tokens.reshape(part_len * row_count, width), (deal_size, width), lambda i, *_: (i, 0))],
            [((rows, part_len, width), BF, (rows, deal_block, width), lambda i, *_: (0, i, 0))] * ntens,
            scalars=1,
            cost=2.0,
        )
        x_parts = [dealt[0]] + [across(dealt[j], "tensor", j) for j in range(1, ntens)]

        mine = lax.dynamic_slice_in_dim(segments, t * rows, rows, 0).reshape(rows, ntens, part_len)
        own_len = lax.dynamic_slice_in_dim(lengths, t * rows, rows, 0)
        seg = jnp.stack([lax.dynamic_index_in_dim(mine, t ^ j, 1, False) for j in range(ntens)], axis=1)
        place = jnp.stack([(t ^ j) * part_len + jnp.arange(part_len) for j in range(ntens)])
        live = (place[None] < own_len[:, None, None]).reshape(rows, seq)
        seg = seg.reshape(rows, seq)
        key_code = jnp.where(live, seg, -1)
        classes = jnp.arange(hd)
        query_features = (jnp.where(live, seg, SEGS)[:, :, None] == classes).astype(BF)
        open_key = live[:, :, None] & ((seg[:, :, None] == classes) | (classes == SEGS))
        key_features = jnp.where(open_key | (classes > SEGS), 0.0, NEG).astype(BF)
        sent_code = jnp.where(live, seg + SEGS * jnp.arange(rows)[:, None], -1).reshape(1, count)
        member = (key_code[:, None, :] == jnp.arange(SEGS)[None, :, None]).astype(F32)
        inv_count = (1.0 / jnp.sum(member, axis=2)).reshape(sents, 1)
        own_ids = (d * row_count + t * rows) * SEGS + jnp.arange(sents, dtype=jnp.int32)
        is_mine = pair_ids[None, :] == own_ids[:, None]
        mates = pair_ids.reshape(-1, 2)[:, ::-1].reshape(-1)
        mate = jnp.sum(jnp.where(is_mine, mates[None, :], 0), axis=1, keepdims=True)
        goal = jnp.sum(jnp.where(is_mine, jnp.repeat(targets, 2)[None, :], 0.0), axis=1, keepdims=True)
        own_ids = own_ids[:, None]

        qv_col = jnp.pad(b_qv.reshape(-1, 1), ((0, rb - b_qv.size), (0, 63)))
        wide = 3 * local + 64
        (first_piece,) = call(
            pack_one_kernel,
            (1,),
            [(w_qkv.reshape(rb, 3 * local), None, None), (qv_col, None, None)],
            [((rb, wide), BF, None, None)],
        )
        extra = jnp.concatenate([ln_gains.T, shifts.T, b_up.reshape(-1, 1), jnp.zeros((rb, 57), BF)], axis=1)
        second_piece = pack(pack_two_kernel, [w_up, w_out, extra], hidden + 256, [])
        third_piece = pack(pack_three_kernel, [w_down], hidden, [])
        if nh <= 4:
            pieces1 = [first_piece] + [turn(first_piece, k) for k in range(1, nh)]
            own1 = call(
                stack_kernel,
                (1,),
                [(p, None, None) for p in pieces1],
                [((nh, rb, wide), BF, None, None)],
                after=[dealt[1], second_piece, third_piece],
            )[0]
        else:
            own1 = along(jnp.broadcast_to(first_piece[None], (nh, rb, wide)))
        lo1 = across(own1, "dp", 1)
        w1 = {0: merged(own1, lo1, here_first, [key_features, query_features, third_piece, inv_count, sent_code])}
        w1[1] = swap(w1[0])
        w1[2] = across(w1[0], "tensor", 2)
        (second_piece,) = gate([second_piece], [own1])
        own2 = along(second_piece)

        k = np.arange(width)
        dd, within = k // rb, k % rb
        up_at = (within // hb) * hd + dd * hb + within % hb
        sup = np.zeros((width, width), np.float32)
        sup[k, up_at] = 1.0
        qv = within < 2 * heads * hb
        qv_at = (within // (heads * hb)) * local + ((within // hb) % heads) * hd + dd * hb + within % hb
        sqv = np.zeros((width, 2 * local), np.float32)
        sqv[k[qv], qv_at[qv]] = 1.0
        sup, sqv = jnp.asarray(sup, BF), jnp.asarray(sqv, BF)

        def whole(array):
            return (array, None, None)

        def whole_out(shape, dtype):
            return (shape, dtype, None, None)

        by_row = lambda r, *_: (r, 0, 0)

        def attend(xs, w, before, cost=9.0):
            outs = [
                ((rows, seq, 3 * local), BF, (1, seq, 3 * local), by_row),
                ((rows, heads, seq, seq), BF, (1, heads, seq, seq), lambda r, *_: (r, 0, 0, 0)),
                ((rows, seq, 256), BF, (1, seq, 256), by_row),
            ]
            if len(xs) > 1:
                outs.append(((rows, seq, width), BF, (1, seq, width), by_row))
            return call(
                functools.partial(attn_fwd_kernel, len(xs)),
                (rows,),
                [(a, (1,) + a.shape[1:], by_row) for a in xs]
                + [
                    whole(w),
                    whole(sqv),
                    (key_features, (1, seq, hd), by_row),
                    (query_features, (1, seq, hd), by_row),
                ],
                outs,
                scratch=[pltpu.VMEM((8, 2 * local), F32)],
                after=before,
                limit=63,
                cost=cost,
            )

        kept = {}
        *kept[0], x = attend(x_parts, w1[0], [second_piece], 25.0)
        (own2,) = gate([own2], [kept[0][2]])
        lo2, far2 = across(own2, "dp", 1), across(own2, "tensor", 2)
        (third_piece,) = gate([third_piece], [own2])
        own3 = along(third_piece)
        kept[1] = attend([x], w1[1], [own2])
        w1[2], lo2 = gate([w1[2], lo2], [kept[1][2]])
        w1[3] = swap(w1[2])
        far_lo2 = across(lo2, "tensor", 2)
        kept[2] = attend([x], w1[2], [lo2])
        own3, far2 = gate([own3, far2], [kept[2][2]])
        lo3, far3 = across(own3, "dp", 1), across(own3, "tensor", 2)
        kept[3] = attend([x], w1[3], [own3, far2])
        far_lo2, lo3 = gate([far_lo2, lo3], [kept[3][2]])
        far_lo3 = across(lo3, "tensor", 2)
        w2 = [(own2, lo2), (swap(own2), swap(lo2)), (far2, far_lo2), (swap(far2), swap(far_lo2))]
        o_parts = [kept[j][2].reshape(count, 256) for j in range(4)]
        x_flat = x.reshape(count, width)

        def rows_of(array):
            return (array, (blk, array.shape[1]), lambda i, *_: (i, 0))

        def rows_out(shape, dtype):
            return (shape, dtype, (blk, shape[1]), lambda i, *_: (i, 0))

        all_w, all_o = pltpu.VMEM((width, 4 * hidden), BF), pltpu.VMEM((width, 4 * 256), BF)
        xh1, rstd1, u, h, g, small = call(
            middle_kernel,
            (steps,),
            [whole(here)] + [rows_of(o) for o in o_parts] + [rows_of(x_flat), whole(sup)] + weights(w2),
            [
                rows_out((count, width), BF),
                rows_out((count, 1), F32),
                rows_out((count, width), BF),
                rows_out((count, 4 * hidden), BF),
                rows_out((count, 4 * hidden), BF),
                whole_out((8, width), F32),
            ],
            scratch=[all_o, all_w, pltpu.VMEM((8, 4 * hidden), F32), sems(16 * depth)],
            scalars=1,
            after=[lo3],
            limit=63,
            cost=20.0,
        )
        far3, far_lo3 = gate([far3, far_lo3], [u])
        w3 = [(own3, lo3), (swap(own3), swap(lo3)), (far3, far_lo3), (swap(far3), swap(far_lo3))]
        code_spec = (sent_code, (1, blk), lambda i, *_: (0, i))
        span = blk // part_len
        part_out = lambda i, *_: (i * span // ntens, 0, 0)
        xh2, rstd2, y0, y1, y2, y3, pooled = call(
            down_kernel,
            (steps,),
            [whole(here), rows_of(h), rows_of(u), whole(small), code_spec, whole(inv_count)] + weights(w3),
            [rows_out((count, width), BF), rows_out((count, 1), F32)]
            + [((rows, part_len, width), BF, (1, part_len, width), part_out)] * ntens
            + [whole_out((nd * ntens, sents, width), BF)],
            scratch=[pltpu.VMEM((sents, width), F32), all_w, sems(8 * depth)],
            scalars=1,
            limit=63,
            cost=14.0,
        )

        def send_back(parts):
            return [parts[0]] + [across(parts[j], "tensor", j) for j in range(1, ntens)]

        def collected(parts, after=()):
            (out,) = call(
                collect_kernel,
                (part_len // deal_block,),
                [whole(t_arr)] + [(a, (rows, deal_block, width), lambda i, *_: (0, i, 0)) for a in parts],
                [((part_len * row_count, width), BF, (deal_size, width), lambda i, *_: (i, 0))],
                scalars=1,
                after=after,
                limit=63,
                cost=30.0,
            )
            return out.reshape(part_len, row_count, width)

        every = lax.all_to_all(pooled, ("dp", "tensor"), 0, 0, tiled=True).reshape(nd * ntens * sents, width)

        shape = (2, 2, depth, rbk, hidden)
        half = (2,) + shape[2:]

        def blocked(array):
            return (blk, array.shape[1]), lambda i, *_: (jnp.minimum(i, steps - 1), 0)

        def blocked_out(shape, dtype):
            return (shape, dtype, *blocked(jax.ShapeDtypeStruct(shape, dtype)))

        late = lambda i: jnp.maximum(i - steps, 0)
        df, de, send3, sums2, dbup = call(
            functools.partial(feed_back_kernel, steps),
            (steps + 2,),
            [whole(here), whole(every), whole(own_ids), whole(mate), whole(goal), whole(inv_count)]
            + [(sent_code, (1, blk), lambda i, *_: (0, jnp.minimum(i, steps - 1)))]
            + [(a, *blocked(a)) for a in (xh2, rstd2)]
            + [whole(small), (g, *blocked(g))]
            + [(h, (count, hidden), lambda i, *_: (0, 2 * late(i) + 1))]
            + weights(w3),
            [
                blocked_out((count, width), BF),
                blocked_out((count, 4 * hidden), BF),
                (shape, BF, (1,) + shape[1:], lambda i, *_: (late(i), 0, 0, 0, 0)),
                whole_out((8, width), F32),
                whole_out((8, 4 * hidden), F32),
            ],
            scratch=[pltpu.VMEM((3, sents, width), BF), pltpu.VMEM((count, width), BF), all_w, sems(8 * depth)],
            scalars=1,
            limit=63,
            cost=32.0,
        )

        hidden_parts = send_back([y0, y1, y2, y3])

        def grad_part(a, b, odd, kernel, got, outs, after):
            return call(
                kernel,
                (2,),
                [whole(here), whole(a), (b, (count, hidden), lambda j, *_: (0, 2 * j + odd))]
                + [(v, (1,) + v.shape[1:], lambda j, *_: (j, 0, 0, 0, 0)) for v in got],
                outs,
                scalars=1,
                after=after,
                limit=63,
                cost=40.0,
            )

        both_out = [(shape, BF, (1,) + shape[1:], lambda j, *_: (j, 0, 0, 0, 0))]
        hidden_out = collected(hidden_parts, [send3])
        (sendu,) = grad_part(u, de, 1, grad_send_kernel, [], both_out, [send3, hidden_out])
        got = uncut(swap(cut(send3)))
        stay3, fly3 = grad_part(
            df, h, 0, functools.partial(grad_keep_kernel, True), [got],
            [(half, BF, (1,) + half[1:], lambda j, *_: (j, 0, 0, 0))] * 2, [sendu],
        )
        if not fused:
            both = cut(jnp.stack([stay3, fly3], axis=1))
            stay3, fly3 = both[:, 0], both[:, 1]
        got = uncut(swap(cut(sendu)))
        stayu, flyu = grad_part(
            u, de, 0, functools.partial(grad_keep_kernel, False), [got], [whole_out(half, BF)] * 2, [fly3]
        )
        stayu, flyu = cut(stayu), cut(flyu)
        got3x = across(fly3, "dp", 1)
        gotuy = across(flyu, "tensor", 2)

        da, do, sums1 = call(
            norm_back_kernel,
            (steps,),
            [whole(here), rows_of(de), rows_of(df), rows_of(xh1), rows_of(rstd1), whole(small)] + weights(w2),
            [
                rows_out((count, width), BF),
                rows_out((count, 4 * 256), BF),
                whole_out((8, width), F32),
            ],
            scratch=[all_w, all_o, sems(16 * depth)],
            scalars=1,
            after=[flyu],
            limit=63,
            cost=14.0,
        )
        da_rows, do_rows = da.reshape(rows, seq, width), do.reshape(rows, seq, 4 * 256)
        grad_cols = 4 * local

        def attend_back(j, got, after):
            qkv, p, o = kept[j]
            half = (depth, rbk, grad_cols)
            kinds = [whole_out((2,) + half, BF)] if got is None else [whole_out(half, BF)] * 2
            keeps = 0 if got is None else 1
            whole_row = pltpu.VMEM((rows, seq, width), BF)
            *outs, sums, dproj = call(
                functools.partial(attn_bwd_kernel, keeps),
                (rows,),
                [
                    whole(here),
                    (qkv, (1, seq, 3 * local), by_row),
                    (p, (1, heads, seq, seq), lambda r, *_: (r, 0, 0, 0)),
                    (o, (1, seq, 256), by_row),
                    (do_rows, (1, seq, 256), lambda r, *_: (r, 0, j)),
                    (x, "any", None),
                    (da_rows, "any", None),
                ]
                + ([] if got is None else [(uncut(got), "any", None)]),
                kinds
                + [whole_out((8, 3 * local), F32), ((rows, seq, wide), BF, (1, seq, wide), by_row)],
                scratch=[pltpu.VMEM((width, grad_cols), F32), whole_row, whole_row, sems(2 * rows + keeps)]
                + [pltpu.VMEM((2,) + half, BF)] * keeps,
                scalars=1,
                after=after,
                limit=63,
                cost=11.0,
            )
            if got is None:
                out = cut(outs[0])
            elif fused:
                out = tuple(outs)
            else:
                both = cut(jnp.stack(outs))
                out = both[0], both[1]
            sums_of[j], dprojs[j] = sums, dproj.reshape(count, wide)
            return out

        sums_of, dprojs = {}, {}
        back3 = attend_back(3, None, [flyu])
        got_far = swap(back3)
        got3x, gotuy = gate([got3x, gotuy], [back3])
        turn3, turnu = summed([[(stay3, (1,)), (got3x, (1,))]], [[(stayu, (1,)), (gotuy, (1,))]])
        got3y, gotux = across(turn3, "tensor", 2), across(turnu, "dp", 1)
        stay_far, fly_far = attend_back(2, got_far, [turn3, turnu])
        got_fly = across(fly_far, "dp", 1)
        small_keep, small_send = call(
            small_kernel,
            (1,),
            [whole(a) for a in (sums1, sums2, dbup, sums_of[2], sums_of[3])],
            [whole_out((24, width), F32)] * 2,
            limit=63,
            after=[stay_far],
        )
        small_keep = small_keep + swap(small_send)
        small_got = across(jnp.concatenate([small_keep[:8], small_keep[16:]], axis=0), "tensor", 2)
        got3y, gotux = gate([got3y, gotux], [small_keep])
        (end,) = summed([[(stay3, (0,)), (got3x, (0,)), (got3y, ())], [(stayu, (0,)), (gotuy, (0,)), (gotux, ())]])
        end_sent = end
        end = along(end)
        back1 = attend_back(1, None, [end_sent])
        got_near = swap(back1)
        got_sums = swap(sums_of[1])
        (got_fly,) = gate([got_fly], [back1])
        (turn1,) = summed([[(stay_far, ()), (got_fly, ())]])
        got_turn1 = across(turn1, "tensor", 2)
        stay_near, fly_near = attend_back(0, got_near, [turn1])
        got1 = across(fly_near, "dp", 1)
        span_out = lambda i, *_: (i * span // ntens, 0, 0)
        dx_parts = call(
            input_back_kernel,
            (steps,),
            [rows_of(dprojs[j]) for j in range(4)] + [rows_of(da)] + [(w1[j], "any", None) for j in range(4)],
            [((rows, part_len, width), BF, (1, part_len, width), span_out)] * ntens,
            scratch=[pltpu.VMEM((width, 4 * wide), BF), sems(4)],
            limit=63,
            after=[stay_near],
            cost=8.0,
        )
        token_parts = send_back(dx_parts)

        got1, got_turn1, end = gate([got1, got_turn1, end], [dx_parts[0]])
        near_sums = sums_of[0] + got_sums
        near_sums = jnp.concatenate([near_sums[:1, :local], near_sums[:1, 2 * local :]], axis=1)
        own = small_keep[:16] + small_got + jnp.pad(near_sums, ((9, 6), (0, width - 2 * local)))
        got = across(own, "dp", 1)
        if fused and nh <= 4:
            last = call(
                last_kernel,
                (1,),
                [whole(here_first)] + [whole(v) for v in (stay_near, got1, got_turn1, own, got)],
                [whole_out((rb + 16, width), BF)] * nh,
                scalars=1,
                after=[token_parts[1]],
                limit=63,
                cost=60.0,
            )
            last_sent = last[0]
            mine = width // (nd * ntens)
            at = jnp.stack([(d * ntens + t) * mine, d * hb]).astype(jnp.int32)
            grad_qkv, grad_out, grad_gains, grad_shifts, grad_b_up, grad_b_qv = call(
                final_kernel,
                (1,),
                [whole(at)] + [whole(v) for v in [last[0]] + [turn(last[k], nh - k) for k in range(1, nh)]],
                [
                    whole_out((rb, 3, local), F32),
                    whole_out((local, rb), F32),
                    whole_out((2, mine), F32),
                    whole_out((4, mine), F32),
                    whole_out((hidden // hd, hb), F32),
                    whole_out((2, heads, hb), F32),
                ],
                scalars=1,
                limit=32,
            )
        else:
            (last_sent,) = summed([[(stay_near, ()), (got1, ()), (got_turn1, ())]])
            small = jnp.broadcast_to(split_small(own + got)[None], (nh, 16, width))
            total = settle(along(jnp.concatenate([last_sent, small], axis=1)))
            grad_qkv, grad_out = total[:rb, : 3 * local].reshape(rb, 3, local), total[:rb, 3 * local :].T
            small = total[rb : rb + 8] + total[rb + 8 :]
            rest = lax.dynamic_slice_in_dim(small[:6], (d * ntens + t) * (width // (nd * ntens)), width // (nd * ntens), 1)
            grad_b_up = lax.dynamic_slice_in_dim(small[6].reshape(hidden // hd, hd), d * hb, hb, 1)
            grad_b_qv = lax.dynamic_slice_in_dim(small[7, : 2 * local].reshape(2, heads, hd), d * hb, hb, 2)
            grad_gains, grad_shifts = rest[:2], rest[2:]
        grad_tokens = collected(token_parts, [last_sent])
        end = settle(end)
        grad_down, grad_up = end[:, :hidden], end[:, hidden:]
        return (
            hidden_out,
            grad_tokens,
            grad_qkv,
            grad_b_qv,
            grad_out,
            grad_up,
            grad_b_up,
            grad_down.T,
            grad_gains,
            grad_shifts,
        )

    return shards


def solution(mesh):
    return jax.shard_map(
        make(mesh),
        mesh=mesh,
        in_specs=(
            P("tensor", "dp", None),
            P("dp", None, "tensor"),
            P(None, "tensor", "dp"),
            P("tensor", "dp"),
            P("dp", "tensor"),
            P("tensor", "dp"),
            P("tensor", "dp"),
            P(None, "dp"),
            P(None, "dp"),
            P("dp"),
            P("dp", None),
            P(),
            P(),
        ),
        out_specs=(
            P("tensor", "dp", None),
            P("tensor", "dp", None),
            P("dp", None, "tensor"),
            P(None, "tensor", "dp"),
            P("tensor", "dp"),
            P("dp", "tensor"),
            P("tensor", "dp"),
            P("tensor", "dp"),
            P(None, ("dp", "tensor")),
            P(None, ("dp", "tensor")),
        ),
        check_vma=False,
    )
```
